32 devices in a mesh: dp: 8 (over z, x), seq: 4 (over y, core).
Axes of the slice: x: 2, y: 2, z: 4, core: 2. Of those that a mesh axis runs over, the one named last changes fastest.
Arguments:
- tokens: bfloat16 [16, 1024, 1024], P('dp', 'seq'), may hold values from -6 to 6
- enc_states: bfloat16 [16, 1024, 1024], P('dp', 'seq'), may hold values from -6 to 6
- dec_lengths: int32 [16], P('dp'), may hold values from 129 to 1024, as said below
- enc_lengths: int32 [16], P('dp'), may hold values from 256 to 1024, as said below
- adapter_step: int32 [16], P('dp'), may hold values from 0 to 4
- out_grad: bfloat16 [16, 1024, 1024], P('dp', 'seq'), may hold values from -6 to 6
- self_query: bfloat16 [1024, 1024], replicated, may hold values from -0.1875 to 0.1875
- self_key: bfloat16 [1024, 1024], replicated, may hold values from -0.1875 to 0.1875
- self_value: bfloat16 [1024, 1024], replicated, may hold values from -0.1875 to 0.1875
- self_out: bfloat16 [1024, 1024], replicated, may hold values from -0.75 to 0.75
- cross_query: bfloat16 [1024, 1024], replicated, may hold values from -0.1875 to 0.1875
- cross_key: bfloat16 [1024, 1024], replicated, may hold values from -0.1875 to 0.1875
- cross_value: bfloat16 [1024, 1024], replicated, may hold values from -0.1875 to 0.1875
- cross_out: bfloat16 [1024, 1024], replicated, may hold values from -0.75 to 0.75
- ffn_in: bfloat16 [1024, 4096], replicated, may hold values from -0.1875 to 0.1875
- ffn_out: bfloat16 [4096, 1024], replicated, may hold values from -0.09375 to 0.09375
- adapter_down: bfloat16 [1024, 512], replicated, may hold values from -0.1875 to 0.1875
- adapter_up: bfloat16 [512, 1024], replicated, may hold values from -0.25 to 0.25
- ln_gain: float32 [3, 1024], replicated, may hold values from 0.5 to 1.5
- ln_bias: float32 [3, 1024], replicated, may hold values from -1.2 to 1.2
Outputs:
- layer_output: bfloat16 [16, 1024, 1024], P('dp', 'seq')
- token_grad: bfloat16 [16, 1024, 1024], P('dp', 'seq')
- enc_grad: bfloat16 [16, 1024, 1024], P('dp', 'seq')
- adapter_down_grad: float32 [1024, 512], replicated
- adapter_up_grad: float32 [512, 1024], replicated
- ln_gain_grad: float32 [3, 1024], replicated
- ln_bias_grad: float32 [3, 1024], replicated
The draws below stay inside these ranges and needn't reach their ends.
Inputs may be any that keep to these rules, and one draw needn't show every extreme that they name: `dec_lengths`: lengths come from buckets of 256, 512 and 1024 positions, each more than half its bucket; among the 2 sequences of each index of dp, one has length 1024. `enc_lengths`: among the 2 sequences of each index of dp, one has length 1024.
All inputs are finite; a program needn't handle non-finite values.
Results may differ from the reference program's by a relative error of at most 0.02.
Values may be sent and summed in bfloat16 or wider, within the bound.
No kernel may reach another device: no remote copies, remote signals or barrier semaphores. Data moves between devices by JAX's collectives and lax.ppermute only.
A program may use at most 320 MiB of HBM per device.

```python
import jax
import jax.numpy as jnp
from jax import lax

D = 1024
HEADS = 16
HEAD_DIM = 64
FF = 4096
AD = 512
SEQ_DEV = 2
SEQ_LEN = 1024
ENC_LEN = 1024
SEQS = 16


def force_full(key, lengths, longest):
    groups = SEQS // SEQ_DEV
    chosen = jax.random.randint(key, (groups,), 0, SEQ_DEV)
    position_slot = jnp.arange(SEQS) % SEQ_DEV
    widest = position_slot == jnp.repeat(chosen, SEQ_DEV)
    return jnp.where(widest, longest, lengths).astype(jnp.int32)


def draw_dec_lengths(key, part):
    key = jax.random.fold_in(key, 11)
    tier_key, size_key, full_key = jax.random.split(key, 3)
    bucket_tier = jax.random.randint(tier_key, (SEQS,), 0, 3)
    bucket = jnp.where(bucket_tier == 0, SEQ_LEN // 4, jnp.where(bucket_tier == 1, SEQ_LEN // 2, SEQ_LEN))
    lengths = jax.random.randint(size_key, (SEQS,), bucket // 2 + 1, bucket + 1)
    return force_full(full_key, lengths, SEQ_LEN)


def draw_enc_lengths(key, part):
    key = jax.random.fold_in(key, 23)
    size_key, full_key = jax.random.split(key)
    lengths = jax.random.randint(size_key, (SEQS,), ENC_LEN // 4, ENC_LEN + 1)
    return force_full(full_key, lengths, ENC_LEN)


def with_ends(values, key, smallest, top_value):
    index_at = [jax.random.randint(jax.random.fold_in(key, axis), (), 0, length) for axis, length in enumerate(values.shape)]
    widest = values.shape.index(max(values.shape))
    neighbour = index_at[:widest] + [(index_at[widest] + 1) % values.shape[widest]] + index_at[widest + 1:]
    return values.at[tuple(index_at)].set(smallest).at[tuple(neighbour)].set(top_value)


def block_levels(rng, shape, pieces, low, high):
    gain = 1.0
    for position, blocks in pieces:
        steps = jax.random.uniform(jax.random.fold_in(jax.random.fold_in(rng, 6), position), (blocks,), jnp.float32, low / len(pieces), high / len(pieces))
        gain = gain * jnp.repeat(jnp.exp(steps), shape[position] // blocks).reshape((-1,) + (1,) * (len(shape) - 1 - position))
    return gain


def gaussian(own_key, shape, width, most, cuts=(), held_as=jnp.bfloat16):
    drawn = width * jax.random.normal(own_key, shape, jnp.float32)
    if cuts:
        drawn = drawn * block_levels(own_key, shape, cuts, -0.22, 0.18)
    return jnp.clip(drawn, -most, most).astype(held_as)


def setup_inputs(seed: int = 0) -> dict:
    arg_keys = jax.random.split(jax.random.key(seed), 21)
    tokens = gaussian(arg_keys[0], (SEQS, SEQ_LEN, D), 1.0, 6.0, ((0, 8), (1, 4)))
    enc_states = gaussian(arg_keys[1], (SEQS, ENC_LEN, D), 1.0, 6.0, ((0, 8), (1, 4)))
    dec_lengths = draw_dec_lengths(jax.random.fold_in(arg_keys[20], 71), 0)
    enc_lengths = draw_enc_lengths(jax.random.fold_in(arg_keys[20], 71), 0)
    adapter_step = with_ends(jax.random.randint(arg_keys[4], (SEQS,), 0, 5), jax.random.fold_in(arg_keys[4], 1), 0, 4).astype(jnp.int32)
    out_grad = gaussian(arg_keys[5], (SEQS, SEQ_LEN, D), 1.0, 6.0, ((0, 8), (1, 4)))
    self_query = gaussian(arg_keys[6], (D, D), D ** -0.5, 0.1875)
    self_key = gaussian(arg_keys[7], (D, D), D ** -0.5, 0.1875)
    self_value = gaussian(arg_keys[8], (D, D), D ** -0.5, 0.1875)
    self_out = gaussian(arg_keys[9], (D, D), (D // 16) ** -0.5, 0.75)
    cross_query = gaussian(arg_keys[10], (D, D), D ** -0.5, 0.1875)
    cross_key = gaussian(arg_keys[11], (D, D), D ** -0.5, 0.1875)
    cross_value = gaussian(arg_keys[12], (D, D), D ** -0.5, 0.1875)
    cross_out = gaussian(arg_keys[13], (D, D), (D // 16) ** -0.5, 0.75)
    ffn_in = gaussian(arg_keys[14], (D, FF), D ** -0.5, 0.1875)
    ffn_out = gaussian(arg_keys[15], (FF, D), FF ** -0.5, 0.09375)
    adapter_down = gaussian(arg_keys[16], (D, AD), D ** -0.5, 0.1875)
    adapter_up = gaussian(arg_keys[17], (AD, D), AD ** -0.5, 0.25)
    ln_gain = jnp.clip(1.0 + 0.1 * jax.random.normal(arg_keys[18], (3, D), jnp.float32), 0.5, 1.5)
    ln_bias = gaussian(arg_keys[19], (3, D), 0.3, 1.2, (), jnp.float32)
    return dict(tokens=tokens, enc_states=enc_states, dec_lengths=dec_lengths, enc_lengths=enc_lengths, adapter_step=adapter_step, out_grad=out_grad, self_query=self_query, self_key=self_key, self_value=self_value, self_out=self_out, cross_query=cross_query, cross_key=cross_key, cross_value=cross_value, cross_out=cross_out, ffn_in=ffn_in, ffn_out=ffn_out, adapter_down=adapter_down, adapter_up=adapter_up, ln_gain=ln_gain, ln_bias=ln_bias)


@jax.custom_vjp
def low(v):
    return lax.optimization_barrier(v.astype(jnp.bfloat16)).astype(jnp.float32)

@jax.custom_vjp
def low_back(v):
    return v

def low_keep(v):
    return (low(v), None)

def low_pass(kept, grad):
    return (grad,)

def back_keep(v):
    return (v, None)

def back_low(kept, grad):
    return (low(grad),)
low.defvjp(low_keep, low_pass)
low_back.defvjp(back_keep, back_low)
EPS = 1e-05
NEGATIVE = -1e+30
HIGHEST = lax.Precision.HIGHEST

def both_round(value):
    return low(low_back(value))

def matmul_high(left_side, right_side):
    return jnp.matmul(left_side, right_side, precision=HIGHEST)

def layer_norm(summed, gain_row, shift_row):
    center = summed - lax.optimization_barrier(jnp.mean(summed, axis=-1, keepdims=True))
    spread = lax.optimization_barrier(jnp.mean(center * center, axis=-1, keepdims=True))
    return center * lax.rsqrt(spread + EPS) * gain_row + shift_row

def attention(queries, all_keys, values, allowed):
    length = queries.shape[0]
    key_count = all_keys.shape[0]
    query_heads = queries.reshape(length, HEADS, HEAD_DIM)
    key_heads = all_keys.reshape(key_count, HEADS, HEAD_DIM)
    value_heads = values.reshape(key_count, HEADS, HEAD_DIM)
    scores = jnp.einsum('qhd,khd->hqk', query_heads, key_heads, precision=HIGHEST) * HEAD_DIM ** (-0.5)
    scores = low_back(scores)
    scores = jnp.where(allowed[None], scores, NEGATIVE)
    highest = lax.optimization_barrier(jnp.max(scores, axis=-1, keepdims=True))
    weights = jnp.exp(scores - highest)
    probabilities = weights / lax.optimization_barrier(jnp.sum(weights, axis=-1, keepdims=True))
    attended = jnp.einsum('hqk,khd->qhd', low(probabilities), value_heads, precision=HIGHEST)
    return attended.reshape(length, HEADS * HEAD_DIM)

def layer_one(token_rows, state_rows, down_weight, up_weight, gains, shifts, dec_length, enc_length, adapter_level, frozen):
    positions = jnp.arange(SEQ_LEN)
    causal = (positions[None, :] <= positions[:, None]) & (positions[None, :] < dec_length)
    queries = both_round(matmul_high(token_rows, frozen[0]))
    all_keys = both_round(matmul_high(token_rows, frozen[1]))
    values = both_round(matmul_high(token_rows, frozen[2]))
    attended = attention(queries, all_keys, values, causal)
    branch = low_back(matmul_high(both_round(attended), frozen[3]))
    first_norm = layer_norm(token_rows + branch, gains[0], shifts[0])
    cross_queries = both_round(matmul_high(low(first_norm), frozen[4]))
    cross_keys = both_round(matmul_high(state_rows, frozen[5]))
    cross_values = both_round(matmul_high(state_rows, frozen[6]))
    enc_reach = jnp.broadcast_to(jnp.arange(ENC_LEN)[None, :] < enc_length, (SEQ_LEN, ENC_LEN))
    cross_attended = attention(cross_queries, cross_keys, cross_values, enc_reach)
    cross_branch = low_back(matmul_high(both_round(cross_attended), frozen[7]))
    second_norm = layer_norm(first_norm + cross_branch, gains[1], shifts[1])
    second_low = low(second_norm)
    inner_act = low_back(matmul_high(second_low, frozen[8]))
    hidden = low(jax.nn.gelu(inner_act, approximate=False))
    adapter_in = low_back(matmul_high(second_low, down_weight))
    factor = (1.0 + adapter_level.astype(jnp.float32)) * 0.25
    adapter_hidden = low(factor * jax.nn.silu(adapter_in))
    update = low_back(matmul_high(hidden, frozen[9]) + matmul_high(adapter_hidden, up_weight))
    return layer_norm(second_norm + update, gains[2], shifts[2])

def reference(tokens, enc_states, dec_lengths, enc_lengths, adapter_step, out_grad, self_query, self_key, self_value, self_out, cross_query, cross_key, cross_value, cross_out, ffn_in, ffn_out, adapter_down, adapter_up, ln_gain, ln_bias):
    frozen = tuple((weight.astype(jnp.float32) for weight in (self_query, self_key, self_value, self_out, cross_query, cross_key, cross_value, cross_out, ffn_in, ffn_out)))
    down_float = adapter_down.astype(jnp.float32)
    up_float = adapter_up.astype(jnp.float32)
    gain_float = ln_gain.astype(jnp.float32)
    shift_float = ln_bias.astype(jnp.float32)

    def per_sequence(running, sequence_item):
        token_rows, state_rows, dec_length, enc_length, adapter_level, cotangent = sequence_item

        def forward(token_part, state_part, down_part, up_part, gain_part, shift_part):
            return layer_one(token_part, state_part, down_part, up_part, gain_part, shift_part, dec_length, enc_length, adapter_level, frozen)
        result, pullback = jax.vjp(forward, token_rows.astype(jnp.float32), state_rows.astype(jnp.float32), down_float, up_float, gain_float, shift_float)
        gradients = pullback(cotangent.astype(jnp.float32))
        running = tuple((before + after for before, after in zip(running, gradients[2:])))
        return (running, (result.astype(jnp.bfloat16), gradients[0].astype(jnp.bfloat16), gradients[1].astype(jnp.bfloat16)))
    zero_grads = (jnp.zeros_like(down_float), jnp.zeros_like(up_float), jnp.zeros_like(gain_float), jnp.zeros_like(shift_float))
    totals, stacked = lax.scan(per_sequence, zero_grads, (tokens, enc_states, dec_lengths, enc_lengths, adapter_step, out_grad))
    return (stacked[0], stacked[1], stacked[2], totals[0], totals[1], totals[2], totals[3])
```

```python
import functools
import math

import jax
import jax.numpy as jnp
from jax import lax
from jax.experimental import pallas as pl
from jax.experimental.pallas import tpu as pltpu
from jax.sharding import PartitionSpec as P

HEAD_DIM = 64
PAIR = 2 * HEAD_DIM
EPS = 1e-05
NEGATIVE = -1e30
SCALE = HEAD_DIM ** (-0.5)
EXP2_SCALE = SCALE * math.log2(math.e)
HALF_LOG2E = 0.5 * math.log2(math.e)

f32 = jnp.float32
bf16 = jnp.bfloat16

NN = (((1,), (0,)), ((), ()))
NT = (((1,), (1,)), ((), ()))
TN = (((0,), (0,)), ((), ()))

ANY = pl.BlockSpec(memory_space=pl.ANY)
SMEM = pl.BlockSpec(memory_space=pltpu.SMEM)
VMEM = pl.BlockSpec(memory_space=pltpu.VMEM)
MIB = 2 ** 20


def dg(left, right, dims):
    return lax.dot_general(left, right, dims, preferred_element_type=f32)


def add(total, term):
    return term if total is None else total + term


def params(limit_mib):
    return pltpu.CompilerParams(vmem_limit_bytes=limit_mib * MIB)


def cost(flops, nbytes, exps=0):
    return pl.CostEstimate(flops=int(flops), bytes_accessed=int(nbytes), transcendentals=int(exps))


def shape(dims, dtype):
    return jax.ShapeDtypeStruct(dims, dtype)


def start_copies(pairs, sems):
    copies = [pltpu.make_async_copy(src, dst, sems.at[n]) for n, (src, dst) in enumerate(pairs)]
    for copy in copies:
        copy.start()
    return copies


def project_kernel(plan, n_in, *refs):
    count = len(plan)
    xs = refs[:n_in]
    ws = refs[n_in:n_in + count]
    n_out = 1 + max(o for _, o, _ in plan)
    outs = refs[n_in + count:n_in + count + n_out]
    held, sems = refs[n_in + count + n_out:]
    copies = start_copies([(w, held.at[j]) for j, w in enumerate(ws)], sems)
    for j, (i, o, row) in enumerate(plan):
        copies[j].wait()
        value = dg(xs[i][...], held[j], NN).astype(bf16)
        if row is None:
            outs[o][...] = value
        else:
            outs[o][row] = value


def project(xs, ws, plan, name):
    rows, width = xs[0].shape
    count = len(plan)
    n_out = 1 + max(o for _, o, _ in plan)
    out_shape = []
    for o in range(n_out):
        used = [row for _, oo, row in plan if oo == o]
        out_shape.append(shape((rows, width) if used[0] is None else (len(used), rows, width), bf16))
    return pl.pallas_call(
        functools.partial(project_kernel, plan, len(xs)),
        in_specs=[VMEM] * len(xs) + [ANY] * count,
        out_specs=[VMEM] * n_out,
        out_shape=out_shape,
        scratch_shapes=[pltpu.VMEM((count, width, width), bf16), pltpu.SemaphoreType.DMA((count,))],
        compiler_params=params(24),
        cost_estimate=cost(2 * count * rows * width * width, 2 * count * width * width),
        name=name,
    )(*xs, *ws)


def pair_masks():
    lane = lax.broadcasted_iota(jnp.int32, (1, PAIR), 1)
    return lane, lane < HEAD_DIM


def key_bias(start, length, rows):
    pos = start + lax.broadcasted_iota(jnp.int32, (rows, PAIR), 0)
    lane = lax.broadcasted_iota(jnp.int32, (rows, PAIR), 1)
    masked = jnp.where(pos < length, 0.0, NEGATIVE)
    return (
        jnp.where(lane == HEAD_DIM, masked, 0.0).astype(bf16),
        jnp.where(lane == 0, masked, 0.0).astype(bf16),
    )


def queries_with_one(q, half):
    one = jnp.ones((), bf16)
    return jnp.where(half, q, one), jnp.where(half, one, q)


def head_only(x, half):
    zero = jnp.zeros((), bf16)
    return jnp.where(half, x, zero), jnp.where(half, zero, x)


def soft(chunks, highest):
    probs = [jnp.exp2((s - highest) * EXP2_SCALE) for s in chunks]
    total = None
    for p in probs:
        total = add(total, p.sum(0, keepdims=True))
    return [p.astype(bf16) for p in probs], total


def top(chunks):
    highest = chunks[0].max(0, keepdims=True)
    for s in chunks[1:]:
        highest = jnp.maximum(highest, s.max(0, keepdims=True))
    return highest


def grad_columns(aT, oT, inverse):
    rows = aT.shape[1]
    sub = lax.broadcasted_iota(jnp.int32, (HEAD_DIM, rows), 0)
    zero = jnp.zeros((HEAD_DIM, rows), bf16)
    full, plain = [], []
    for h in range(2):
        sl = slice(h * HEAD_DIM, (h + 1) * HEAD_DIM)
        a = aT[sl].astype(f32) * inverse[h:h + 1]
        d = -(a * oT[sl].astype(f32)).sum(0, keepdims=True)
        high = d.astype(bf16).astype(f32)
        extra = jnp.where(sub == 0, high, jnp.where(sub == 1, d - high, 0.0)).astype(bf16)
        a = a.astype(bf16)
        full.append(jnp.concatenate([a, extra] if h == 0 else [extra, a], 0))
        plain.append(jnp.concatenate([a, zero] if h == 0 else [zero, a], 0))
    return full, plain


def values_with_ones(v, lane, half):
    first = jnp.where((lane == HEAD_DIM) | (lane == HEAD_DIM + 1), 1.0, 0.0).astype(bf16)
    second = jnp.where(lane < 2, 1.0, 0.0).astype(bf16)
    return jnp.where(half, v, first), jnp.where(half, second, v)


def cross_forward_kernel(n, sc_ref, q_ref, *refs):
    kvs = refs[:n]
    oT_ref, p_ref, inv_ref, bias_ref = refs[n:]
    rows = q_ref.shape[0]
    block = kvs[0].shape[1]
    lane, half = pair_masks()

    @pl.when(pl.program_id(0) == 0)
    def _():
        for j in range(n):
            bias_ref[0, j], bias_ref[1, j] = key_bias(sc_ref[1 + j], sc_ref[0], block)

    keys = [[], []]
    valuesT = []
    for j in range(n):
        k = kvs[j][0]
        keys[0].append(jnp.where(half, k, bias_ref[0, j]))
        keys[1].append(jnp.where(half, bias_ref[1, j], k))
        valuesT.append(kvs[j][1].T)
    queries = queries_with_one(q_ref[...], half)
    items = [(h, b) for b in range(rows // block) for h in range(2)]

    def score(item):
        h, b = item
        q = queries[h][b * block:(b + 1) * block]
        return [dg(keys[h][j], q, NT) for j in range(n)]

    later = score(items[0])
    for step, (h, b) in enumerate(items):
        chunks = later
        if step + 1 < len(items):
            later = score(items[step + 1])
        probs, total = soft(chunks, top(chunks))
        cols = pl.ds(b * block, block)
        out = None
        for j in range(n):
            p_ref[h, pl.ds(j * block, block), cols] = probs[j]
            out = add(out, dg(valuesT[j][h * HEAD_DIM:(h + 1) * HEAD_DIM], probs[j], NN))
        inverse = 1.0 / total
        inv_ref[0, pl.ds(h, 1), cols] = inverse
        oT_ref[pl.ds(h * HEAD_DIM, HEAD_DIM), cols] = (out * inverse).astype(bf16)


def feature_rows(rows):
    return pl.BlockSpec((PAIR, rows), lambda i: (i, 0))


def feature_cols(rows):
    return pl.BlockSpec((rows, PAIR), lambda i: (0, i))


def kv_cols(rows, count=2):
    return pl.BlockSpec((count, rows, PAIR), lambda i: (0, 0, i))


def pair_block(*dims):
    return pl.BlockSpec(dims, lambda i: (i,) + (0,) * (len(dims) - 1))


def cross_forward(scalars, q, kvs):
    n = len(kvs)
    rows, width = q.shape
    block = kvs[0].shape[1]
    pairs = width // PAIR
    every = n * block
    return pl.pallas_call(
        functools.partial(cross_forward_kernel, n),
        grid=(pairs,),
        in_specs=[SMEM, feature_cols(rows)] + [kv_cols(block)] * n,
        out_specs=[feature_rows(rows), pair_block(2, every, rows), pair_block(1, 2, rows)],
        out_shape=[
            shape((width, rows), bf16),
            shape((2 * pairs, every, rows), bf16),
            shape((pairs, 2, rows), f32),
        ],
        scratch_shapes=[pltpu.VMEM((2, n, block, PAIR), bf16)],
        compiler_params=params(32),
        cost_estimate=cost(16 * rows * every * width, 4 * pairs * every * rows, 2 * pairs * every * rows),
        name="cross_forward",
    )(scalars, q, *kvs)


def cross_backward_kernel(n, q_ref, p_ref, aT_ref, oT_ref, inv_ref, *refs):
    kvs = refs[:n]
    dqT_ref = refs[n]
    dkvs = refs[n + 1:]
    rows = q_ref.shape[0]
    block = kvs[0].shape[1]
    lane, half = pair_masks()
    values = [[], []]
    keysT = []
    for j in range(n):
        first, second = values_with_ones(kvs[j][1], lane, half)
        values[0].append(first)
        values[1].append(second)
        keysT.append(kvs[j][0].T)
    queries = head_only(q_ref[...], half)
    full, plain = grad_columns(aT_ref[...], oT_ref[...], inv_ref[0])
    items = [(h, b) for b in range(rows // block) for h in range(2)]

    def grad_probs(item):
        h, b = item
        a = full[h][:, b * block:(b + 1) * block]
        return [dg(values[h][j], a, NN) for j in range(n)]

    dk = [None] * n
    dv = [None] * n
    later = grad_probs(items[0])
    for step, (h, b) in enumerate(items):
        dps = later
        if step + 1 < len(items):
            later = grad_probs(items[step + 1])
        dq = None
        sl = slice(b * block, (b + 1) * block)
        for j in range(n):
            p = p_ref[h, pl.ds(j * block, block), pl.ds(b * block, block)]
            ds = (p * dps[j]).astype(bf16)
            dv[j] = add(dv[j], dg(p, plain[h][:, sl], NT))
            dk[j] = add(dk[j], dg(ds, queries[h][sl], NN))
            dq = add(dq, dg(keysT[j][h * HEAD_DIM:(h + 1) * HEAD_DIM], ds, NN))
        dqT_ref[pl.ds(h * HEAD_DIM, HEAD_DIM), pl.ds(b * block, block)] = (dq * SCALE).astype(bf16)
    for j in range(n):
        dkvs[j][0] = (dk[j] * SCALE).astype(bf16)
        dkvs[j][1] = dv[j].astype(bf16)


def cross_backward(q, probs, aT, oT, inverse, kvs):
    n = len(kvs)
    rows, width = q.shape
    block = kvs[0].shape[1]
    pairs = width // PAIR
    every = n * block
    return pl.pallas_call(
        functools.partial(cross_backward_kernel, n),
        grid=(pairs,),
        in_specs=[feature_cols(rows), pair_block(2, every, rows), feature_rows(rows), feature_rows(rows),
                  pair_block(1, 2, rows)] + [kv_cols(block)] * n,
        out_specs=[feature_rows(rows)] + [kv_cols(block)] * n,
        out_shape=[shape((width, rows), bf16)] + [shape((2, block, width), bf16)] * n,
        compiler_params=params(32),
        cost_estimate=cost(32 * rows * every * width, 4 * pairs * every * rows),
        name="cross_backward",
    )(q, probs, aT, oT, inverse, *kvs)


def self_forward_kernel(others, sc_ref, q_own, q_swap, *refs):
    kvs = refs[:2 + 2 * others]
    oT_ref, p_ref, inv_ref, tri_ref = refs[2 + 2 * others:]
    block = q_own.shape[0]
    lane, half = pair_masks()
    swapped = sc_ref[1] == 1

    @pl.when(pl.program_id(0) == 0)
    def _():
        key = lax.broadcasted_iota(jnp.int32, (block, block), 0)
        query = lax.broadcasted_iota(jnp.int32, (block, block), 1)
        tri_ref[...] = jnp.where(key <= query, 0.0, NEGATIVE)

    def low_high(first, second):
        return jnp.where(swapped, second, first), jnp.where(swapped, first, second)

    def prepare(k, start):
        bias = key_bias(start, sc_ref[0], block)
        return jnp.where(half, k, bias[0]), jnp.where(half, bias[1], k)

    q_low, q_high = low_high(q_own[...], q_swap[...])
    k_low, k_high = low_high(kvs[0][0], kvs[1][0])
    v_low, v_high = low_high(kvs[0][1], kvs[1][1])
    keys = [prepare(k_low, sc_ref[2]), prepare(k_high, sc_ref[3])]
    valuesT = [v_low.T, v_high.T]
    wraps = []
    for r in range(others):
        wrap = sc_ref[4 + 3 * r] == 1
        wraps.append(wrap)
        k_first, k_second = low_high(kvs[2 + 2 * r][0], kvs[3 + 2 * r][0])
        v_first, v_second = low_high(kvs[2 + 2 * r][1], kvs[3 + 2 * r][1])
        keys.append(prepare(k_first, sc_ref[5 + 3 * r]))
        keys.append(prepare(jnp.where(wrap, k_first, k_second), sc_ref[6 + 3 * r]))
        valuesT.append(v_first.T)
        valuesT.append(jnp.where(wrap, v_first, v_second).T)
    ones = [queries_with_one(q_low, half), queries_with_one(q_high, half)]
    either = [tuple(jnp.where(w, ones[0][h], ones[1][h]) for h in range(2)) for w in wraps]
    tri = tri_ref[...]

    def score(h):
        low = dg(keys[0][h], ones[0][h], NT) + tri
        high = [dg(keys[0][h], ones[1][h], NT), dg(keys[1][h], ones[1][h], NT) + tri]
        either_way = []
        for r in range(others):
            high.append(dg(keys[2 + 2 * r][h], ones[1][h], NT))
            either_way.append(dg(keys[3 + 2 * r][h], either[r][h], NT))
        return low, high, either_way

    later = score(0)
    for h in range(2):
        low, high, either_way = later
        if h == 0:
            later = score(1)
        top_low = low.max(0, keepdims=True)
        top_high = top(high)
        for r in range(others):
            peak = either_way[r].max(0, keepdims=True)
            top_low = jnp.where(wraps[r], jnp.maximum(top_low, peak), top_low)
            top_high = jnp.where(wraps[r], top_high, jnp.maximum(top_high, peak))
        p_low, sum_low = soft([low], top_low)
        p_high, sum_high = soft(high, top_high)
        sl = slice(h * HEAD_DIM, (h + 1) * HEAD_DIM)
        out_low = dg(valuesT[0][sl], p_low[0], NN)
        out_high = dg(valuesT[0][sl], p_high[0], NN) + dg(valuesT[1][sl], p_high[1], NN)
        p_ref[h, 0] = p_low[0]
        p_ref[h, 1] = p_high[0]
        p_ref[h, 2] = p_high[1]
        for r in range(others):
            p, total = soft([either_way[r]], jnp.where(wraps[r], top_low, top_high))
            out = dg(valuesT[3 + 2 * r][sl], p[0], NN)
            sum_low = jnp.where(wraps[r], sum_low + total, sum_low)
            sum_high = jnp.where(wraps[r], sum_high, sum_high + total)
            out_low = jnp.where(wraps[r], out_low + out, out_low)
            out_high = jnp.where(wraps[r], out_high, out_high + out)
            out_high = out_high + dg(valuesT[2 + 2 * r][sl], p_high[2 + r], NN)
            p_ref[h, 3 + 2 * r] = p_high[2 + r]
            p_ref[h, 4 + 2 * r] = p[0]
        inverse_low, inverse_high = 1.0 / sum_low, 1.0 / sum_high
        out_low, out_high = (out_low * inverse_low).astype(bf16), (out_high * inverse_high).astype(bf16)
        for n, value, inverse in ((0, out_low, inverse_low), (1, out_high, inverse_high)):
            inv_ref[0, n, pl.ds(h, 1), :] = inverse
        first, second = low_high(out_low, out_high)
        oT_ref[pl.ds(h * HEAD_DIM, HEAD_DIM), pl.ds(0, block)] = first
        oT_ref[pl.ds(h * HEAD_DIM, HEAD_DIM), pl.ds(block, block)] = second


def self_forward(scalars, q_own, q_swap, kvs):
    others = len(kvs) // 2 - 1
    block, width = q_own.shape
    pairs = width // PAIR
    tiles = 3 + 2 * others
    return pl.pallas_call(
        functools.partial(self_forward_kernel, others),
        grid=(pairs,),
        in_specs=[SMEM] + [feature_cols(block)] * 2 + [kv_cols(block)] * len(kvs),
        out_specs=[feature_rows(2 * block), pair_block(2, tiles, block, block), pair_block(1, 2, 2, block)],
        out_shape=[
            shape((width, 2 * block), bf16),
            shape((2 * pairs, tiles, block, block), bf16),
            shape((pairs, 2, 2, block), f32),
        ],
        scratch_shapes=[pltpu.VMEM((block, block), f32)],
        compiler_params=params(32),
        cost_estimate=cost(16 * tiles * block * block * width, 4 * pairs * tiles * block * block,
                           2 * pairs * tiles * block * block),
        name="self_forward",
    )(scalars, q_own, q_swap, *kvs)


def self_backward_kernel(others, sc_ref, q_own, q_swap, p_ref, aT_ref, oT_ref, inv_ref, *refs):
    kvs = refs[:2 + 2 * others]
    dqT_ref = refs[2 + 2 * others]
    dkvs = refs[3 + 2 * others:]
    block = q_own.shape[0]
    lane, half = pair_masks()
    swapped = sc_ref[1] == 1

    def low_high(first, second):
        return jnp.where(swapped, second, first), jnp.where(swapped, first, second)

    q_low, q_high = low_high(q_own[...], q_swap[...])
    k_low, k_high = low_high(kvs[0][0], kvs[1][0])
    v_low, v_high = low_high(kvs[0][1], kvs[1][1])
    keysT = [k_low.T, k_high.T]
    values = [values_with_ones(v_low, lane, half), values_with_ones(v_high, lane, half)]
    wraps = []
    for r in range(others):
        wrap = sc_ref[4 + 3 * r] == 1
        wraps.append(wrap)
        k_first, k_second = low_high(kvs[2 + 2 * r][0], kvs[3 + 2 * r][0])
        v_first, v_second = low_high(kvs[2 + 2 * r][1], kvs[3 + 2 * r][1])
        keysT.append(k_first.T)
        keysT.append(jnp.where(wrap, k_first, k_second).T)
        values.append(values_with_ones(v_first, lane, half))
        values.append(values_with_ones(jnp.where(wrap, v_first, v_second), lane, half))
    queries = [head_only(q_low, half), head_only(q_high, half)]
    a_low, a_high = low_high(aT_ref[:, 0:block], aT_ref[:, block:2 * block])
    o_low, o_high = low_high(oT_ref[:, 0:block], oT_ref[:, block:2 * block])
    grads = [grad_columns(a_low, o_low, inv_ref[0, 0]), grad_columns(a_high, o_high, inv_ref[0, 1])]
    tiles = [(0, 0, 0), (1, 0, 1), (2, 1, 1)]
    for r in range(others):
        tiles.append((3 + 2 * r, 2 + 2 * r, 1))
        tiles.append((4 + 2 * r, 3 + 2 * r, None))

    def side(tile, h, which):
        _, key, query = tile
        if query is not None:
            return queries[query][h] if which == 2 else grads[query][which][h]
        wrap = wraps[(key - 3) // 2]
        if which == 2:
            return jnp.where(wrap, queries[0][h], queries[1][h])
        return jnp.where(wrap, grads[0][which][h], grads[1][which][h])

    dk = [None] * len(keysT)
    dv = [None] * len(keysT)

    def grad_probs(h):
        return [dg(values[tile[1]][h], side(tile, h, 0), NN) for tile in tiles]

    later = grad_probs(0)
    for h in range(2):
        dps = later
        if h == 0:
            later = grad_probs(1)
        dq = [None, None]
        free = []
        for tile, dp in zip(tiles, dps):
            index, key, query = tile
            p = p_ref[h, index]
            ds = (p * dp).astype(bf16)
            dv[key] = add(dv[key], dg(p, side(tile, h, 1), NT))
            dk[key] = add(dk[key], dg(ds, side(tile, h, 2), NN))
            term = dg(keysT[key][h * HEAD_DIM:(h + 1) * HEAD_DIM], ds, NN)
            if query is None:
                free.append((wraps[(key - 3) // 2], term))
            else:
                dq[query] = add(dq[query], term)
        for wrap, term in free:
            dq = [jnp.where(wrap, dq[0] + term, dq[0]), jnp.where(wrap, dq[1], dq[1] + term)]
        first, second = low_high(dq[0], dq[1])
        dqT_ref[pl.ds(h * HEAD_DIM, HEAD_DIM), pl.ds(0, block)] = (first * SCALE).astype(bf16)
        dqT_ref[pl.ds(h * HEAD_DIM, HEAD_DIM), pl.ds(block, block)] = (second * SCALE).astype(bf16)

    def emit(n, row, low, high):
        first, second = low_high(low, high)
        dkvs[n][row] = first.astype(bf16)
        dkvs[n + 1][row] = second.astype(bf16)

    emit(0, 0, dk[0] * SCALE, dk[1] * SCALE)
    emit(0, 1, dv[0], dv[1])
    for r in range(others):
        wrap = wraps[r]
        for row, terms, factor in ((0, dk, SCALE), (1, dv, 1.0)):
            always, either = terms[2 + 2 * r] * factor, terms[3 + 2 * r] * factor
            emit(2 + 2 * r, row, jnp.where(wrap, always + either, always), jnp.where(wrap, 0.0, either))


def self_backward(scalars, q_own, q_swap, probs, aT, oT, inverse, kvs):
    others = len(kvs) // 2 - 1
    block, width = q_own.shape
    pairs = width // PAIR
    tiles = 3 + 2 * others
    return pl.pallas_call(
        functools.partial(self_backward_kernel, others),
        grid=(pairs,),
        in_specs=[SMEM] + [feature_cols(block)] * 2
        + [pair_block(2, tiles, block, block), feature_rows(2 * block), feature_rows(2 * block),
           pair_block(1, 2, 2, block)] + [kv_cols(block)] * len(kvs),
        out_specs=[feature_rows(2 * block)] + [kv_cols(block)] * len(kvs),
        out_shape=[shape((width, 2 * block), bf16)] + [shape((2, block, width), bf16)] * len(kvs),
        compiler_params=params(32),
        cost_estimate=cost(32 * tiles * block * block * width, 4 * pairs * tiles * block * block),
        name="self_backward",
    )(scalars, q_own, q_swap, probs, aT, oT, inverse, *kvs)


ROWS = 64


def normalized(z):
    center = z - jnp.mean(z, axis=-1, keepdims=True)
    spread = jnp.mean(center * center, axis=-1, keepdims=True)
    r = lax.rsqrt(spread + EPS)
    return center * r, r


def norm_back(G, n, r, gain):
    scaled = G * gain
    return r * (scaled - jnp.mean(scaled, -1, keepdims=True) - n * jnp.mean(scaled * n, -1, keepdims=True))


def spread_lanes(r):
    return jnp.broadcast_to(r, (r.shape[0], PAIR))


def for_rows(total, body, init=0):
    def step(i, carry):
        return body(pl.ds(pl.multiple_of(i * ROWS, ROWS), ROWS), carry)

    return lax.fori_loop(0, total // ROWS, step, init)


def fold(x):
    return x.reshape(x.shape[0] // 8, 8, x.shape[1]).sum(0)


def zero_sums(count, width):
    return tuple(jnp.zeros((8, width), f32) for _ in range(count))


def first_norm_kernel(oT_ref, x_own, x_swap, w_out, w_query, gain_ref, bias_ref, n_ref, r_ref, cq_ref,
                      held, low_ref, sems):
    copies = start_copies([(w_out, held.at[0]), (w_query, held.at[1])], sems)
    block = x_own.shape[0]
    rows = 2 * block
    copies[0].wait()
    n_ref[...] = dg(oT_ref[...], held[0], TN)
    gain, bias = gain_ref[0:1], bias_ref[0:1]
    for half, x_ref in enumerate((x_own, x_swap)):
        def body(sl, carry, half=half, x_ref=x_ref):
            rows_here = pl.ds(pl.multiple_of(sl.start + half * block, ROWS), ROWS)
            n, r = normalized(n_ref[rows_here] + x_ref[sl].astype(f32))
            n_ref[rows_here] = n
            r_ref[rows_here] = spread_lanes(r)
            low_ref[rows_here] = (n * gain + bias).astype(bf16)
            return carry
        for_rows(block, body)
    copies[1].wait()
    cq_ref[...] = dg(low_ref[...], held[1], NN).astype(bf16)


def first_norm(oT, x_own, x_swap, w_out, w_query, gain, bias):
    width, rows = oT.shape
    return pl.pallas_call(
        first_norm_kernel,
        in_specs=[VMEM] * 3 + [ANY] * 2 + [VMEM] * 2,
        out_specs=[VMEM] * 3,
        out_shape=[shape((rows, width), f32), shape((rows, PAIR), f32), shape((rows, width), bf16)],
        scratch_shapes=[pltpu.VMEM((2, width, width), bf16), pltpu.VMEM((rows, width), bf16),
                        pltpu.SemaphoreType.DMA((2,))],
        compiler_params=params(24),
        cost_estimate=cost(4 * rows * width * width, 4 * width * width + 10 * rows * width),
        name="first_norm",
    )(oT, x_own, x_swap, w_out, w_query, gain, bias)


def gelu_parts(x):
    gauss = jnp.exp2(x * x * (-HALF_LOG2E))
    t = 1.0 / (1.0 + (0.3275911 * math.sqrt(0.5)) * jnp.abs(x))
    poly = t * (0.254829592 + t * (-0.284496736 + t * (1.421413741 + t * (-1.453152027 + t * 1.061405429))))
    tail = 0.5 * poly * gauss
    phi = jnp.where(x >= 0.0, 1.0 - tail, tail)
    return x * phi, phi + x * gauss * (1.0 / math.sqrt(2.0 * math.pi))


def feed_forward_kernel(chunk, sc_ref, oT_ref, n1_ref, g_own, g_swap, w_out, w_in, w_back, w_down, w_up,
                        gain_ref, bias_ref,
                        out_own, out_swap, n2_ref, r2_ref, slope_ref, g3_ref, gai_ref, wg_ref, sums_ref,
                        out_w, in_w, back_w, down_w, up_w, low_ref, upd_ref, sems):
    block = g_own.shape[0]
    rows, width = n1_ref.shape
    hidden_units = w_in.shape[1]
    chunks = hidden_units // chunk
    adapter = w_down.shape[1]

    def in_copy(c):
        return pltpu.make_async_copy(
            w_in.at[:, pl.ds(pl.multiple_of(c * chunk, chunk), chunk)], in_w.at[c], sems.at[3 + c])

    def back_copy(c):
        return pltpu.make_async_copy(
            w_back.at[pl.ds(pl.multiple_of(c * chunk, chunk), chunk)], back_w.at[c], sems.at[3 + chunks + c])

    copies = start_copies([(w_out, out_w)], sems)
    for c in range(chunks):
        in_copy(c).start()
        back_copy(c).start()
        if c == 0:
            copies += [pltpu.make_async_copy(w_down, down_w, sems.at[1]),
                       pltpu.make_async_copy(w_up, up_w, sems.at[2])]
            copies[1].start()
            copies[2].start()

    gain1, bias1 = gain_ref[0:1], bias_ref[0:1]
    gain2, bias2 = gain_ref[1:2], bias_ref[1:2]
    gain3, bias3 = gain_ref[2:3], bias_ref[2:3]
    copies[0].wait()
    n2_ref[...] = dg(oT_ref[...], out_w[...], TN)

    def second(sl, carry):
        n, r = normalized(n2_ref[sl] + n1_ref[sl] * gain1 + bias1)
        n2_ref[sl] = n
        r2_ref[sl] = spread_lanes(r)
        low_ref[sl] = (n * gain2 + bias2).astype(bf16)
        return carry

    for_rows(rows, second)

    copies[1].wait()
    copies[2].wait()
    factor = (1.0 + sc_ref[0].astype(f32)) * 0.25
    adapter_in = dg(low_ref[...], down_w[...], NN)
    sig = 1.0 / (1.0 + jnp.exp(-adapter_in))
    adapter_hidden = (factor * (adapter_in * sig)).astype(bf16)
    adapter_slope = factor * (sig * (1.0 + adapter_in * (1.0 - sig)))
    upd_ref[...] = dg(adapter_hidden, up_w[...], NN)

    def step(c, carry):
        in_copy(c).wait()
        weight = in_w[c]
        parts = [dg(low_ref[pl.ds(b * block, block)], weight, NN) for b in range(2)]
        back_copy(c).wait()
        weight = back_w[c]
        cols = pl.ds(pl.multiple_of(c * chunk, chunk), chunk)
        for b in range(2):
            value, slope = gelu_parts(parts[b])
            slope_ref[pl.ds(b * block, block), cols] = slope.astype(bf16)
            upd_ref[pl.ds(b * block, block)] += dg(value.astype(bf16), weight, NN)
        return carry

    lax.fori_loop(0, chunks, step, 0)

    sums = zero_sums(2, width)
    for half, (g_ref, out_ref) in enumerate(((g_own, out_own), (g_swap, out_swap))):
        def third(sl, carry, half=half, g_ref=g_ref, out_ref=out_ref):
            here = pl.ds(pl.multiple_of(sl.start + half * block, ROWS), ROWS)
            n, r = normalized(n2_ref[here] * gain2 + bias2 + upd_ref[here])
            out_ref[sl] = (n * gain3 + bias3).astype(bf16)
            G = g_ref[sl].astype(f32)
            g3_ref[here] = norm_back(G, n, r, gain3)
            return carry[0] + fold(G * n), carry[1] + fold(G)
        sums = for_rows(block, third, sums)
    sums_ref[0:1] = sums[0].sum(0, keepdims=True)
    sums_ref[1:2] = sums[1].sum(0, keepdims=True)

    grad_update = g3_ref[...].astype(bf16)
    wg_ref[0:adapter] = dg(adapter_hidden, grad_update, TN).astype(wg_ref.dtype)
    gai = (adapter_slope * dg(grad_update, up_w[...], NT)).astype(bf16)
    gai_ref[...] = gai
    wg_ref[adapter:2 * adapter] = dg(gai, low_ref[...], TN).astype(wg_ref.dtype)


def feed_forward(scalars, oT, n1, g_own, g_swap, w_out, w_in, w_back, w_down, w_up, gain, bias):
    rows, width = n1.shape
    block = g_own.shape[0]
    units = w_in.shape[1]
    adapter = w_down.shape[1]
    chunk = 512
    chunks = units // chunk
    return pl.pallas_call(
        functools.partial(feed_forward_kernel, chunk),
        in_specs=[SMEM] + [VMEM] * 4 + [ANY] * 5 + [VMEM] * 2,
        out_specs=[VMEM] * 9,
        out_shape=[
            shape((block, width), bf16), shape((block, width), bf16), shape((rows, width), f32),
            shape((rows, PAIR), f32), shape((rows, units), bf16), shape((rows, width), f32),
            shape((rows, adapter), bf16), shape((2 * adapter, width), bf16), shape((2, width), f32),
        ],
        scratch_shapes=[
            pltpu.VMEM((width, width), bf16), pltpu.VMEM((chunks, width, chunk), bf16),
            pltpu.VMEM((chunks, chunk, width), bf16), pltpu.VMEM((width, adapter), bf16),
            pltpu.VMEM((adapter, width), bf16), pltpu.VMEM((rows, width), bf16),
            pltpu.VMEM((rows, width), f32), pltpu.SemaphoreType.DMA((3 + 2 * chunks,)),
        ],
        compiler_params=params(56),
        cost_estimate=cost(4 * rows * width * units + 12 * rows * width * adapter + 2 * rows * width * width,
                           4 * width * units, 2 * rows * units),
        name="feed_forward",
    )(scalars, oT, n1, g_own, g_swap, w_out, w_in, w_back, w_down, w_up, gain, bias)


def feed_back_kernel(chunk, g3_ref, slope_ref, gai_ref, n2_ref, r2_ref, w_in, w_back, w_down, w_out, gain_ref,
                     g2_ref, aT_ref, sums_ref, out_w, in_w, back_w, down_w, low_ref, sems):
    rows, width = g3_ref.shape
    chunks = w_in.shape[1] // chunk
    block = rows // 2

    def in_copy(c):
        return pltpu.make_async_copy(
            w_in.at[:, pl.ds(pl.multiple_of(c * chunk, chunk), chunk)], in_w.at[c], sems.at[2 + c])

    def back_copy(c):
        return pltpu.make_async_copy(
            w_back.at[pl.ds(pl.multiple_of(c * chunk, chunk), chunk)], back_w.at[c], sems.at[2 + chunks + c])

    copies = start_copies([(w_down, down_w)], sems)
    for c in range(chunks):
        back_copy(c).start()
        in_copy(c).start()
    copies.append(pltpu.make_async_copy(w_out, out_w, sems.at[1]))
    copies[1].start()
    low_ref[...] = g3_ref[...].astype(bf16)
    copies[0].wait()
    g2_ref[...] = g3_ref[...] + dg(gai_ref[...], down_w[...], NT)

    def step(c, carry):
        cols = pl.ds(pl.multiple_of(c * chunk, chunk), chunk)
        back_copy(c).wait()
        weight = back_w[c]
        parts = [dg(low_ref[pl.ds(b * block, block)], weight, NT) for b in range(2)]
        in_copy(c).wait()
        weight = in_w[c]
        for b in range(2):
            here = pl.ds(b * block, block)
            inner = (parts[b] * slope_ref[here, cols].astype(f32)).astype(bf16)
            g2_ref[here] += dg(inner, weight, NT)
        return carry

    lax.fori_loop(0, chunks, step, 0)
    gain2 = gain_ref[1:2]

    def second(sl, carry):
        G = g2_ref[sl]
        n = n2_ref[sl]
        grad = norm_back(G, n, r2_ref[sl][:, 0:1], gain2)
        g2_ref[sl] = grad
        low_ref[sl] = grad.astype(bf16)
        return carry[0] + fold(G * n), carry[1] + fold(G)

    sums = for_rows(rows, second, zero_sums(2, width))
    sums_ref[0:1] = sums[0].sum(0, keepdims=True)
    sums_ref[1:2] = sums[1].sum(0, keepdims=True)
    copies[1].wait()
    aT_ref[...] = dg(out_w[...], low_ref[...], NT).astype(bf16)


def feed_back(g3, slope, gai, n2, r2, w_in, w_back, w_down, w_out, gain):
    rows, width = g3.shape
    units = w_in.shape[1]
    adapter = w_down.shape[1]
    chunk = 512
    chunks = units // chunk
    return pl.pallas_call(
        functools.partial(feed_back_kernel, chunk),
        in_specs=[VMEM] * 5 + [ANY] * 4 + [VMEM],
        out_specs=[VMEM] * 3,
        out_shape=[shape((rows, width), f32), shape((width, rows), bf16), shape((2, width), f32)],
        scratch_shapes=[
            pltpu.VMEM((width, width), bf16), pltpu.VMEM((chunks, width, chunk), bf16),
            pltpu.VMEM((chunks, chunk, width), bf16), pltpu.VMEM((width, adapter), bf16),
            pltpu.VMEM((rows, width), bf16), pltpu.SemaphoreType.DMA((2 + 2 * chunks,)),
        ],
        compiler_params=params(52),
        cost_estimate=cost(4 * rows * width * units + 2 * rows * width * adapter + 2 * rows * width * width,
                           4 * width * units),
        name="feed_back",
    )(g3, slope, gai, n2, r2, w_in, w_back, w_down, w_out, gain)


def first_back_kernel(g2_ref, dqT_ref, n_ref, r_ref, w_query, w_out, gain_ref, g1_ref, aT_ref, sums_ref,
                      held, low_ref, sems):
    copies = start_copies([(w_query, held.at[0]), (w_out, held.at[1])], sems)
    rows, width = g2_ref.shape
    dq = dqT_ref[...].T
    copies[0].wait()
    g1_ref[...] = g2_ref[...] + dg(dq, held[0], NT)
    gain = gain_ref[0:1]

    def body(sl, carry):
        G = g1_ref[sl]
        n = n_ref[sl]
        grad = norm_back(G, n, r_ref[sl][:, 0:1], gain)
        g1_ref[sl] = grad
        low_ref[sl] = grad.astype(bf16)
        return carry[0] + fold(G * n), carry[1] + fold(G)

    sums = for_rows(rows, body, zero_sums(2, width))
    sums_ref[0:1] = sums[0].sum(0, keepdims=True)
    sums_ref[1:2] = sums[1].sum(0, keepdims=True)
    copies[1].wait()
    aT_ref[...] = dg(held[1], low_ref[...], NT).astype(bf16)


def first_back(g2, dqT, n1, r1, w_query, w_out, gain):
    rows, width = g2.shape
    return pl.pallas_call(
        first_back_kernel,
        in_specs=[VMEM] * 4 + [ANY] * 2 + [VMEM],
        out_specs=[VMEM] * 3,
        out_shape=[shape((rows, width), f32), shape((width, rows), bf16), shape((2, width), f32)],
        scratch_shapes=[pltpu.VMEM((2, width, width), bf16), pltpu.VMEM((rows, width), bf16),
                        pltpu.SemaphoreType.DMA((2,))],
        compiler_params=params(28),
        cost_estimate=cost(4 * rows * width * width, 4 * width * width + 10 * rows * width),
        name="first_back",
    )(g2, dqT, n1, r1, w_query, w_out, gain)


def key_grad_kernel(others, *refs):
    mine = refs[0]
    received = refs[1:1 + others]
    w_key, w_value, out_ref, held, sems = refs[1 + others:]
    copies = start_copies([(w_key, held.at[0]), (w_value, held.at[1])], sems)
    total = None
    for n in range(2):
        part = mine[n].astype(f32)
        for ref in received:
            part = part + ref[n].astype(f32)
        part = part.astype(bf16)
        copies[n].wait()
        total = add(total, dg(part, held[n], NT))
    out_ref[...] = total.astype(bf16)


def key_grad(mine, received, w_key, w_value):
    _, block, width = mine.shape
    others = len(received)
    return pl.pallas_call(
        functools.partial(key_grad_kernel, others),
        in_specs=[VMEM] * (1 + others) + [ANY] * 2,
        out_specs=VMEM,
        out_shape=shape((block, width), bf16),
        scratch_shapes=[pltpu.VMEM((2, width, width), bf16), pltpu.SemaphoreType.DMA((2,))],
        compiler_params=params(20),
        cost_estimate=cost(4 * block * width * width, 4 * width * width),
        name="enc_grad",
    )(mine, *received, w_key, w_value)


def token_grad_kernel(others, half, *refs):
    g1_ref, dqT_ref, mine = refs[:3]
    received = refs[3:3 + others]
    w_query, w_key, w_value, out_ref, held, sems = refs[3 + others:]
    copies = start_copies([(w, held.at[n]) for n, w in enumerate((w_query, w_key, w_value))], sems)
    block = out_ref.shape[0]
    rows = pl.ds(half * block, block)
    dq = dqT_ref[:, rows].T
    copies[0].wait()
    total = g1_ref[rows] + dg(dq, held[0], NT)
    for n in range(2):
        part = mine[n].astype(f32)
        for ref in received:
            part = part + ref[n].astype(f32)
        part = part.astype(bf16)
        copies[n + 1].wait()
        total = total + dg(part, held[n + 1], NT)
    out_ref[...] = total.astype(bf16)


def token_grad(half, g1, dqT, mine, received, w_query, w_key, w_value):
    _, block, width = mine.shape
    others = len(received)
    return pl.pallas_call(
        functools.partial(token_grad_kernel, others, half),
        in_specs=[VMEM] * (3 + others) + [ANY] * 3,
        out_specs=VMEM,
        out_shape=shape((block, width), bf16),
        scratch_shapes=[pltpu.VMEM((3, width, width), bf16), pltpu.SemaphoreType.DMA((3,))],
        compiler_params=params(24),
        cost_estimate=cost(6 * block * width * width, 6 * width * width),
        name="token_grad",
    )(g1, dqT, mine, *received, w_query, w_key, w_value)


def exchange_bits(x, axis, bit):
    return lax.ppermute(x, axis, [(i, i ^ bit) for i in range(lax.axis_size(axis))])


def reduce_everywhere(x, steps):
    for axis, bit in steps:
        mine = (lax.axis_index(axis) // bit) % 2
        half = x.shape[0] // 2
        send = lax.dynamic_slice_in_dim(x, (1 - mine) * half, half, 0)
        keep = lax.dynamic_slice_in_dim(x, mine * half, half, 0)
        x = (keep.astype(f32) + exchange_bits(send, axis, bit).astype(f32)).astype(bf16)
    for axis, bit in reversed(steps):
        mine = (lax.axis_index(axis) // bit) % 2
        other = exchange_bits(x, axis, bit)
        x = jnp.where(mine == 1, jnp.concatenate([other, x]), jnp.concatenate([x, other]))
    return x


def bits(size):
    return [1 << n for n in range(size.bit_length() - 1)]


def per_device(
    tokens, enc_states, dec_lengths, enc_lengths, adapter_step, out_grad,
    self_query, self_key, self_value, self_out, cross_query, cross_key, cross_value, cross_out,
    ffn_in, ffn_out, adapter_down, adapter_up, ln_gain, ln_bias,
):
    group = lax.axis_size("seq")
    half = group // 2
    others = half - 1
    member = lax.axis_index("seq")
    side = member // half
    block = tokens.shape[1]
    low = jnp.where(side == 1, group - 1 - member, member)
    swap = [(i, group - 1 - i) for i in range(group)]

    def place(s, index):
        return group - 1 - index if s == 1 else index

    def from_shift(r):
        return [(place(s, (i + r) % half), place(s, i)) for s in range(2) for i in range(half)]

    def to_shift(r):
        return [(place(s, i), place(s, (i + r) % half)) for s in range(2) for i in range(half)]

    def split(x):
        mine = lax.dynamic_index_in_dim(x, side, 0, keepdims=False)
        theirs = lax.dynamic_index_in_dim(x, 1 - side, 0, keepdims=False)
        return mine, lax.ppermute(theirs, "seq", swap)

    def joined(mine, theirs):
        back = lax.ppermute(theirs, "seq", swap)
        return jnp.where(side == 1, jnp.stack([back, mine]), jnp.stack([mine, back]))

    dec_length = dec_lengths[side]
    enc_length = enc_lengths[side]
    x_own, x_swap = split(tokens)
    e_own, e_swap = split(enc_states)
    g_own, g_swap = split(out_grad)

    def starts(index):
        own = jnp.where(side == 1, group - 1 - index, index)
        return own * block, (group - 1 - own) * block

    self_scalars = [dec_length, side, low * block, (group - 1 - low) * block]
    cross_scalars = [enc_length, *starts(low)]
    for r in range(1, half):
        index = (low + r) % half
        wrap = low + r >= half
        first = index * block
        second = (group - 1 - index) * block
        self_scalars += [wrap.astype(jnp.int32), first, jnp.where(wrap, first, second)]
        cross_scalars += [*starts(index)]
    self_scalars = jnp.stack([jnp.asarray(s, jnp.int32) for s in self_scalars])
    cross_scalars = jnp.stack([jnp.asarray(s, jnp.int32) for s in cross_scalars])

    q_own, kv_own, ckv_own = project(
        [x_own, e_own], [self_key, self_value, self_query, cross_key, cross_value],
        ((0, 1, 0), (0, 1, 1), (0, 0, None), (1, 2, 0), (1, 2, 1)), "project_own")
    kv_swap, q_swap = project(
        [x_swap], [self_key, self_value, self_query], ((0, 0, 0), (0, 0, 1), (0, 1, None)), "project_swap")
    ckv_swap, = project([e_swap], [cross_key, cross_value], ((0, 0, 0), (0, 0, 1)), "project_enc")

    def gathered(own, swapped):
        every = [own, swapped]
        for r in range(1, half):
            every += [lax.ppermute(own, "seq", from_shift(r)), lax.ppermute(swapped, "seq", from_shift(r))]
        return every

    kvs = gathered(kv_own, kv_swap)
    oT, probs, inverse = self_forward(self_scalars, q_own, q_swap, kvs)
    n1, r1, cq = first_norm(oT, x_own, x_swap, self_out, cross_query, ln_gain, ln_bias)
    ckvs = gathered(ckv_own, ckv_swap)
    coT, cprobs, cinverse = cross_forward(cross_scalars, cq, ckvs)
    step_of = adapter_step[side][None]
    out_own, out_swap, n2, r2, slope, g3, gai, weight_grads, sums3 = feed_forward(
        step_of, coT, n1, g_own, g_swap, cross_out, ffn_in, ffn_out, adapter_down, adapter_up, ln_gain, ln_bias)
    layer_output = joined(out_own, out_swap)

    seq_bits, dp_bits = bits(group), bits(lax.axis_size("dp"))
    steps = [("seq", seq_bits[0])] + [("dp", b) for b in dp_bits] + [("seq", b) for b in seq_bits[1:]]
    weight_grads = reduce_everywhere(weight_grads, steps)
    adapter = adapter_down.shape[1]
    adapter_up_grad = weight_grads[:adapter].astype(f32)
    adapter_down_grad = weight_grads[adapter:].astype(f32).T

    g2, caT, sums2 = feed_back(g3, slope, gai, n2, r2, ffn_in, ffn_out, adapter_down, cross_out, ln_gain)
    cdqT, *cdkvs = cross_backward(cq, cprobs, caT, coT, cinverse, ckvs)

    def returned(parts):
        own, swapped = [], []
        for r in range(1, half):
            own.append(lax.ppermute(parts[2 * r], "seq", to_shift(r)))
            swapped.append(lax.ppermute(parts[2 * r + 1], "seq", to_shift(r)))
        return own, swapped

    enc_back = returned(cdkvs)
    enc_swap = key_grad(cdkvs[1], enc_back[1], cross_key, cross_value)
    enc_own = key_grad(cdkvs[0], enc_back[0], cross_key, cross_value)
    enc_grad = joined(enc_own, enc_swap)

    g1, aT, sums1 = first_back(g2, cdqT, n1, r1, cross_query, self_out, ln_gain)
    sums = jnp.concatenate([sums1, sums2, sums3])
    sums = jnp.sum(lax.all_gather(sums, ("dp", "seq")), 0)
    dqT, *dkvs = self_backward(self_scalars, q_own, q_swap, probs, aT, oT, inverse, kvs)
    token_back = returned(dkvs)
    t_swap = token_grad(1, g1, dqT, dkvs[1], token_back[1], self_query, self_key, self_value)
    t_own = token_grad(0, g1, dqT, dkvs[0], token_back[0], self_query, self_key, self_value)
    return (
        layer_output,
        joined(t_own, t_swap),
        enc_grad,
        adapter_down_grad,
        adapter_up_grad,
        sums[0::2],
        sums[1::2],
    )


def solution(mesh):
    rows = P("dp", "seq", None)
    return jax.shard_map(
        per_device,
        mesh=mesh,
        in_specs=(rows, rows, P("dp"), P("dp"), P("dp"), rows) + (P(),) * 14,
        out_specs=(rows, rows, rows, P(), P(), P(), P()),
        check_vma=False,
    )
```

```python
import functools
import math

import jax
import jax.numpy as jnp
from jax import lax
from jax.experimental import pallas as pl
from jax.experimental.pallas import tpu as pltpu
from jax.sharding import PartitionSpec as P

HEAD_DIM = 64
PAIR = 2 * HEAD_DIM
EPS = 1e-05
NEGATIVE = -1e30
SCALE = HEAD_DIM ** (-0.5)
EXP2_SCALE = SCALE * math.log2(math.e)
HALF_LOG2E = 0.5 * math.log2(math.e)

f32 = jnp.float32
bf16 = jnp.bfloat16

NN = (((1,), (0,)), ((), ()))
NT = (((1,), (1,)), ((), ()))
TN = (((0,), (0,)), ((), ()))

HBM = pl.BlockSpec(memory_space=pltpu.HBM)
SMEM = pl.BlockSpec(memory_space=pltpu.SMEM)
VMEM = pl.BlockSpec(memory_space=pltpu.VMEM)
MIB = 2 ** 20

SIDE, CORE, HALF, LOW, HIGH, STARTS = range(6)


def dg(left, right, dims):
    return lax.dot_general(left, right, dims, preferred_element_type=f32)


def add(total, term):
    return term if total is None else total + term


def params(limit_mib):
    return pltpu.CompilerParams(vmem_limit_bytes=limit_mib * MIB)


def cost(flops, nbytes, exps=0):
    return pl.CostEstimate(flops=int(flops), bytes_accessed=int(nbytes), transcendentals=int(exps))


def shape(dims, dtype):
    return jax.ShapeDtypeStruct(dims, dtype)


def far(*arrays):
    return [pltpu.with_memory_space_constraint(x, pltpu.HBM) for x in arrays]


def far_shape(dims, dtype):
    return pltpu.HBM(dims, dtype)


def start_copies(pairs, sems):
    copies = [pltpu.make_async_copy(src, dst, sems.at[n]) for n, (src, dst) in enumerate(pairs)]
    for copy in copies:
        copy.start()
    return copies


def project_kernel(plan, n_in, sc_ref, *refs):
    count = len(plan)
    xs = refs[:n_in]
    ws = refs[n_in:n_in + count]
    n_out = 1 + max(o for _, o, _ in plan)
    outs = refs[n_in + count:n_in + count + n_out]
    x_held, held, out_held, sems, out_sems = refs[n_in + count + n_out:]
    side = sc_ref[0]
    first = [(x.at[side] if len(x.shape) == 3 else x, x_held.at[i]) for i, x in enumerate(xs)]
    copies = start_copies(first + [(w, held.at[j]) for j, w in enumerate(ws)], sems)
    for i in range(n_in):
        copies[i].wait()
    sent = []
    for j, (i, o, row) in enumerate(plan):
        copies[n_in + j].wait()
        out_held[j] = dg(x_held[i], held[j], NN).astype(bf16)
        target = outs[o] if row is None else outs[o].at[row]
        sent.append(pltpu.make_async_copy(out_held.at[j], target, out_sems.at[j]))
        sent[-1].start()
    for copy in sent:
        copy.wait()


def project(scalars, xs, ws, plan, name, pin=False):
    rows, width = xs[0].shape[-2:]
    count = len(plan)
    n_out = 1 + max(o for _, o, _ in plan)
    out_shape = []
    for o in range(n_out):
        used = [row for _, oo, row in plan if oo == o]
        out_shape.append(shape((rows, width) if used[0] is None else (len(used), rows, width), bf16))
    return pl.pallas_call(
        functools.partial(project_kernel, plan, len(xs)),
        in_specs=[SMEM] + [HBM] * (len(xs) + count),
        out_specs=[HBM] * n_out,
        out_shape=out_shape,
        scratch_shapes=[pltpu.VMEM((len(xs), rows, width), bf16), pltpu.VMEM((count, width, width), bf16),
                        pltpu.VMEM((count, rows, width), bf16),
                        pltpu.SemaphoreType.DMA((len(xs) + count,)), pltpu.SemaphoreType.DMA((count,))],
        compiler_params=params(28),
        cost_estimate=cost(2 * count * rows * width * width, 2 * count * width * width),
        name=name,
    )(scalars, *(far(*xs, *ws) if pin else (*xs, *ws)))


def pair_masks():
    lane = lax.broadcasted_iota(jnp.int32, (1, PAIR), 1)
    return lane, lane < HEAD_DIM


def key_bias(start, length, rows):
    pos = start + lax.broadcasted_iota(jnp.int32, (rows, PAIR), 0)
    lane = lax.broadcasted_iota(jnp.int32, (rows, PAIR), 1)
    masked = jnp.where(pos < length, 0.0, NEGATIVE)
    return (
        jnp.where(lane == HEAD_DIM, masked, 0.0).astype(bf16),
        jnp.where(lane == 0, masked, 0.0).astype(bf16),
    )


def queries_with_one(q, half):
    one = jnp.ones((), bf16)
    return jnp.where(half, q, one), jnp.where(half, one, q)


def head_only(x, half):
    zero = jnp.zeros((), bf16)
    return jnp.where(half, x, zero), jnp.where(half, zero, x)


def soft(scores, highest):
    return jnp.exp2((scores - highest) * EXP2_SCALE).astype(bf16)


def heads_with_ones(vT):
    ones = jnp.ones((16, vT.shape[1]), bf16)
    return [jnp.concatenate([vT[h * HEAD_DIM:(h + 1) * HEAD_DIM], ones], 0) for h in range(2)]


def top(chunks):
    highest = chunks[0].max(0, keepdims=True)
    for s in chunks[1:]:
        highest = jnp.maximum(highest, s.max(0, keepdims=True))
    return highest


def grad_columns(aT, oT, inverse):
    rows = aT.shape[1]
    sub = lax.broadcasted_iota(jnp.int32, (HEAD_DIM, rows), 0)
    zero = jnp.zeros((HEAD_DIM, rows), bf16)
    full, plain = [], []
    for h in range(2):
        sl = slice(h * HEAD_DIM, (h + 1) * HEAD_DIM)
        a = aT[sl].astype(f32) * inverse[h:h + 1]
        d = -(a * oT[sl].astype(f32)).sum(0, keepdims=True)
        high = d.astype(bf16).astype(f32)
        extra = jnp.where(sub == 0, high, jnp.where(sub == 1, d - high, 0.0)).astype(bf16)
        a = a.astype(bf16)
        full.append(jnp.concatenate([a, extra] if h == 0 else [extra, a], 0))
        plain.append(jnp.concatenate([a, zero] if h == 0 else [zero, a], 0))
    return full, plain


def values_with_ones(v, lane, half):
    first = jnp.where((lane == HEAD_DIM) | (lane == HEAD_DIM + 1), 1.0, 0.0).astype(bf16)
    second = jnp.where(lane < 2, 1.0, 0.0).astype(bf16)
    return jnp.where(half, v, first), jnp.where(half, second, v)


def cross_forward_kernel(n, per, sc_ref, len_ref, q_ref, *refs):
    kvs = refs[:n]
    oT_ref, p_ref, inv_ref, bias_ref = refs[n:]
    rows = q_ref.shape[0]
    block = kvs[0].shape[1]
    lane, half = pair_masks()

    @pl.when(pl.program_id(0) == 0)
    def _():
        length = len_ref[sc_ref[SIDE]]
        for j in range(n):
            bias_ref[0, j], bias_ref[1, j] = key_bias(sc_ref[STARTS + j], length, block)

    def prepare(u):
        lanes = slice(u * PAIR, (u + 1) * PAIR)
        keys, values = [[], []], [[], []]
        for j in range(n):
            k = kvs[j][0, :, lanes]
            keys[0].append(jnp.where(half, k, bias_ref[0, j]))
            keys[1].append(jnp.where(half, bias_ref[1, j], k))
            for h, v in enumerate(heads_with_ones(kvs[j][1, :, lanes].T)):
                values[h].append(v)
        return keys, values, queries_with_one(q_ref[:, lanes], half)

    ready = [prepare(u) for u in range(per)]
    items = [(u, b, h) for u in range(per) for b in range(rows // block) for h in range(2)]

    def score(item):
        u, b, h = item
        q = ready[u][2][h][b * block:(b + 1) * block]
        return [dg(k, q, NT) for k in ready[u][0][h]]

    later = score(items[0])
    for step, (u, b, h) in enumerate(items):
        chunks = later
        if step + 1 < len(items):
            later = score(items[step + 1])
        highest = top(chunks)
        cols = pl.ds(b * block, block)
        out = None
        for j in range(n):
            p = soft(chunks[j], highest)
            p_ref[2 * u + h, pl.ds(j * block, block), cols] = p
            out = add(out, dg(ready[u][1][h][j], p, NN))
        inverse = 1.0 / out[HEAD_DIM:HEAD_DIM + 1]
        inv_ref[u, pl.ds(h, 1), cols] = inverse
        oT_ref[pl.ds((2 * u + h) * HEAD_DIM, HEAD_DIM), cols] = (out[:HEAD_DIM] * inverse).astype(bf16)


def feature_rows(rows, per=1):
    return pl.BlockSpec((per * PAIR, rows), lambda i: (i, 0))


def feature_cols(rows, per=1):
    return pl.BlockSpec((rows, per * PAIR), lambda i: (0, i))


def kv_cols(rows, per=1):
    return pl.BlockSpec((2, rows, per * PAIR), lambda i: (0, 0, i))


def pair_block(*dims):
    return pl.BlockSpec(dims, lambda i: (i,) + (0,) * (len(dims) - 1))


CROSS_FORWARD_PAIRS, CROSS_BACKWARD_PAIRS, SELF_FORWARD_PAIRS, SELF_BACKWARD_PAIRS = 2, 2, 2, 2


def cross_forward(scalars, lengths, q, kvs):
    n = len(kvs)
    rows, width = q.shape
    block = kvs[0].shape[1]
    pairs = width // PAIR
    every = n * block
    per = CROSS_FORWARD_PAIRS
    return pl.pallas_call(
        functools.partial(cross_forward_kernel, n, per),
        grid=(pairs // per,),
        in_specs=[SMEM, SMEM, feature_cols(rows, per)] + [kv_cols(block, per)] * n,
        out_specs=[feature_rows(rows, per), pair_block(2 * per, every, rows), pair_block(per, 2, rows)],
        out_shape=[
            shape((width, rows), bf16),
            far_shape((2 * pairs, every, rows), bf16),
            shape((pairs, 2, rows), f32),
        ],
        scratch_shapes=[pltpu.VMEM((2, n, block, PAIR), bf16)],
        compiler_params=params(18),
        cost_estimate=cost(16 * rows * every * width, 4 * pairs * every * rows, 2 * pairs * every * rows),
        name="cross_forward",
    )(scalars, lengths, q, *kvs)


def cross_backward_kernel(n, per, q_ref, p_ref, aT_ref, oT_ref, inv_ref, *refs):
    kvs = refs[:n]
    dq_ref = refs[n]
    dkvs = refs[n + 1:]
    rows = q_ref.shape[0]
    block = kvs[0].shape[1]
    lane, half = pair_masks()

    def prepare(u):
        lanes = slice(u * PAIR, (u + 1) * PAIR)
        values, keysT = [[], []], []
        for j in range(n):
            first, second = values_with_ones(kvs[j][1, :, lanes], lane, half)
            values[0].append(first)
            values[1].append(second)
            keysT.append(kvs[j][0, :, lanes].T)
        full, plain = grad_columns(aT_ref[lanes], oT_ref[lanes], inv_ref[u])
        return values, keysT, head_only(q_ref[:, lanes], half), full, plain

    ready = [prepare(u) for u in range(per)]
    items = [(u, b, h) for u in range(per) for b in range(rows // block) for h in range(2)]

    def grad_probs(item):
        u, b, h = item
        a = ready[u][3][h][:, b * block:(b + 1) * block]
        return [dg(v, a, NN) for v in ready[u][0][h]]

    later = grad_probs(items[0])
    for step, (u, b, h) in enumerate(items):
        values, keysT, queries, full, plain = ready[u]
        dps = later
        if step + 1 < len(items):
            later = grad_probs(items[step + 1])
        if (b, h) == (0, 0):
            dk, dv, halves = [None] * n, [None] * n, []
        dq = None
        sl = slice(b * block, (b + 1) * block)
        for j in range(n):
            p = p_ref[2 * u + h, pl.ds(j * block, block), pl.ds(b * block, block)]
            ds = (p * dps[j]).astype(bf16)
            dv[j] = add(dv[j], dg(p, plain[h][:, sl], NT))
            dk[j] = add(dk[j], dg(ds, queries[h][sl], NN))
            dq = add(dq, dg(keysT[j][h * HEAD_DIM:(h + 1) * HEAD_DIM], ds, NN))
        halves.append((dq * SCALE).astype(bf16))
        lanes = slice(u * PAIR, (u + 1) * PAIR)
        if h == 1:
            dq_ref[sl, lanes] = jnp.concatenate(halves[-2:], 0).T
        if sl.stop == rows and h == 1:
            for j in range(n):
                dkvs[j][0, :, lanes] = (dk[j] * SCALE).astype(bf16)
                dkvs[j][1, :, lanes] = dv[j].astype(bf16)


def cross_backward(q, probs, aT, oT, inverse, kvs):
    n = len(kvs)
    rows, width = q.shape
    block = kvs[0].shape[1]
    pairs = width // PAIR
    every = n * block
    per = CROSS_BACKWARD_PAIRS
    return pl.pallas_call(
        functools.partial(cross_backward_kernel, n, per),
        grid=(pairs // per,),
        in_specs=[feature_cols(rows, per), pair_block(2 * per, every, rows), feature_rows(rows, per),
                  feature_rows(rows, per), pair_block(per, 2, rows)] + [kv_cols(block, per)] * n,
        out_specs=[feature_cols(rows, per)] + [kv_cols(block, per)] * n,
        out_shape=[shape((rows, width), bf16)] + [shape((2, block, width), bf16)] * n,
        compiler_params=params(22),
        cost_estimate=cost(32 * rows * every * width, 4 * pairs * every * rows),
        name="cross_backward",
    )(*far(q, probs), aT, *far(oT, inverse, *kvs))


def self_forward_kernel(others, per, sc_ref, len_ref, q_own, q_swap, *refs):
    kvs = refs[:2 + 2 * others]
    oT_ref, p_ref, inv_ref, tri_ref = refs[2 + 2 * others:]
    block = q_own.shape[0]
    lane, half = pair_masks()
    swapped = sc_ref[SIDE] == 1
    length = len_ref[sc_ref[SIDE]]
    first_wrap = STARTS + 2 + 2 * others
    wraps = [sc_ref[first_wrap + 3 * r] == 1 for r in range(others)]
    key_starts = [sc_ref[LOW], sc_ref[HIGH]]
    for r in range(others):
        key_starts += [sc_ref[first_wrap + 3 * r + 1], sc_ref[first_wrap + 3 * r + 2]]

    @pl.when(pl.program_id(0) == 0)
    def _():
        key = lax.broadcasted_iota(jnp.int32, (block, block), 0)
        query = lax.broadcasted_iota(jnp.int32, (block, block), 1)
        tri_ref[...] = jnp.where(key <= query, 0.0, NEGATIVE)

    biases = [key_bias(start, length, block) for start in key_starts]

    def low_high(first, second):
        return jnp.where(swapped, second, first), jnp.where(swapped, first, second)

    def prepare(u):
        lanes = slice(u * PAIR, (u + 1) * PAIR)
        q_low, q_high = low_high(q_own[:, lanes], q_swap[:, lanes])
        ks = list(low_high(kvs[0][0, :, lanes], kvs[1][0, :, lanes]))
        vs = list(low_high(kvs[0][1, :, lanes], kvs[1][1, :, lanes]))
        for r in range(others):
            first, second = low_high(kvs[2 + 2 * r][0, :, lanes], kvs[3 + 2 * r][0, :, lanes])
            ks += [first, jnp.where(wraps[r], first, second)]
            first, second = low_high(kvs[2 + 2 * r][1, :, lanes], kvs[3 + 2 * r][1, :, lanes])
            vs += [first, jnp.where(wraps[r], first, second)]
        keys = [(jnp.where(half, k, bias[0]), jnp.where(half, bias[1], k)) for k, bias in zip(ks, biases)]
        values = [heads_with_ones(v.T) for v in vs]
        ones = [queries_with_one(q_low, half), queries_with_one(q_high, half)]
        either = [tuple(jnp.where(w, ones[0][h], ones[1][h]) for h in range(2)) for w in wraps]
        return keys, values, ones, either

    ready = [prepare(u) for u in range(per)]
    tri = tri_ref[...]
    items = [(u, h) for u in range(per) for h in range(2)]

    def score(item):
        u, h = item
        keys, _, ones, either = ready[u]
        low = dg(keys[0][h], ones[0][h], NT) + tri
        high = [dg(keys[0][h], ones[1][h], NT), dg(keys[1][h], ones[1][h], NT) + tri]
        free = []
        for r in range(others):
            high.append(dg(keys[2 + 2 * r][h], ones[1][h], NT))
            free.append(dg(keys[3 + 2 * r][h], either[r][h], NT))
        return low, high, free

    later = score(items[0])
    for step, (u, h) in enumerate(items):
        values = ready[u][1]
        low, high, free = later
        if step + 1 < len(items):
            later = score(items[step + 1])
        top_low = low.max(0, keepdims=True)
        top_high = top(high)
        for r in range(others):
            peak = free[r].max(0, keepdims=True)
            top_low = jnp.where(wraps[r], jnp.maximum(top_low, peak), top_low)
            top_high = jnp.where(wraps[r], top_high, jnp.maximum(top_high, peak))

        def weigh(tile, scores, highest, v):
            p = soft(scores, highest)
            p_ref[2 * u + h, tile] = p
            return dg(v[h], p, NN)

        out_low = weigh(0, low, top_low, values[0])
        out_high = weigh(1, high[0], top_high, values[0]) + weigh(2, high[1], top_high, values[1])
        for r in range(others):
            out_high = out_high + weigh(3 + 2 * r, high[2 + r], top_high, values[2 + 2 * r])
            out = weigh(4 + 2 * r, free[r], jnp.where(wraps[r], top_low, top_high), values[3 + 2 * r])
            out_low = jnp.where(wraps[r], out_low + out, out_low)
            out_high = jnp.where(wraps[r], out_high, out_high + out)
        results = []
        for n, out in enumerate((out_low, out_high)):
            inverse = 1.0 / out[HEAD_DIM:HEAD_DIM + 1]
            inv_ref[u, n, pl.ds(h, 1), :] = inverse
            results.append((out[:HEAD_DIM] * inverse).astype(bf16))
        for n, out in enumerate(low_high(*results)):
            oT_ref[pl.ds((2 * u + h) * HEAD_DIM, HEAD_DIM), pl.ds(n * block, block)] = out


def self_forward(scalars, lengths, q_own, q_swap, kvs):
    others = len(kvs) // 2 - 1
    block, width = q_own.shape
    pairs = width // PAIR
    tiles = 3 + 2 * others
    per = SELF_FORWARD_PAIRS
    return pl.pallas_call(
        functools.partial(self_forward_kernel, others, per),
        grid=(pairs // per,),
        in_specs=[SMEM, SMEM] + [feature_cols(block, per)] * 2 + [kv_cols(block, per)] * len(kvs),
        out_specs=[feature_rows(2 * block, per), pair_block(2 * per, tiles, block, block),
                   pair_block(per, 2, 2, block)],
        out_shape=[
            shape((width, 2 * block), bf16),
            far_shape((2 * pairs, tiles, block, block), bf16),
            shape((pairs, 2, 2, block), f32),
        ],
        scratch_shapes=[pltpu.VMEM((block, block), f32)],
        compiler_params=params(16),
        cost_estimate=cost(16 * tiles * block * block * width, 4 * pairs * tiles * block * block,
                           2 * pairs * tiles * block * block),
        name="self_forward",
    )(scalars, lengths, q_own, q_swap, *kvs)


def self_backward_kernel(others, per, sc_ref, q_own, q_swap, p_ref, aT_ref, oT_ref, inv_ref, *refs):
    kvs = refs[:2 + 2 * others]
    dq_ref = refs[2 + 2 * others]
    dkvs = refs[3 + 2 * others:]
    block = q_own.shape[0]
    lane, half = pair_masks()
    swapped = sc_ref[SIDE] == 1
    first_wrap = STARTS + 2 + 2 * others
    wraps = [sc_ref[first_wrap + 3 * r] == 1 for r in range(others)]

    def low_high(first, second):
        return jnp.where(swapped, second, first), jnp.where(swapped, first, second)

    def prepare(u):
        lanes = slice(u * PAIR, (u + 1) * PAIR)
        ks = list(low_high(kvs[0][0, :, lanes], kvs[1][0, :, lanes]))
        vs = list(low_high(kvs[0][1, :, lanes], kvs[1][1, :, lanes]))
        for r in range(others):
            first, second = low_high(kvs[2 + 2 * r][0, :, lanes], kvs[3 + 2 * r][0, :, lanes])
            ks += [first, jnp.where(wraps[r], first, second)]
            first, second = low_high(kvs[2 + 2 * r][1, :, lanes], kvs[3 + 2 * r][1, :, lanes])
            vs += [first, jnp.where(wraps[r], first, second)]
        keysT = [k.T for k in ks]
        values = [values_with_ones(v, lane, half) for v in vs]
        sides = []
        a_blocks = low_high(aT_ref[lanes, 0:block], aT_ref[lanes, block:2 * block])
        o_blocks = low_high(oT_ref[lanes, 0:block], oT_ref[lanes, block:2 * block])
        q_blocks = low_high(q_own[:, lanes], q_swap[:, lanes])
        for n in range(2):
            full, plain = grad_columns(a_blocks[n], o_blocks[n], inv_ref[u, n])
            sides.append((full, plain, head_only(q_blocks[n], half)))
        for w in wraps:
            sides.append(tuple([jnp.where(w, x, y) for x, y in zip(first, second)]
                               for first, second in zip(sides[0], sides[1])))
        return keysT, values, sides

    ready = [prepare(u) for u in range(per)]
    tiles = [(0, 0, 0), (1, 0, 1), (2, 1, 1)]
    for r in range(others):
        tiles += [(3 + 2 * r, 2 + 2 * r, 1), (4 + 2 * r, 3 + 2 * r, 2 + r)]
    items = [(u, h) for u in range(per) for h in range(2)]

    def grad_probs(item):
        u, h = item
        _, values, sides = ready[u]
        return [dg(values[key][h], sides[side][0][h], NN) for _, key, side in tiles]

    later = grad_probs(items[0])
    for step, (u, h) in enumerate(items):
        keysT, _, sides = ready[u]
        dps = later
        if step + 1 < len(items):
            later = grad_probs(items[step + 1])
        if h == 0:
            dk, dv, both = [None] * len(keysT), [None] * len(keysT), []
        dq = [None] * len(sides)
        for (index, key, side), dp in zip(tiles, dps):
            p = p_ref[2 * u + h, index]
            ds = (p * dp).astype(bf16)
            dv[key] = add(dv[key], dg(p, sides[side][1][h], NT))
            dk[key] = add(dk[key], dg(ds, sides[side][2][h], NN))
            dq[side] = add(dq[side], dg(keysT[key][h * HEAD_DIM:(h + 1) * HEAD_DIM], ds, NN))
        for wrap, term in zip(wraps, dq[2:]):
            dq[0] = jnp.where(wrap, dq[0] + term, dq[0])
            dq[1] = jnp.where(wrap, dq[1], dq[1] + term)
        both.append([(x * SCALE).astype(bf16) for x in low_high(dq[0], dq[1])])
        if h == 0:
            continue
        lanes = slice(u * PAIR, (u + 1) * PAIR)
        for n in range(2):
            dq_ref[pl.ds(n * block, block), lanes] = jnp.concatenate([both[0][n], both[1][n]], 0).T

        for row, terms, factor in ((0, dk, SCALE), (1, dv, 1.0)):
            pairs = [(terms[0], terms[1])]
            for r, wrap in enumerate(wraps):
                always, either = terms[2 + 2 * r], terms[3 + 2 * r]
                pairs.append((jnp.where(wrap, always + either, always), jnp.where(wrap, 0.0, either)))
            for n, pair in enumerate(pairs):
                first, second = low_high(*pair)
                dkvs[2 * n][row, :, lanes] = (first * factor).astype(bf16)
                dkvs[2 * n + 1][row, :, lanes] = (second * factor).astype(bf16)


def self_backward(scalars, q_own, q_swap, probs, aT, oT, inverse, kvs):
    others = len(kvs) // 2 - 1
    block, width = q_own.shape
    pairs = width // PAIR
    tiles = 3 + 2 * others
    per = SELF_BACKWARD_PAIRS
    return pl.pallas_call(
        functools.partial(self_backward_kernel, others, per),
        grid=(pairs // per,),
        in_specs=[SMEM] + [feature_cols(block, per)] * 2
        + [pair_block(2 * per, tiles, block, block), feature_rows(2 * block, per), feature_rows(2 * block, per),
           pair_block(per, 2, 2, block)] + [kv_cols(block, per)] * len(kvs),
        out_specs=[feature_cols(2 * block, per)] + [kv_cols(block, per)] * len(kvs),
        out_shape=[shape((2 * block, width), bf16)] + [shape((2, block, width), bf16)] * len(kvs),
        compiler_params=params(22),
        cost_estimate=cost(32 * tiles * block * block * width, 4 * pairs * tiles * block * block),
        name="self_backward",
    )(scalars, *far(q_own, q_swap, probs), aT, *far(oT, inverse, *kvs))


ROWS = 256


def normalized(z):
    center = z - jnp.mean(z, axis=-1, keepdims=True)
    spread = jnp.mean(center * center, axis=-1, keepdims=True)
    r = lax.rsqrt(spread + EPS)
    return center * r, r


def norm_back(G, n, r, gain):
    scaled = G * gain
    return r * (scaled - jnp.mean(scaled, -1, keepdims=True) - n * jnp.mean(scaled * n, -1, keepdims=True))


def spread_lanes(r):
    return jnp.broadcast_to(r, (r.shape[0], PAIR))


def for_rows(total, body, init=0):
    count = min(ROWS, total)

    def step(i, carry):
        return body(lambda base: pl.ds(pl.multiple_of(i * count + base, count), count), carry)

    return lax.fori_loop(0, total // count, step, init)


def fold(x):
    return x.reshape(x.shape[0] // 8, 8, x.shape[1]).sum(0)


def zero_sums(count, width):
    return tuple(jnp.zeros((8, width), f32) for _ in range(count))


def store_sums(ref, sums):
    for n, total in enumerate(sums):
        ref[n:n + 1] = total.sum(0, keepdims=True)


def wait_all(copies):
    for copy in copies:
        copy.wait()


def send(src, dst, sem):
    copy = pltpu.make_async_copy(src, dst, sem)
    copy.start()
    return copy


def dma(count):
    return pltpu.SemaphoreType.DMA((count,))


def first_norm_kernel(sc_ref, oT, tokens, x_swap, w_out, w_query, gain_ref, bias_ref, n_out, r_out, cq_out,
                      oT_v, x_v, held, n_v, r_v, low_v, cq_v, sems, out_sems):
    copies = start_copies([(oT, oT_v), (w_out, held.at[0]), (tokens.at[sc_ref[SIDE]], x_v.at[0]),
                           (x_swap, x_v.at[1]), (w_query, held.at[1])], sems)
    block = x_v.shape[1]
    wait_all(copies[:2])
    n_v[...] = dg(oT_v[...], held[0], TN)
    gain, bias = gain_ref[0:1], bias_ref[0:1]
    wait_all(copies[2:4])
    for half in range(2):
        def body(at, carry, half=half):
            here = at(half * block)
            n, r = normalized(n_v[here] + x_v[half, at(0)].astype(f32))
            n_v[here] = n
            r_v[here] = spread_lanes(r)
            low_v[here] = (n * gain + bias).astype(bf16)
            return carry
        for_rows(block, body)
    sent = [send(n_v, n_out, out_sems.at[0]), send(r_v, r_out, out_sems.at[1])]
    copies[4].wait()
    cq_v[...] = dg(low_v[...], held[1], NN).astype(bf16)
    sent.append(send(cq_v, cq_out, out_sems.at[2]))
    wait_all(sent)


def first_norm(scalars, oT, tokens, x_swap, w_out, w_query, gain, bias):
    width, rows = oT.shape
    block = x_swap.shape[0]
    return pl.pallas_call(
        first_norm_kernel,
        in_specs=[SMEM] + [HBM] * 5 + [VMEM] * 2,
        out_specs=[HBM] * 3,
        out_shape=[shape((rows, width), f32), shape((rows, PAIR), f32), shape((rows, width), bf16)],
        scratch_shapes=[pltpu.VMEM((width, rows), bf16), pltpu.VMEM((2, block, width), bf16),
                        pltpu.VMEM((2, width, width), bf16), pltpu.VMEM((rows, width), f32),
                        pltpu.VMEM((rows, PAIR), f32), pltpu.VMEM((rows, width), bf16),
                        pltpu.VMEM((rows, width), bf16), dma(5), dma(3)],
        compiler_params=params(16),
        cost_estimate=cost(4 * rows * width * width, 4 * width * width + 10 * rows * width),
        name="first_norm",
    )(scalars, oT, tokens, x_swap, w_out, w_query, gain, bias)


def reciprocal(x):
    near = pl.reciprocal(x, approx=True)
    return near * (2.0 - x * near)


def gelu_parts(x):
    gauss = jnp.exp2(x * x * (-HALF_LOG2E))
    t = reciprocal(1.0 + (0.3275911 * math.sqrt(0.5)) * jnp.abs(x))
    poly = t * (0.127414796 + t * (-0.142248368 + t * (0.7107068705 + t * (-0.7265760135 + t * 0.5307027145))))
    tail = poly * gauss
    phi = jnp.where(x >= 0.0, 1.0 - tail, tail)
    return x * phi, phi + x * gauss * (1.0 / math.sqrt(2.0 * math.pi))


def feed_forward_kernel(chunk, sc_ref, step_ref, oT, n1, grads, g_swap, w_out, w_in, w_back, w_down, w_up,
                        gain_ref, bias_ref,
                        out_own, out_swap, n2_out, r2_out, slope_out, g3_out, gai_out, keep_out, send_out, sums_ref,
                        oT_v, n1_v, g_v, out_w, in_w, back_w, down_w, up_w, n2_v, r2_v, low_v, upd_v, slope_v,
                        g3_v, y_v, gai_v, wg_v, sems, in_sems, back_sems, out_sems, slope_sems):
    block = g_v.shape[1]
    rows, width = n1_v.shape
    chunks = in_w.shape[0]
    adapter = down_w.shape[1]
    side = sc_ref[SIDE]

    def in_copy(c):
        return pltpu.make_async_copy(
            w_in.at[:, pl.ds(pl.multiple_of(c * chunk, chunk), chunk)], in_w.at[c], in_sems.at[c])

    def back_copy(c):
        return pltpu.make_async_copy(
            w_back.at[pl.ds(pl.multiple_of(c * chunk, chunk), chunk)], back_w.at[c], back_sems.at[c])

    def slope_copy(c):
        cols = pl.ds(pl.multiple_of(c * chunk, chunk), chunk)
        return pltpu.make_async_copy(slope_v.at[c], slope_out.at[:, cols], slope_sems.at[c])

    copies = start_copies([(oT, oT_v), (w_out, out_w), (n1, n1_v), (w_down, down_w), (w_up, up_w),
                           (grads.at[side], g_v.at[0]), (g_swap, g_v.at[1])], sems)
    for c in range(chunks):
        in_copy(c).start()
        back_copy(c).start()

    gain1, bias1 = gain_ref[0:1], bias_ref[0:1]
    gain2, bias2 = gain_ref[1:2], bias_ref[1:2]
    gain3, bias3 = gain_ref[2:3], bias_ref[2:3]
    wait_all(copies[:2])
    n2_v[...] = dg(oT_v[...], out_w[...], TN)
    copies[2].wait()

    def second(at, carry):
        sl = at(0)
        n, r = normalized(n2_v[sl] + n1_v[sl] * gain1 + bias1)
        n2_v[sl] = n
        r2_v[sl] = spread_lanes(r)
        low_v[sl] = (n * gain2 + bias2).astype(bf16)
        return carry

    for_rows(rows, second)
    sent = [send(n2_v, n2_out, out_sems.at[0]), send(r2_v, r2_out, out_sems.at[1])]

    wait_all(copies[3:5])
    factor = (1.0 + step_ref[side].astype(f32)) * 0.25
    adapter_in = dg(low_v[...], down_w[...], NN)
    sig = 1.0 / (1.0 + jnp.exp(-adapter_in))
    adapter_hidden = (factor * (adapter_in * sig)).astype(bf16)
    adapter_slope = factor * (sig * (1.0 + adapter_in * (1.0 - sig)))
    upd_v[...] = dg(adapter_hidden, up_w[...], NN)

    def step(c, carry):
        in_copy(c).wait()
        weight = in_w[c]
        parts = [dg(low_v[pl.ds(b * block, block)], weight, NN) for b in range(2)]
        back_copy(c).wait()
        weight = back_w[c]
        for b in range(2):
            here = pl.ds(b * block, block)
            value, slope = gelu_parts(parts[b])
            slope_v[c, here] = slope.astype(bf16)
            upd_v[here] += dg(value.astype(bf16), weight, NN)
        slope_copy(c).start()
        return carry

    lax.fori_loop(0, chunks, step, 0)

    sums = zero_sums(2, width)
    wait_all(copies[5:])
    for half, target in enumerate((out_own.at[side], out_swap)):
        def third(at, carry, half=half):
            sl = at(0)
            here = at(half * block)
            n, r = normalized(n2_v[here] * gain2 + bias2 + upd_v[here])
            y_v[half, sl] = (n * gain3 + bias3).astype(bf16)
            G = g_v[half, sl].astype(f32)
            g3_v[here] = norm_back(G, n, r, gain3)
            return carry[0] + fold(G * n), carry[1] + fold(G)
        sums = for_rows(block, third, sums)
        sent.append(send(y_v.at[half], target, out_sems.at[2 + half]))
    sent.append(send(g3_v, g3_out, out_sems.at[4]))
    store_sums(sums_ref, sums)

    core, rank = sc_ref[CORE], sc_ref[HALF]

    def put(which, value):
        for n in range(2):
            start = pl.multiple_of((n ^ rank) * (adapter // 2), adapter // 2)
            wg_v[which ^ core, pl.ds(start, adapter // 2)] = value[n * (adapter // 2):(n + 1) * (adapter // 2)]

    grad_update = g3_v[...].astype(bf16)
    put(0, dg(adapter_hidden, grad_update, TN).astype(bf16))
    gai = (adapter_slope * dg(grad_update, up_w[...], NT)).astype(bf16)
    gai_v[...] = gai
    sent.append(send(gai_v, gai_out, out_sems.at[5]))
    put(1, dg(gai, low_v[...], TN).astype(bf16))
    sent.append(send(wg_v.at[0], keep_out, out_sems.at[6]))
    sent.append(send(wg_v.at[1], send_out, out_sems.at[7]))

    def drain(c, carry):
        slope_copy(c).wait()
        return carry

    lax.fori_loop(0, chunks, drain, 0)
    wait_all(sent)


def feed_forward(scalars, steps, oT, n1, grads, g_swap, w_out, w_in, w_back, w_down, w_up, gain, bias):
    rows, width = n1.shape
    block = g_swap.shape[0]
    units = w_in.shape[1]
    adapter = w_down.shape[1]
    chunk = 1024
    chunks = units // chunk
    return pl.pallas_call(
        functools.partial(feed_forward_kernel, chunk),
        in_specs=[SMEM, SMEM] + [HBM] * 9 + [VMEM] * 2,
        out_specs=[HBM] * 9 + [VMEM],
        out_shape=[
            far_shape((2, block, width), bf16), far_shape((block, width), bf16), far_shape((rows, width), f32),
            far_shape((rows, PAIR), f32), far_shape((rows, units), bf16), far_shape((rows, width), f32),
            far_shape((rows, adapter), bf16), far_shape((adapter, width), bf16), far_shape((adapter, width), bf16),
            shape((2, width), f32),
        ],
        scratch_shapes=[
            pltpu.VMEM((width, rows), bf16), pltpu.VMEM((rows, width), f32), pltpu.VMEM((2, block, width), bf16),
            pltpu.VMEM((width, width), bf16), pltpu.VMEM((chunks, width, chunk), bf16),
            pltpu.VMEM((chunks, chunk, width), bf16), pltpu.VMEM((width, adapter), bf16),
            pltpu.VMEM((adapter, width), bf16), pltpu.VMEM((rows, width), f32), pltpu.VMEM((rows, PAIR), f32),
            pltpu.VMEM((rows, width), bf16), pltpu.VMEM((rows, width), f32),
            pltpu.VMEM((chunks, rows, chunk), bf16), pltpu.VMEM((rows, width), f32),
            pltpu.VMEM((2, block, width), bf16), pltpu.VMEM((rows, adapter), bf16),
            pltpu.VMEM((2, adapter, width), bf16),
            dma(7), dma(chunks), dma(chunks), dma(8), dma(chunks),
        ],
        compiler_params=params(54),
        cost_estimate=cost(4 * rows * width * units + 12 * rows * width * adapter + 2 * rows * width * width,
                           4 * width * units, 2 * rows * units),
        name="feed_forward",
    )(scalars, steps, oT, n1, grads, g_swap, w_out, *far(w_in, w_back), w_down, w_up, gain, bias)


def feed_back_kernel(chunk, g3, slope, gai, n2, r2, w_in, w_back, w_down, w_out, gain_ref, sums3_ref,
                     g2_out, aT_out, sums_ref,
                     g2_v, slope_v, gai_v, n2_v, r2_v, out_w, in_w, back_w, down_w, low_v, aT_v,
                     sems, in_sems, back_sems, slope_sems, out_sems):
    rows, width = g2_v.shape
    chunks = in_w.shape[0]
    block = rows // 2

    def in_copy(c):
        return pltpu.make_async_copy(
            w_in.at[:, pl.ds(pl.multiple_of(c * chunk, chunk), chunk)], in_w.at[c], in_sems.at[c])

    def back_copy(c):
        return pltpu.make_async_copy(
            w_back.at[pl.ds(pl.multiple_of(c * chunk, chunk), chunk)], back_w.at[c], back_sems.at[c])

    def slope_copy(c):
        cols = pl.ds(pl.multiple_of(c * chunk, chunk), chunk)
        return pltpu.make_async_copy(slope.at[:, cols], slope_v.at[c], slope_sems.at[c])

    copies = start_copies([(g3, g2_v), (w_down, down_w), (gai, gai_v)], sems)
    for c in range(chunks):
        back_copy(c).start()
        slope_copy(c).start()
        in_copy(c).start()
    copies += [send(n2, n2_v, sems.at[3]), send(r2, r2_v, sems.at[4]), send(w_out, out_w, sems.at[5])]
    copies[0].wait()
    low_v[...] = g2_v[...].astype(bf16)
    wait_all(copies[1:3])
    g2_v[...] += dg(gai_v[...], down_w[...], NT)

    def step(c, carry):
        back_copy(c).wait()
        weight = back_w[c]
        parts = [dg(low_v[pl.ds(b * block, block)], weight, NT) for b in range(2)]
        in_copy(c).wait()
        slope_copy(c).wait()
        weight = in_w[c]
        for b in range(2):
            here = pl.ds(b * block, block)
            inner = (parts[b] * slope_v[c, here].astype(f32)).astype(bf16)
            g2_v[here] += dg(inner, weight, NT)
        return carry

    lax.fori_loop(0, chunks, step, 0)
    gain2 = gain_ref[1:2]
    wait_all(copies[3:])

    def second(at, carry):
        sl = at(0)
        G = g2_v[sl]
        n = n2_v[sl]
        grad = norm_back(G, n, r2_v[sl][:, 0:1], gain2)
        g2_v[sl] = grad
        low_v[sl] = grad.astype(bf16)
        return carry[0] + fold(G * n), carry[1] + fold(G)

    sums = for_rows(rows, second, zero_sums(2, width))
    sent = [send(g2_v, g2_out, out_sems.at[0])]
    store_sums(sums_ref, sums)
    sums_ref[2:4] = sums3_ref[...]
    aT_v[...] = dg(out_w[...], low_v[...], NT).astype(bf16)
    sent.append(send(aT_v, aT_out, out_sems.at[1]))
    wait_all(sent)


def feed_back(g3, slope, gai, n2, r2, w_in, w_back, w_down, w_out, gain, sums3):
    rows, width = g3.shape
    units = w_in.shape[1]
    adapter = w_down.shape[1]
    chunk = 1024
    chunks = units // chunk
    return pl.pallas_call(
        functools.partial(feed_back_kernel, chunk),
        in_specs=[HBM] * 9 + [VMEM] * 2,
        out_specs=[HBM] * 2 + [VMEM],
        out_shape=[shape((rows, width), f32), shape((width, rows), bf16), shape((4, width), f32)],
        scratch_shapes=[
            pltpu.VMEM((rows, width), f32), pltpu.VMEM((chunks, rows, chunk), bf16),
            pltpu.VMEM((rows, adapter), bf16), pltpu.VMEM((rows, width), f32), pltpu.VMEM((rows, PAIR), f32),
            pltpu.VMEM((width, width), bf16), pltpu.VMEM((chunks, width, chunk), bf16),
            pltpu.VMEM((chunks, chunk, width), bf16), pltpu.VMEM((width, adapter), bf16),
            pltpu.VMEM((rows, width), bf16), pltpu.VMEM((width, rows), bf16),
            dma(6), dma(chunks), dma(chunks), dma(chunks), dma(2),
        ],
        compiler_params=params(38),
        cost_estimate=cost(4 * rows * width * units + 2 * rows * width * adapter + 2 * rows * width * width,
                           4 * width * units),
        name="feed_back",
    )(*far(g3, slope), gai, *far(n2, r2, w_in, w_back), w_down, w_out, gain, sums3)


def first_back_kernel(g2, dq, n1, r1, w_query, w_out, gain_ref, sums2_ref, g1_out, aT_out, sums_ref,
                      g1_v, dq_v, n_v, r_v, held, low_v, aT_v, sems, out_sems):
    copies = start_copies([(dq, dq_v), (w_query, held.at[0]), (g2, g1_v), (n1, n_v), (r1, r_v),
                           (w_out, held.at[1])], sems)
    rows, width = g1_v.shape
    wait_all(copies[:3])
    g1_v[...] += dg(dq_v[...], held[0], NT)
    gain = gain_ref[0:1]
    wait_all(copies[3:5])

    def body(at, carry):
        sl = at(0)
        G = g1_v[sl]
        n = n_v[sl]
        grad = norm_back(G, n, r_v[sl][:, 0:1], gain)
        g1_v[sl] = grad
        low_v[sl] = grad.astype(bf16)
        return carry[0] + fold(G * n), carry[1] + fold(G)

    sums = for_rows(rows, body, zero_sums(2, width))
    sent = [send(g1_v, g1_out, out_sems.at[0])]
    store_sums(sums_ref, sums)
    sums_ref[2:6] = sums2_ref[...]
    copies[5].wait()
    aT_v[...] = dg(held[1], low_v[...], NT).astype(bf16)
    sent.append(send(aT_v, aT_out, out_sems.at[1]))
    wait_all(sent)


def first_back(g2, dq, n1, r1, w_query, w_out, gain, sums2):
    rows, width = g2.shape
    return pl.pallas_call(
        first_back_kernel,
        in_specs=[HBM] * 6 + [VMEM] * 2,
        out_specs=[HBM] * 2 + [VMEM],
        out_shape=[shape((rows, width), f32), shape((width, rows), bf16), shape((6, width), f32)],
        scratch_shapes=[pltpu.VMEM((rows, width), f32), pltpu.VMEM((rows, width), bf16),
                        pltpu.VMEM((rows, width), f32), pltpu.VMEM((rows, PAIR), f32),
                        pltpu.VMEM((2, width, width), bf16), pltpu.VMEM((rows, width), bf16),
                        pltpu.VMEM((width, rows), bf16), dma(6), dma(2)],
        compiler_params=params(18),
        cost_estimate=cost(4 * rows * width * width, 4 * width * width + 10 * rows * width),
        name="first_back",
    )(g2, dq, *far(n1, r1), w_query, w_out, gain, sums2)


def summed(first, others):
    total = first.astype(f32)
    for ref in others:
        total = total + ref.astype(f32)
    return total.astype(bf16)


def enc_grad_kernel(others, sc_ref, *refs):
    parts = refs[:2 * (1 + others)]
    w_key, w_value, own_out, swap_out, part_v, held, out_v, sems, out_sems = refs[2 * (1 + others):]
    block = out_v.shape[1]
    copies = start_copies([(w_key, held.at[0]), (w_value, held.at[1])]
                          + [(ref, part_v.at[n]) for n, ref in enumerate(parts)], sems)
    wait_all(copies)
    total = None
    for n in range(2):
        value = jnp.concatenate(
            [summed(part_v[b, n], [part_v[2 * r + b, n] for r in range(1, 1 + others)]) for b in range(2)], 0)
        total = add(total, dg(value, held[n], NT))
    sent = []
    for b, target in ((1, swap_out), (0, own_out.at[sc_ref[SIDE]])):
        out_v[b] = total[b * block:(b + 1) * block].astype(bf16)
        sent.append(send(out_v.at[b], target, out_sems.at[b]))
    wait_all(sent)


def key_grads(scalars, parts, w_key, w_value):
    _, block, width = parts[0].shape
    others = len(parts) // 2 - 1
    return pl.pallas_call(
        functools.partial(enc_grad_kernel, others),
        in_specs=[SMEM] + [HBM] * (len(parts) + 2),
        out_specs=[HBM] * 2,
        out_shape=[far_shape((2, block, width), bf16), far_shape((block, width), bf16)],
        scratch_shapes=[pltpu.VMEM((len(parts), 2, block, width), bf16), pltpu.VMEM((2, width, width), bf16),
                        pltpu.VMEM((2, block, width), bf16), dma(2 + len(parts)), dma(2)],
        compiler_params=params(18),
        cost_estimate=cost(8 * block * width * width, 4 * width * width),
        name="enc_grad",
    )(scalars, *parts, w_key, w_value)


def token_grad_kernel(others, half, sc_ref, *refs):
    g1, dq = refs[:2]
    parts = refs[2:3 + others]
    w_query, w_key, w_value, out, g1_v, dq_v, part_v, held, out_v, sems, out_sems = refs[3 + others:]
    block = out_v.shape[0]
    rows = pl.ds(half * block, block)
    copies = start_copies([(dq.at[rows], dq_v), (w_query, held.at[0]), (g1.at[rows], g1_v),
                           (w_key, held.at[1]), (w_value, held.at[2])]
                          + [(ref, part_v.at[n]) for n, ref in enumerate(parts)], sems)
    wait_all(copies[:3])
    total = g1_v[...] + dg(dq_v[...], held[0], NT)
    wait_all(copies[3:])
    for n in range(2):
        value = summed(part_v[0, n], [part_v[r, n] for r in range(1, 1 + others)])
        total = total + dg(value, held[n + 1], NT)
    out_v[...] = total.astype(bf16)
    send(out_v, out.at[sc_ref[SIDE]] if half == 0 else out, out_sems.at[0]).wait()


def token_grad(scalars, half, g1, dq, parts, w_query, w_key, w_value):
    _, block, width = parts[0].shape
    others = len(parts) - 1
    return pl.pallas_call(
        functools.partial(token_grad_kernel, others, half),
        in_specs=[SMEM] + [HBM] * (6 + others),
        out_specs=HBM,
        out_shape=far_shape((2, block, width) if half == 0 else (block, width), bf16),
        scratch_shapes=[pltpu.VMEM((block, width), f32), pltpu.VMEM((block, width), bf16),
                        pltpu.VMEM((1 + others, 2, block, width), bf16), pltpu.VMEM((3, width, width), bf16),
                        pltpu.VMEM((block, width), bf16), dma(6 + others), dma(1)],
        compiler_params=params(16),
        cost_estimate=cost(6 * block * width * width, 6 * width * width),
        name="token_grad",
    )(scalars, g1, dq, *parts, w_query, w_key, w_value)


def assemble_kernel(sc_ref, *refs):
    pieces = refs[:4]
    sums_a, sums_b, up_ref, down_ref, gains_ref, biases_ref = refs[4:]
    part = pieces[0].shape[0]
    core, rank = sc_ref[CORE], sc_ref[HALF]
    for position, piece in enumerate(pieces):
        block = (position // 2) ^ core
        at = pl.ds(pl.multiple_of(((position % 2) ^ rank) * part, part), part)

        @pl.when(block == 0)
        def _():
            up_ref[at] = piece[...].astype(f32)

        @pl.when(block == 1)
        def _():
            down_ref[:, at] = piece[...].T.astype(f32)
    total = sums_a[...] + sums_b[...]
    for n in range(3):
        gains_ref[n:n + 1] = total[2 * n:2 * n + 1]
        biases_ref[n:n + 1] = total[2 * n + 1:2 * n + 2]


def assemble(scalars, pieces, sums_a, sums_b):
    part, width = pieces[0].shape
    return pl.pallas_call(
        assemble_kernel,
        in_specs=[SMEM] + [VMEM] * 6,
        out_specs=[VMEM] * 4,
        out_shape=[shape((2 * part, width), f32), shape((width, 2 * part), f32), shape((3, width), f32),
                   shape((3, width), f32)],
        compiler_params=params(14),
        cost_estimate=cost(0, 24 * part * width),
        name="assemble",
    )(scalars, *pieces, sums_a, sums_b)


def exchange(x, step):
    axis, bit = step
    return lax.ppermute(x, axis, [(i, i ^ bit) for i in range(lax.axis_size(axis))])


def after(x, *others):
    return lax.optimization_barrier((x,) + others)[0]


def plus(x, y):
    return (x.astype(f32) + y.astype(f32)).astype(x.dtype)


def bits(size):
    return [1 << n for n in range(size.bit_length() - 1)]


def position_table(group, block, far_bit, ranks):
    half = group // 2
    table = []
    for rank in range(ranks):
        for member in range(group):
            side = member // half
            low = group - 1 - member if side else member

            def starts(index):
                own = group - 1 - index if side else index
                return [own * block, (group - 1 - own) * block]

            row = [side, member & 1, int(rank & far_bit != 0), low * block, (group - 1 - low) * block]
            row += starts(low)
            tail = []
            for r in range(1, half):
                index = (low + r) % half
                wrap = low + r >= half
                row += starts(index)
                first, second = index * block, (group - 1 - index) * block
                tail += [int(wrap), first, first if wrap else second]
            table.append(row + tail)
    return jnp.asarray(table, jnp.int32)


def per_device(
    tokens, enc_states, dec_lengths, enc_lengths, adapter_step, out_grad,
    self_query, self_key, self_value, self_out, cross_query, cross_key, cross_value, cross_out,
    ffn_in, ffn_out, adapter_down, adapter_up, ln_gain, ln_bias,
):
    group, ranks = lax.axis_size("seq"), lax.axis_size("dp")
    half = group // 2
    member = lax.axis_index("seq")
    side = member // half
    block = tokens.shape[1]
    swap = [(i, group - 1 - i) for i in range(group)]
    seq_bits, dp_bits = bits(group), bits(ranks)
    core_step, far_step, side_step = ("seq", 1), ("dp", dp_bits[1]), ("dp", 1)
    full_steps = [("dp", b) for b in dp_bits[2:]] + [("seq", b) for b in seq_bits[1:]] + [side_step]
    scalars = lax.dynamic_index_in_dim(
        position_table(group, block, far_step[1], ranks), lax.axis_index("dp") * group + member, 0, keepdims=False)

    def place(s, index):
        return group - 1 - index if s == 1 else index

    def from_shift(r):
        return [(place(s, (i + r) % half), place(s, i)) for s in range(2) for i in range(half)]

    def to_shift(r):
        return [(place(s, i), place(s, (i + r) % half)) for s in range(2) for i in range(half)]

    def theirs(x):
        return lax.dynamic_index_in_dim(x, 1 - side, 0, keepdims=False)

    def swapped(x):
        return lax.ppermute(x, "seq", swap)

    def joined(out, back):
        return lax.dynamic_update_index_in_dim(out, back, 1 - side, 0)

    def gathered(own, other):
        every = [own, other]
        for r in range(1, half):
            every += [lax.ppermute(own, "seq", from_shift(r)), lax.ppermute(other, "seq", from_shift(r))]
        return every

    def returned(parts):
        every = list(parts[:2])
        for r in range(1, half):
            every += [lax.ppermute(parts[2 * r], "seq", to_shift(r)),
                      lax.ppermute(parts[2 * r + 1], "seq", to_shift(r))]
        return every

    x_swap = swapped(theirs(tokens))
    q_own, kv_own, ckv_own = project(
        scalars, [tokens, enc_states], [self_key, self_value, self_query, cross_key, cross_value],
        ((0, 1, 0), (0, 1, 1), (0, 0, None), (1, 2, 0), (1, 2, 1)), "project_own", pin=True)
    e_theirs, g_theirs = theirs(enc_states), theirs(out_grad)
    e_swap = swapped(after(e_theirs, x_swap))
    kv_swap, q_swap = project(
        scalars, [x_swap], [self_key, self_value, self_query], ((0, 0, 0), (0, 0, 1), (0, 1, None)),
        "project_swap")
    kvs = gathered(kv_own, kv_swap)
    oT, probs, inverse = self_forward(scalars, dec_lengths, q_own, q_swap, kvs)
    ckv_swap, = project(
        scalars, [after(e_swap, oT)], [cross_key, cross_value], ((0, 0, 0), (0, 0, 1)), "project_enc")
    g_swap = swapped(after(g_theirs, e_swap))
    ckvs = gathered(ckv_own, ckv_swap)
    n1, r1, cq = first_norm(scalars, after(oT, ckv_swap), tokens, x_swap, self_out, cross_query, ln_gain, ln_bias)
    coT, cprobs, cinverse = cross_forward(scalars, enc_lengths, cq, ckvs)
    out_own, out_swap, n2, r2, slope, g3, gai, wg_keep, wg_send, sums3 = feed_forward(
        scalars, adapter_step, coT, n1, out_grad, g_swap, cross_out, ffn_in, ffn_out, adapter_down, adapter_up,
        ln_gain, ln_bias)

    wg = plus(wg_keep, exchange(wg_send, core_step))
    kept = wg.shape[0] // 2
    received = exchange(wg[kept:], far_step)
    out_back = swapped(out_swap)
    g2, caT, sums2 = feed_back(after(g3, wg), slope, gai, n2, r2, ffn_in, ffn_out, adapter_down, cross_out,
                               ln_gain, sums3)
    wg = plus(wg[:kept], after(received, g2))
    layer_output = joined(out_own, after(out_back, g2))

    received = exchange(wg, full_steps[0])
    cdq, *cdkvs = cross_backward(cq, cprobs, after(caT, wg, layer_output), coT, cinverse, ckvs)
    enc_parts = returned(cdkvs)
    for step in full_steps[1:-1]:
        wg = plus(wg, after(received, cdq))
        received = exchange(wg, step)
    g1, aT, sums = first_back(after(g2, wg), cdq, n1, r1, cross_query, self_out, ln_gain, sums2)
    received_sums = exchange(sums, core_step)
    enc_own, enc_swap = key_grads(scalars, [after(enc_parts[0], aT)] + enc_parts[1:], cross_key, cross_value)
    wg = plus(wg, after(received, enc_swap))
    sums = plus(sums, after(received_sums, enc_swap))
    received = exchange(wg, side_step)
    received_sums = exchange(sums, side_step)
    enc_back = swapped(enc_swap)

    dq, *dkvs = self_backward(scalars, q_own, q_swap, probs, after(aT, wg, sums, enc_swap), oT, inverse, kvs)
    wg = plus(wg, after(received, dq))
    sums = plus(sums, after(received_sums, dq))
    enc_grad = joined(enc_own, after(enc_back, dq))
    parts = returned([after(x, wg, sums, enc_back) for x in dkvs])
    pieces = [wg, exchange(wg, far_step), exchange(wg, core_step)]
    for bit in seq_bits[1:]:
        sums = plus(sums, exchange(sums, ("seq", bit)))
    received_sums = exchange(sums, far_step)
    t_swap = token_grad(scalars, 1, after(g1, wg, sums), dq, parts[1::2], self_query, self_key, self_value)
    t_back = swapped(t_swap)
    t_own = token_grad(scalars, 0, after(g1, t_swap), dq, parts[0::2], self_query, self_key, self_value)
    sums = plus(sums, after(received_sums, t_own))
    pieces.append(exchange(after(pieces[1], t_own), core_step))
    last_steps = [("dp", b) for b in dp_bits[2:]]
    for step in last_steps[:-1]:
        sums = plus(sums, exchange(sums, step))
    up, down, gains, biases = assemble(scalars, pieces, sums, exchange(sums, last_steps[-1]))
    return layer_output, joined(t_own, after(t_back, up)), enc_grad, down, up, gains, biases


def solution(mesh):
    rows = P("dp", "seq", None)
    return jax.shard_map(
        per_device,
        mesh=mesh,
        in_specs=(rows, rows, P("dp"), P("dp"), P("dp"), rows) + (P(),) * 14,
        out_specs=(rows, rows, rows, P(), P(), P(), P()),
        check_vma=False,
    )
```

```python
import functools
import math

import jax
import jax.numpy as jnp
from jax import lax
from jax.experimental import pallas as pl
from jax.experimental.pallas import tpu as pltpu
from jax.sharding import PartitionSpec as P

HEAD_DIM = 64
PAIR = 2 * HEAD_DIM
EPS = 1e-05
NEGATIVE = -1e30
SCALE = HEAD_DIM ** (-0.5)
EXP2_SCALE = SCALE * math.log2(math.e)
HALF_LOG2E = 0.5 * math.log2(math.e)

f32 = jnp.float32
bf16 = jnp.bfloat16

NN = (((1,), (0,)), ((), ()))
NT = (((1,), (1,)), ((), ()))
TN = (((0,), (0,)), ((), ()))

HBM = pl.BlockSpec(memory_space=pltpu.HBM)
SMEM = pl.BlockSpec(memory_space=pltpu.SMEM)
VMEM = pl.BlockSpec(memory_space=pltpu.VMEM)
MIB = 2 ** 20

SIDE, CORE, HALF, LOW, HIGH, STARTS = range(6)


def dg(left, right, dims):
    return lax.dot_general(left, right, dims, preferred_element_type=f32)


def add(total, term):
    return term if total is None else total + term


def params(limit_mib):
    return pltpu.CompilerParams(vmem_limit_bytes=limit_mib * MIB)


def cost(flops, nbytes, exps=0):
    return pl.CostEstimate(flops=int(flops), bytes_accessed=int(nbytes), transcendentals=int(exps))


def shape(dims, dtype):
    return jax.ShapeDtypeStruct(dims, dtype)


def far(*arrays):
    return [pltpu.with_memory_space_constraint(x, pltpu.HBM) for x in arrays]


def far_shape(dims, dtype):
    return pltpu.HBM(dims, dtype)


def start_copies(pairs, sems):
    copies = [pltpu.make_async_copy(src, dst, sems.at[n]) for n, (src, dst) in enumerate(pairs)]
    for copy in copies:
        copy.start()
    return copies


def project_kernel(plan, n_in, sc_ref, *refs):
    count = len(plan)
    xs = refs[:n_in]
    ws = refs[n_in:n_in + count]
    n_out = 1 + max(o for _, o, _ in plan)
    outs = refs[n_in + count:n_in + count + n_out]
    x_held, held, out_held, sems, out_sems = refs[n_in + count + n_out:]
    side = sc_ref[0]
    first = [(x.at[side] if len(x.shape) == 3 else x, x_held.at[i]) for i, x in enumerate(xs)]
    copies = start_copies(first + [(w, held.at[j]) for j, w in enumerate(ws)], sems)
    for i in range(n_in):
        copies[i].wait()
    sent = []
    for j, (i, o, row) in enumerate(plan):
        copies[n_in + j].wait()
        out_held[j] = dg(x_held[i], held[j], NN).astype(bf16)
        target = outs[o] if row is None else outs[o].at[row]
        sent.append(pltpu.make_async_copy(out_held.at[j], target, out_sems.at[j]))
        sent[-1].start()
    for copy in sent:
        copy.wait()


def project(scalars, xs, ws, plan, name, pin=False):
    rows, width = xs[0].shape[-2:]
    count = len(plan)
    n_out = 1 + max(o for _, o, _ in plan)
    out_shape = []
    for o in range(n_out):
        used = [row for _, oo, row in plan if oo == o]
        out_shape.append(shape((rows, width) if used[0] is None else (len(used), rows, width), bf16))
    return pl.pallas_call(
        functools.partial(project_kernel, plan, len(xs)),
        in_specs=[SMEM] + [HBM] * (len(xs) + count),
        out_specs=[HBM] * n_out,
        out_shape=out_shape,
        scratch_shapes=[pltpu.VMEM((len(xs), rows, width), bf16), pltpu.VMEM((count, width, width), bf16),
                        pltpu.VMEM((count, rows, width), bf16),
                        pltpu.SemaphoreType.DMA((len(xs) + count,)), pltpu.SemaphoreType.DMA((count,))],
        compiler_params=params(28),
        cost_estimate=cost(2 * count * rows * width * width, 2 * count * width * width),
        name=name,
    )(scalars, *(far(*xs, *ws) if pin else (*xs, *ws)))


def pair_masks():
    lane = lax.broadcasted_iota(jnp.int32, (1, PAIR), 1)
    return lane, lane < HEAD_DIM


def key_bias(start, length, rows):
    pos = start + lax.broadcasted_iota(jnp.int32, (rows, PAIR), 0)
    lane = lax.broadcasted_iota(jnp.int32, (rows, PAIR), 1)
    masked = jnp.where(pos < length, 0.0, NEGATIVE)
    return (
        jnp.where(lane == HEAD_DIM, masked, 0.0).astype(bf16),
        jnp.where(lane == 0, masked, 0.0).astype(bf16),
    )


def queries_with_one(q, half):
    one = jnp.ones((), bf16)
    return jnp.where(half, q, one), jnp.where(half, one, q)


def head_only(x, half):
    zero = jnp.zeros((), bf16)
    return jnp.where(half, x, zero), jnp.where(half, zero, x)


def soft(scores, highest):
    if highest is None:
        return jnp.exp2(scores * EXP2_SCALE).astype(bf16)
    return jnp.exp2((scores - highest) * EXP2_SCALE).astype(bf16)


EXPONENTS = 80.0


def scores_are_small(queries, keys):
    width = queries[0].shape[1]
    row = lax.broadcasted_iota(jnp.int32, (16, width), 0)
    lane = lax.broadcasted_iota(jnp.int32, (16, width), 1)
    pick = jnp.where(row == lane // HEAD_DIM, 1.0, 0.0).astype(bf16)

    def largest(blocks):
        total = None
        for x in blocks:
            norms = dg(pick, x * x, NT)
            total = norms if total is None else jnp.maximum(total, norms)
        return total.max(1, keepdims=True)

    limit = EXPONENTS / EXP2_SCALE / 1.02
    return jnp.max(largest(queries) * largest(keys)) <= limit * limit


def heads_with_ones(vT):
    ones = jnp.ones((16, vT.shape[1]), bf16)
    return [jnp.concatenate([vT[h * HEAD_DIM:(h + 1) * HEAD_DIM], ones], 0) for h in range(2)]


def top(chunks):
    highest = chunks[0].max(0, keepdims=True)
    for s in chunks[1:]:
        highest = jnp.maximum(highest, s.max(0, keepdims=True))
    return highest


def grad_columns(aT, oT, inverse):
    rows = aT.shape[1]
    sub = lax.broadcasted_iota(jnp.int32, (HEAD_DIM, rows), 0)
    zero = jnp.zeros((HEAD_DIM, rows), bf16)
    full, plain = [], []
    for h in range(2):
        sl = slice(h * HEAD_DIM, (h + 1) * HEAD_DIM)
        a = aT[sl].astype(f32) * inverse[h:h + 1]
        d = -(a * oT[sl].astype(f32)).sum(0, keepdims=True)
        high = d.astype(bf16).astype(f32)
        extra = jnp.where(sub == 0, high, jnp.where(sub == 1, d - high, 0.0)).astype(bf16)
        a = a.astype(bf16)
        full.append(jnp.concatenate([a, extra] if h == 0 else [extra, a], 0))
        plain.append(jnp.concatenate([a, zero] if h == 0 else [zero, a], 0))
    return full, plain


def values_with_ones(v, lane, half):
    first = jnp.where((lane == HEAD_DIM) | (lane == HEAD_DIM + 1), 1.0, 0.0).astype(bf16)
    second = jnp.where(lane < 2, 1.0, 0.0).astype(bf16)
    return jnp.where(half, v, first), jnp.where(half, second, v)


def cross_forward_kernel(n, per, sc_ref, len_ref, q_ref, *refs):
    kvs = refs[:n]
    oT_ref, p_ref, inv_ref, bias_ref = refs[n:]
    rows = q_ref.shape[0]
    block = kvs[0].shape[1]
    lane, half = pair_masks()

    @pl.when(pl.program_id(0) == 0)
    def _():
        length = len_ref[sc_ref[SIDE]]
        for j in range(n):
            bias_ref[0, j], bias_ref[1, j] = key_bias(sc_ref[STARTS + j], length, block)

    def prepare(u):
        lanes = slice(u * PAIR, (u + 1) * PAIR)
        keys, values = [[], []], [[], []]
        for j in range(n):
            k = kvs[j][0, :, lanes]
            keys[0].append(jnp.where(half, k, bias_ref[0, j]))
            keys[1].append(jnp.where(half, bias_ref[1, j], k))
            for h, v in enumerate(heads_with_ones(kvs[j][1, :, lanes].T)):
                values[h].append(v)
        return keys, values, queries_with_one(q_ref[:, lanes], half)

    items = [(u, b, h) for u in range(per) for b in range(rows // block) for h in range(2)]

    def attend(small):
        ready = [prepare(u) for u in range(per)]

        def score(item):
            u, b, h = item
            q = ready[u][2][h][b * block:(b + 1) * block]
            return [dg(k, q, NT) for k in ready[u][0][h]]

        later = score(items[0])
        for step, (u, b, h) in enumerate(items):
            chunks = later
            if step + 1 < len(items):
                later = score(items[step + 1])
            highest = None if small else top(chunks)
            cols = pl.ds(b * block, block)
            out = None
            for j in range(n):
                p = soft(chunks[j], highest)
                p_ref[2 * u + h, pl.ds(j * block, block), cols] = p
                out = add(out, dg(ready[u][1][h][j], p, NN))
            inverse = 1.0 / out[HEAD_DIM:HEAD_DIM + 1]
            inv_ref[u, pl.ds(h, 1), cols] = inverse
            oT_ref[pl.ds((2 * u + h) * HEAD_DIM, HEAD_DIM), cols] = (out[:HEAD_DIM] * inverse).astype(bf16)

    small = scores_are_small([q_ref[:block], q_ref[block:]], [kv[0] for kv in kvs])
    pl.when(small)(lambda: attend(True))
    pl.when(jnp.logical_not(small))(lambda: attend(False))


def feature_rows(rows, per=1):
    return pl.BlockSpec((per * PAIR, rows), lambda i: (i, 0))


def feature_cols(rows, per=1):
    return pl.BlockSpec((rows, per * PAIR), lambda i: (0, i))


def kv_cols(rows, per=1):
    return pl.BlockSpec((2, rows, per * PAIR), lambda i: (0, 0, i))


def pair_block(*dims):
    return pl.BlockSpec(dims, lambda i: (i,) + (0,) * (len(dims) - 1))


CROSS_FORWARD_PAIRS, CROSS_BACKWARD_PAIRS, SELF_FORWARD_PAIRS, SELF_BACKWARD_PAIRS = 2, 2, 2, 2


def cross_forward(scalars, lengths, q, kvs):
    n = len(kvs)
    rows, width = q.shape
    block = kvs[0].shape[1]
    pairs = width // PAIR
    every = n * block
    per = CROSS_FORWARD_PAIRS
    return pl.pallas_call(
        functools.partial(cross_forward_kernel, n, per),
        grid=(pairs // per,),
        in_specs=[SMEM, SMEM, feature_cols(rows, per)] + [kv_cols(block, per)] * n,
        out_specs=[feature_rows(rows, per), pair_block(2 * per, every, rows), pair_block(per, 2, rows)],
        out_shape=[
            far_shape((width, rows), bf16),
            far_shape((2 * pairs, every, rows), bf16),
            far_shape((pairs, 2, rows), f32),
        ],
        scratch_shapes=[pltpu.VMEM((2, n, block, PAIR), bf16)],
        compiler_params=params(18),
        cost_estimate=cost(16 * rows * every * width, 4 * pairs * every * rows, 2 * pairs * every * rows),
        name="cross_forward",
    )(scalars, lengths, q, *kvs)


def cross_backward_kernel(n, per, q_ref, p_ref, aT_ref, oT_ref, inv_ref, *refs):
    kvs = refs[:n]
    dq_ref = refs[n]
    dkvs = refs[n + 1:]
    rows = q_ref.shape[0]
    block = kvs[0].shape[1]
    lane, half = pair_masks()

    def prepare(u):
        lanes = slice(u * PAIR, (u + 1) * PAIR)
        values, keysT = [[], []], []
        for j in range(n):
            first, second = values_with_ones(kvs[j][1, :, lanes], lane, half)
            values[0].append(first)
            values[1].append(second)
            keysT.append(kvs[j][0, :, lanes].T)
        full, plain = grad_columns(aT_ref[lanes], oT_ref[lanes], inv_ref[u])
        return values, keysT, head_only(q_ref[:, lanes], half), full, plain

    ready = [prepare(u) for u in range(per)]
    items = [(u, b, h) for u in range(per) for b in range(rows // block) for h in range(2)]

    def grad_probs(item):
        u, b, h = item
        a = ready[u][3][h][:, b * block:(b + 1) * block]
        return [dg(v, a, NN) for v in ready[u][0][h]]

    later = grad_probs(items[0])
    for step, (u, b, h) in enumerate(items):
        values, keysT, queries, full, plain = ready[u]
        dps = later
        if step + 1 < len(items):
            later = grad_probs(items[step + 1])
        if (b, h) == (0, 0):
            dk, dv, halves = [None] * n, [None] * n, []
        dq = None
        sl = slice(b * block, (b + 1) * block)
        for j in range(n):
            p = p_ref[2 * u + h, pl.ds(j * block, block), pl.ds(b * block, block)]
            ds = (p * dps[j]).astype(bf16)
            dv[j] = add(dv[j], dg(p, plain[h][:, sl], NT))
            dk[j] = add(dk[j], dg(ds, queries[h][sl], NN))
            dq = add(dq, dg(keysT[j][h * HEAD_DIM:(h + 1) * HEAD_DIM], ds, NN))
        halves.append((dq * SCALE).astype(bf16))
        lanes = slice(u * PAIR, (u + 1) * PAIR)
        if h == 1:
            dq_ref[sl, lanes] = jnp.concatenate(halves[-2:], 0).T
        if sl.stop == rows and h == 1:
            for j in range(n):
                dkvs[j][0, :, lanes] = (dk[j] * SCALE).astype(bf16)
                dkvs[j][1, :, lanes] = dv[j].astype(bf16)


def cross_backward(q, probs, aT, oT, inverse, kvs):
    n = len(kvs)
    rows, width = q.shape
    block = kvs[0].shape[1]
    pairs = width // PAIR
    every = n * block
    per = CROSS_BACKWARD_PAIRS
    return pl.pallas_call(
        functools.partial(cross_backward_kernel, n, per),
        grid=(pairs // per,),
        in_specs=[feature_cols(rows, per), pair_block(2 * per, every, rows), feature_rows(rows, per),
                  feature_rows(rows, per), pair_block(per, 2, rows)] + [kv_cols(block, per)] * n,
        out_specs=[feature_cols(rows, per)] + [kv_cols(block, per)] * n,
        out_shape=[shape((rows, width), bf16)] + [shape((2, block, width), bf16)] * n,
        compiler_params=params(22),
        cost_estimate=cost(32 * rows * every * width, 4 * pairs * every * rows),
        name="cross_backward",
    )(*far(q, probs), aT, *far(oT, inverse, *kvs))


def self_forward_kernel(others, per, sc_ref, len_ref, q_own, q_swap, *refs):
    kvs = refs[:2 + 2 * others]
    oT_ref, p_ref, inv_ref, tri_ref = refs[2 + 2 * others:]
    block = q_own.shape[0]
    lane, half = pair_masks()
    swapped = sc_ref[SIDE] == 1
    length = len_ref[sc_ref[SIDE]]
    first_wrap = STARTS + 2 + 2 * others
    wraps = [sc_ref[first_wrap + 3 * r] == 1 for r in range(others)]
    key_starts = [sc_ref[LOW], sc_ref[HIGH]]
    for r in range(others):
        key_starts += [sc_ref[first_wrap + 3 * r + 1], sc_ref[first_wrap + 3 * r + 2]]

    @pl.when(pl.program_id(0) == 0)
    def _():
        key = lax.broadcasted_iota(jnp.int32, (block, block), 0)
        query = lax.broadcasted_iota(jnp.int32, (block, block), 1)
        tri_ref[...] = jnp.where(key <= query, 0.0, NEGATIVE)

    biases = [key_bias(start, length, block) for start in key_starts]

    def low_high(first, second):
        return jnp.where(swapped, second, first), jnp.where(swapped, first, second)

    def prepare(u):
        lanes = slice(u * PAIR, (u + 1) * PAIR)
        q_low, q_high = low_high(q_own[:, lanes], q_swap[:, lanes])
        ks = list(low_high(kvs[0][0, :, lanes], kvs[1][0, :, lanes]))
        vs = list(low_high(kvs[0][1, :, lanes], kvs[1][1, :, lanes]))
        for r in range(others):
            first, second = low_high(kvs[2 + 2 * r][0, :, lanes], kvs[3 + 2 * r][0, :, lanes])
            ks += [first, jnp.where(wraps[r], first, second)]
            first, second = low_high(kvs[2 + 2 * r][1, :, lanes], kvs[3 + 2 * r][1, :, lanes])
            vs += [first, jnp.where(wraps[r], first, second)]
        keys = [(jnp.where(half, k, bias[0]), jnp.where(half, bias[1], k)) for k, bias in zip(ks, biases)]
        values = [heads_with_ones(v.T) for v in vs]
        ones = [queries_with_one(q_low, half), queries_with_one(q_high, half)]
        either = [tuple(jnp.where(w, ones[0][h], ones[1][h]) for h in range(2)) for w in wraps]
        return keys, values, ones, either

    def attend(small):
        ready = [prepare(u) for u in range(per)]
        tri = tri_ref[...]
        items = [(u, h) for u in range(per) for h in range(2)]

        def score(item):
            u, h = item
            keys, _, ones, either = ready[u]
            low = dg(keys[0][h], ones[0][h], NT) + tri
            high = [dg(keys[0][h], ones[1][h], NT), dg(keys[1][h], ones[1][h], NT) + tri]
            free = []
            for r in range(others):
                high.append(dg(keys[2 + 2 * r][h], ones[1][h], NT))
                free.append(dg(keys[3 + 2 * r][h], either[r][h], NT))
            return low, high, free

        later = score(items[0])
        for step, (u, h) in enumerate(items):
            values = ready[u][1]
            low, high, free = later
            if step + 1 < len(items):
                later = score(items[step + 1])
            top_low, top_high = None, None
            if not small:
                top_low = low.max(0, keepdims=True)
                top_high = top(high)
                for r in range(others):
                    peak = free[r].max(0, keepdims=True)
                    top_low = jnp.where(wraps[r], jnp.maximum(top_low, peak), top_low)
                    top_high = jnp.where(wraps[r], top_high, jnp.maximum(top_high, peak))

            def weigh(tile, scores, highest, v):
                p = soft(scores, highest)
                p_ref[2 * u + h, tile] = p
                return dg(v[h], p, NN)

            out_low = weigh(0, low, top_low, values[0])
            out_high = weigh(1, high[0], top_high, values[0]) + weigh(2, high[1], top_high, values[1])
            for r in range(others):
                out_high = out_high + weigh(3 + 2 * r, high[2 + r], top_high, values[2 + 2 * r])
                highest = None if small else jnp.where(wraps[r], top_low, top_high)
                out = weigh(4 + 2 * r, free[r], highest, values[3 + 2 * r])
                out_low = jnp.where(wraps[r], out_low + out, out_low)
                out_high = jnp.where(wraps[r], out_high, out_high + out)
            results = []
            for n, out in enumerate((out_low, out_high)):
                inverse = 1.0 / out[HEAD_DIM:HEAD_DIM + 1]
                inv_ref[u, n, pl.ds(h, 1), :] = inverse
                results.append((out[:HEAD_DIM] * inverse).astype(bf16))
            for n, out in enumerate(low_high(*results)):
                oT_ref[pl.ds((2 * u + h) * HEAD_DIM, HEAD_DIM), pl.ds(n * block, block)] = out

    small = scores_are_small([q_own[...], q_swap[...]], [kv[0] for kv in kvs])
    pl.when(small)(lambda: attend(True))
    pl.when(jnp.logical_not(small))(lambda: attend(False))


def self_forward(scalars, lengths, q_own, q_swap, kvs):
    others = len(kvs) // 2 - 1
    block, width = q_own.shape
    pairs = width // PAIR
    tiles = 3 + 2 * others
    per = SELF_FORWARD_PAIRS
    return pl.pallas_call(
        functools.partial(self_forward_kernel, others, per),
        grid=(pairs // per,),
        in_specs=[SMEM, SMEM] + [feature_cols(block, per)] * 2 + [kv_cols(block, per)] * len(kvs),
        out_specs=[feature_rows(2 * block, per), pair_block(2 * per, tiles, block, block),
                   pair_block(per, 2, 2, block)],
        out_shape=[
            shape((width, 2 * block), bf16),
            far_shape((2 * pairs, tiles, block, block), bf16),
            far_shape((pairs, 2, 2, block), f32),
        ],
        scratch_shapes=[pltpu.VMEM((block, block), f32)],
        compiler_params=params(16),
        cost_estimate=cost(16 * tiles * block * block * width, 4 * pairs * tiles * block * block,
                           2 * pairs * tiles * block * block),
        name="self_forward",
    )(scalars, lengths, q_own, q_swap, *kvs)


def self_backward_kernel(others, per, sc_ref, q_own, q_swap, p_ref, aT_ref, oT_ref, inv_ref, *refs):
    kvs = refs[:2 + 2 * others]
    dq_ref = refs[2 + 2 * others]
    dkvs = refs[3 + 2 * others:]
    block = q_own.shape[0]
    lane, half = pair_masks()
    swapped = sc_ref[SIDE] == 1
    first_wrap = STARTS + 2 + 2 * others
    wraps = [sc_ref[first_wrap + 3 * r] == 1 for r in range(others)]

    def low_high(first, second):
        return jnp.where(swapped, second, first), jnp.where(swapped, first, second)

    def prepare(u):
        lanes = slice(u * PAIR, (u + 1) * PAIR)
        ks = list(low_high(kvs[0][0, :, lanes], kvs[1][0, :, lanes]))
        vs = list(low_high(kvs[0][1, :, lanes], kvs[1][1, :, lanes]))
        for r in range(others):
            first, second = low_high(kvs[2 + 2 * r][0, :, lanes], kvs[3 + 2 * r][0, :, lanes])
            ks += [first, jnp.where(wraps[r], first, second)]
            first, second = low_high(kvs[2 + 2 * r][1, :, lanes], kvs[3 + 2 * r][1, :, lanes])
            vs += [first, jnp.where(wraps[r], first, second)]
        keysT = [k.T for k in ks]
        values = [values_with_ones(v, lane, half) for v in vs]
        sides = []
        a_blocks = low_high(aT_ref[lanes, 0:block], aT_ref[lanes, block:2 * block])
        o_blocks = low_high(oT_ref[lanes, 0:block], oT_ref[lanes, block:2 * block])
        q_blocks = low_high(q_own[:, lanes], q_swap[:, lanes])
        for n in range(2):
            full, plain = grad_columns(a_blocks[n], o_blocks[n], inv_ref[u, n])
            sides.append((full, plain, head_only(q_blocks[n], half)))
        for w in wraps:
            sides.append(tuple([jnp.where(w, x, y) for x, y in zip(first, second)]
                               for first, second in zip(sides[0], sides[1])))
        return keysT, values, sides

    ready = [prepare(u) for u in range(per)]
    tiles = [(0, 0, 0), (1, 0, 1), (2, 1, 1)]
    for r in range(others):
        tiles += [(3 + 2 * r, 2 + 2 * r, 1), (4 + 2 * r, 3 + 2 * r, 2 + r)]
    items = [(u, h) for u in range(per) for h in range(2)]

    def grad_probs(item):
        u, h = item
        _, values, sides = ready[u]
        return [dg(values[key][h], sides[side][0][h], NN) for _, key, side in tiles]

    later = grad_probs(items[0])
    for step, (u, h) in enumerate(items):
        keysT, _, sides = ready[u]
        dps = later
        if step + 1 < len(items):
            later = grad_probs(items[step + 1])
        if h == 0:
            dk, dv, both = [None] * len(keysT), [None] * len(keysT), []
        dq = [None] * len(sides)
        for (index, key, side), dp in zip(tiles, dps):
            p = p_ref[2 * u + h, index]
            ds = (p * dp).astype(bf16)
            dv[key] = add(dv[key], dg(p, sides[side][1][h], NT))
            dk[key] = add(dk[key], dg(ds, sides[side][2][h], NN))
            dq[side] = add(dq[side], dg(keysT[key][h * HEAD_DIM:(h + 1) * HEAD_DIM], ds, NN))
        for wrap, term in zip(wraps, dq[2:]):
            dq[0] = jnp.where(wrap, dq[0] + term, dq[0])
            dq[1] = jnp.where(wrap, dq[1], dq[1] + term)
        both.append([(x * SCALE).astype(bf16) for x in low_high(dq[0], dq[1])])
        if h == 0:
            continue
        lanes = slice(u * PAIR, (u + 1) * PAIR)
        for n in range(2):
            dq_ref[pl.ds(n * block, block), lanes] = jnp.concatenate([both[0][n], both[1][n]], 0).T

        for row, terms, factor in ((0, dk, SCALE), (1, dv, 1.0)):
            pairs = [(terms[0], terms[1])]
            for r, wrap in enumerate(wraps):
                always, either = terms[2 + 2 * r], terms[3 + 2 * r]
                pairs.append((jnp.where(wrap, always + either, always), jnp.where(wrap, 0.0, either)))
            for n, pair in enumerate(pairs):
                first, second = low_high(*pair)
                dkvs[2 * n][row, :, lanes] = (first * factor).astype(bf16)
                dkvs[2 * n + 1][row, :, lanes] = (second * factor).astype(bf16)


def self_backward(scalars, q_own, q_swap, probs, aT, oT, inverse, kvs):
    others = len(kvs) // 2 - 1
    block, width = q_own.shape
    pairs = width // PAIR
    tiles = 3 + 2 * others
    per = SELF_BACKWARD_PAIRS
    return pl.pallas_call(
        functools.partial(self_backward_kernel, others, per),
        grid=(pairs // per,),
        in_specs=[SMEM] + [feature_cols(block, per)] * 2
        + [pair_block(2 * per, tiles, block, block), feature_rows(2 * block, per), feature_rows(2 * block, per),
           pair_block(per, 2, 2, block)] + [kv_cols(block, per)] * len(kvs),
        out_specs=[feature_cols(2 * block, per)] + [kv_cols(block, per)] * len(kvs),
        out_shape=[shape((2 * block, width), bf16)] + [shape((2, block, width), bf16)] * len(kvs),
        compiler_params=params(22),
        cost_estimate=cost(32 * tiles * block * block * width, 4 * pairs * tiles * block * block),
        name="self_backward",
    )(scalars, *far(q_own, q_swap, probs), aT, *far(oT, inverse, *kvs))


ROWS = 256


def normalized(z):
    center = z - jnp.mean(z, axis=-1, keepdims=True)
    spread = jnp.mean(center * center, axis=-1, keepdims=True)
    r = lax.rsqrt(spread + EPS)
    return center * r, r


def norm_back(G, n, r, gain):
    scaled = G * gain
    return r * (scaled - jnp.mean(scaled, -1, keepdims=True) - n * jnp.mean(scaled * n, -1, keepdims=True))


def spread_lanes(r):
    return jnp.broadcast_to(r, (r.shape[0], PAIR))


def for_rows(total, body, init=0):
    count = min(ROWS, total)

    def step(i, carry):
        return body(lambda base: pl.ds(pl.multiple_of(i * count + base, count), count), carry)

    return lax.fori_loop(0, total // count, step, init)


def fold(x):
    return x.reshape(x.shape[0] // 8, 8, x.shape[1]).sum(0)


def zero_sums(count, width):
    return tuple(jnp.zeros((8, width), f32) for _ in range(count))


def store_sums(ref, sums):
    for n, total in enumerate(sums):
        ref[n:n + 1] = total.sum(0, keepdims=True)


def wait_all(copies):
    for copy in copies:
        copy.wait()


def send(src, dst, sem):
    copy = pltpu.make_async_copy(src, dst, sem)
    copy.start()
    return copy


def dma(count):
    return pltpu.SemaphoreType.DMA((count,))


def first_norm_kernel(sc_ref, oT, tokens, x_swap, w_out, w_query, gain_ref, bias_ref, n_out, r_out, cq_out,
                      oT_v, x_v, held, n_v, r_v, low_v, cq_v, sems, out_sems):
    copies = start_copies([(oT, oT_v), (w_out, held.at[0]), (tokens.at[sc_ref[SIDE]], x_v.at[0]),
                           (x_swap, x_v.at[1]), (w_query, held.at[1])], sems)
    block = x_v.shape[1]
    wait_all(copies[:2])
    n_v[...] = dg(oT_v[...], held[0], TN)
    gain, bias = gain_ref[0:1], bias_ref[0:1]
    wait_all(copies[2:4])
    for half in range(2):
        def body(at, carry, half=half):
            here = at(half * block)
            n, r = normalized(n_v[here] + x_v[half, at(0)].astype(f32))
            n_v[here] = n
            r_v[here] = spread_lanes(r)
            low_v[here] = (n * gain + bias).astype(bf16)
            return carry
        for_rows(block, body)
    sent = [send(n_v, n_out, out_sems.at[0]), send(r_v, r_out, out_sems.at[1])]
    copies[4].wait()
    cq_v[...] = dg(low_v[...], held[1], NN).astype(bf16)
    sent.append(send(cq_v, cq_out, out_sems.at[2]))
    wait_all(sent)


def first_norm(scalars, oT, tokens, x_swap, w_out, w_query, gain, bias):
    width, rows = oT.shape
    block = x_swap.shape[0]
    return pl.pallas_call(
        first_norm_kernel,
        in_specs=[SMEM] + [HBM] * 5 + [VMEM] * 2,
        out_specs=[HBM] * 3,
        out_shape=[far_shape((rows, width), f32), far_shape((rows, PAIR), f32), shape((rows, width), bf16)],
        scratch_shapes=[pltpu.VMEM((width, rows), bf16), pltpu.VMEM((2, block, width), bf16),
                        pltpu.VMEM((2, width, width), bf16), pltpu.VMEM((rows, width), f32),
                        pltpu.VMEM((rows, PAIR), f32), pltpu.VMEM((rows, width), bf16),
                        pltpu.VMEM((rows, width), bf16), dma(5), dma(3)],
        compiler_params=params(16),
        cost_estimate=cost(4 * rows * width * width, 4 * width * width + 10 * rows * width),
        name="first_norm",
    )(scalars, oT, tokens, x_swap, w_out, w_query, gain, bias)


def gelu_parts(x):
    phi = 0.5 + 0.5 * lax.erf(x * math.sqrt(0.5))
    gauss = jnp.exp2(x * x * (-HALF_LOG2E))
    return x * phi, phi + x * gauss * (1.0 / math.sqrt(2.0 * math.pi))


def feed_forward_kernel(chunk, sc_ref, step_ref, oT, n1, grads, g_swap, w_out, w_in, w_back, w_down, w_up,
                        gain_ref, bias_ref,
                        out_own, out_swap, n2_out, r2_out, slope_out, g3_out, gai_out, wg_out0, wg_out1, wg_out2, wg_out3, sums_ref,
                        oT_v, g_v, out_w, in_w, back_w, down_w, up_w, n2_v, r2_v, low_v, upd_v, slope_v,
                        y_v, gai_v, wg_v, sems, in_sems, back_sems, out_sems, slope_sems):
    block = g_v.shape[1]
    rows, width = upd_v.shape
    chunks = in_w.shape[0]
    adapter = down_w.shape[1]
    side = sc_ref[SIDE]
    wg_outs = (wg_out0, wg_out1, wg_out2, wg_out3)

    def in_copy(c):
        return pltpu.make_async_copy(
            w_in.at[:, pl.ds(pl.multiple_of(c * chunk, chunk), chunk)], in_w.at[c], in_sems.at[c])

    def back_copy(c):
        return pltpu.make_async_copy(
            w_back.at[pl.ds(pl.multiple_of(c * chunk, chunk), chunk)], back_w.at[c], back_sems.at[c])

    def slope_copy(c):
        cols = pl.ds(pl.multiple_of(c * chunk, chunk), chunk)
        return pltpu.make_async_copy(slope_v.at[c], slope_out.at[:, cols], slope_sems.at[c])

    copies = [pltpu.make_async_copy(src, dst, sems.at[n]) for n, (src, dst) in enumerate(
        ((oT, oT_v), (w_out, out_w), (n1, upd_v), (w_down, down_w), (w_up, up_w),
         (grads.at[side], g_v.at[0]), (g_swap, g_v.at[1])))]
    for copy in copies[:3]:
        copy.start()
    in_copy(0).start()

    gain1, bias1 = gain_ref[0:1], bias_ref[0:1]
    gain2, bias2 = gain_ref[1:2], bias_ref[1:2]
    gain3, bias3 = gain_ref[2:3], bias_ref[2:3]
    wait_all(copies[:2])
    for copy in copies[3:5]:
        copy.start()
    back_copy(0).start()
    n2_v[...] = dg(oT_v[...], out_w[...], TN)
    copies[2].wait()
    for c in range(1, chunks):
        in_copy(c).start()
        back_copy(c).start()
        if c == 1:
            for copy in copies[5:]:
                copy.start()

    def second(at, carry):
        sl = at(0)
        n, r = normalized(n2_v[sl] + upd_v[sl] * gain1 + bias1)
        n2_v[sl] = n
        r2_v[sl] = spread_lanes(r)
        low_v[sl] = (n * gain2 + bias2).astype(bf16)
        return carry

    for_rows(rows, second)
    sent = [send(n2_v, n2_out, out_sems.at[0]), send(r2_v, r2_out, out_sems.at[1])]

    wait_all(copies[3:5])
    factor = (1.0 + step_ref[side].astype(f32)) * 0.25
    adapter_in = dg(low_v[...], down_w[...], NN)
    sig = 1.0 / (1.0 + jnp.exp(-adapter_in))
    adapter_hidden = (factor * (adapter_in * sig)).astype(bf16)
    adapter_slope = factor * (sig * (1.0 + adapter_in * (1.0 - sig)))
    upd_v[...] = dg(adapter_hidden, up_w[...], NN)

    def step(c, carry):
        in_copy(c).wait()
        weight = in_w[c]
        parts = [dg(low_v[pl.ds(b * block, block)], weight, NN) for b in range(2)]
        back_copy(c).wait()
        weight = back_w[c]
        for b in range(2):
            here = pl.ds(b * block, block)
            value, slope = gelu_parts(parts[b])
            slope_v[c, here] = slope.astype(bf16)
            upd_v[here] += dg(value.astype(bf16), weight, NN)
        slope_copy(c).start()
        return carry

    lax.fori_loop(0, chunks, step, 0)

    sums = zero_sums(2, width)
    wait_all(copies[5:])
    for half, target in enumerate((out_own.at[side], out_swap)):
        def third(at, carry, half=half):
            sl = at(0)
            here = at(half * block)
            n, r = normalized(n2_v[here] * gain2 + bias2 + upd_v[here])
            y_v[half, sl] = (n * gain3 + bias3).astype(bf16)
            G = g_v[half, sl].astype(f32)
            upd_v[here] = norm_back(G, n, r, gain3)
            return carry[0] + fold(G * n), carry[1] + fold(G)
        sums = for_rows(block, third, sums)
        sent.append(send(y_v.at[half], target, out_sems.at[2 + half]))
    sent.append(send(upd_v, g3_out, out_sems.at[4]))
    store_sums(sums_ref, sums)

    core, rank = sc_ref[CORE], sc_ref[HALF]

    def put(which, value):
        part = adapter // 2
        for n in range(2):
            wg_v[2 * (which ^ core) + (n ^ rank)] = value[n * part:(n + 1) * part]

    grad_update = upd_v[...].astype(bf16)
    put(0, dg(adapter_hidden, grad_update, TN).astype(bf16))
    gai = (adapter_slope * dg(grad_update, up_w[...], NT)).astype(bf16)
    gai_v[...] = gai
    sent.append(send(gai_v, gai_out, out_sems.at[5]))
    put(1, dg(gai, low_v[...], TN).astype(bf16))
    for n in (3, 1, 2, 0):
        sent.append(send(wg_v.at[n], wg_outs[n], out_sems.at[6 + n]))

    def drain(c, carry):
        slope_copy(c).wait()
        return carry

    lax.fori_loop(0, chunks, drain, 0)
    wait_all(sent)


def feed_forward(scalars, steps, oT, n1, grads, g_swap, w_out, w_in, w_back, w_down, w_up, gain, bias):
    rows, width = n1.shape
    block = g_swap.shape[0]
    units = w_in.shape[1]
    adapter = w_down.shape[1]
    chunk = 1024
    chunks = units // chunk
    return pl.pallas_call(
        functools.partial(feed_forward_kernel, chunk),
        in_specs=[SMEM, SMEM] + [HBM] * 9 + [VMEM] * 2,
        out_specs=[HBM] * 11 + [VMEM],
        out_shape=[
            far_shape((2, block, width), bf16), far_shape((block, width), bf16), far_shape((rows, width), f32),
            far_shape((rows, PAIR), f32), far_shape((rows, units), bf16), far_shape((rows, width), f32),
            far_shape((rows, adapter), bf16)]
        + [far_shape((adapter // 2, width), bf16)] * 4 + [
            shape((2, width), f32),
        ],
        scratch_shapes=[
            pltpu.VMEM((width, rows), bf16), pltpu.VMEM((2, block, width), bf16),
            pltpu.VMEM((width, width), bf16), pltpu.VMEM((chunks, width, chunk), bf16),
            pltpu.VMEM((chunks, chunk, width), bf16), pltpu.VMEM((width, adapter), bf16),
            pltpu.VMEM((adapter, width), bf16), pltpu.VMEM((rows, width), f32), pltpu.VMEM((rows, PAIR), f32),
            pltpu.VMEM((rows, width), bf16), pltpu.VMEM((rows, width), f32),
            pltpu.VMEM((chunks, rows, chunk), bf16),
            pltpu.VMEM((2, block, width), bf16), pltpu.VMEM((rows, adapter), bf16),
            pltpu.VMEM((4, adapter // 2, width), bf16),
            dma(7), dma(chunks), dma(chunks), dma(10), dma(chunks),
        ],
        compiler_params=params(50),
        cost_estimate=cost(4 * rows * width * units + 12 * rows * width * adapter + 2 * rows * width * width,
                           4 * width * units, 2 * rows * units),
        name="feed_forward",
    )(scalars, steps, *far(oT, n1, grads), g_swap, *far(w_out, w_in, w_back, w_down, w_up), gain, bias)


def feed_back_kernel(chunk, g3, slope, gai, n2, r2, w_in, w_back, w_down, w_out, gain_ref, sums3_ref,
                     g2_out, aT_out, sums_ref,
                     g2_v, slope_v, gai_v, n2_v, r2_v, out_w, in_w, back_w, down_w, low_v, aT_v,
                     sems, in_sems, back_sems, slope_sems, out_sems):
    rows, width = g2_v.shape
    chunks = in_w.shape[0]
    block = rows // 2

    def in_copy(c):
        return pltpu.make_async_copy(
            w_in.at[:, pl.ds(pl.multiple_of(c * chunk, chunk), chunk)], in_w.at[c], in_sems.at[c])

    def back_copy(c):
        return pltpu.make_async_copy(
            w_back.at[pl.ds(pl.multiple_of(c * chunk, chunk), chunk)], back_w.at[c], back_sems.at[c])

    def slope_copy(c):
        cols = pl.ds(pl.multiple_of(c * chunk, chunk), chunk)
        return pltpu.make_async_copy(slope.at[:, cols], slope_v.at[c], slope_sems.at[c])

    copies = start_copies([(g3, g2_v), (w_down, down_w), (gai, gai_v)], sems)
    for c in range(chunks):
        back_copy(c).start()
        slope_copy(c).start()
        in_copy(c).start()
    copies += [send(n2, n2_v, sems.at[3]), send(r2, r2_v, sems.at[4]), send(w_out, out_w, sems.at[5])]
    copies[0].wait()
    low_v[...] = g2_v[...].astype(bf16)
    wait_all(copies[1:3])
    g2_v[...] += dg(gai_v[...], down_w[...], NT)

    def step(c, carry):
        back_copy(c).wait()
        weight = back_w[c]
        parts = [dg(low_v[pl.ds(b * block, block)], weight, NT) for b in range(2)]
        in_copy(c).wait()
        slope_copy(c).wait()
        weight = in_w[c]
        for b in range(2):
            here = pl.ds(b * block, block)
            inner = (parts[b] * slope_v[c, here].astype(f32)).astype(bf16)
            g2_v[here] += dg(inner, weight, NT)
        return carry

    lax.fori_loop(0, chunks, step, 0)
    gain2 = gain_ref[1:2]
    wait_all(copies[3:])

    def second(at, carry):
        sl = at(0)
        G = g2_v[sl]
        n = n2_v[sl]
        grad = norm_back(G, n, r2_v[sl][:, 0:1], gain2)
        g2_v[sl] = grad
        low_v[sl] = grad.astype(bf16)
        return carry[0] + fold(G * n), carry[1] + fold(G)

    sums = for_rows(rows, second, zero_sums(2, width))
    sent = [send(g2_v, g2_out, out_sems.at[0])]
    store_sums(sums_ref, sums)
    sums_ref[2:4] = sums3_ref[...]
    aT_v[...] = dg(out_w[...], low_v[...], NT).astype(bf16)
    sent.append(send(aT_v, aT_out, out_sems.at[1]))
    wait_all(sent)


def feed_back(g3, slope, gai, n2, r2, w_in, w_back, w_down, w_out, gain, sums3):
    rows, width = g3.shape
    units = w_in.shape[1]
    adapter = w_down.shape[1]
    chunk = 1024
    chunks = units // chunk
    return pl.pallas_call(
        functools.partial(feed_back_kernel, chunk),
        in_specs=[HBM] * 9 + [VMEM] * 2,
        out_specs=[HBM] * 2 + [VMEM],
        out_shape=[shape((rows, width), f32), shape((width, rows), bf16), shape((4, width), f32)],
        scratch_shapes=[
            pltpu.VMEM((rows, width), f32), pltpu.VMEM((chunks, rows, chunk), bf16),
            pltpu.VMEM((rows, adapter), bf16), pltpu.VMEM((rows, width), f32), pltpu.VMEM((rows, PAIR), f32),
            pltpu.VMEM((width, width), bf16), pltpu.VMEM((chunks, width, chunk), bf16),
            pltpu.VMEM((chunks, chunk, width), bf16), pltpu.VMEM((width, adapter), bf16),
            pltpu.VMEM((rows, width), bf16), pltpu.VMEM((width, rows), bf16),
            dma(6), dma(chunks), dma(chunks), dma(chunks), dma(2),
        ],
        compiler_params=params(38),
        cost_estimate=cost(4 * rows * width * units + 2 * rows * width * adapter + 2 * rows * width * width,
                           4 * width * units),
        name="feed_back",
    )(*far(g3, slope, gai, n2, r2, w_in, w_back, w_down, w_out), gain, sums3)


def first_back_kernel(g2, dq, n1, r1, w_query, w_out, gain_ref, sums2_ref, g1_out, aT_out, sums_ref,
                      g1_v, dq_v, n_v, r_v, held, low_v, aT_v, sems, out_sems):
    copies = start_copies([(dq, dq_v), (w_query, held.at[0]), (g2, g1_v), (n1, n_v), (r1, r_v),
                           (w_out, held.at[1])], sems)
    rows, width = g1_v.shape
    wait_all(copies[:3])
    g1_v[...] += dg(dq_v[...], held[0], NT)
    gain = gain_ref[0:1]
    wait_all(copies[3:5])

    def body(at, carry):
        sl = at(0)
        G = g1_v[sl]
        n = n_v[sl]
        grad = norm_back(G, n, r_v[sl][:, 0:1], gain)
        g1_v[sl] = grad
        low_v[sl] = grad.astype(bf16)
        return carry[0] + fold(G * n), carry[1] + fold(G)

    sums = for_rows(rows, body, zero_sums(2, width))
    sent = [send(g1_v, g1_out, out_sems.at[0])]
    store_sums(sums_ref, sums)
    sums_ref[2:6] = sums2_ref[...]
    copies[5].wait()
    aT_v[...] = dg(held[1], low_v[...], NT).astype(bf16)
    sent.append(send(aT_v, aT_out, out_sems.at[1]))
    wait_all(sent)


def first_back(g2, dq, n1, r1, w_query, w_out, gain, sums2):
    rows, width = g2.shape
    return pl.pallas_call(
        first_back_kernel,
        in_specs=[HBM] * 6 + [VMEM] * 2,
        out_specs=[HBM] * 2 + [VMEM],
        out_shape=[shape((rows, width), f32), shape((width, rows), bf16), shape((6, width), f32)],
        scratch_shapes=[pltpu.VMEM((rows, width), f32), pltpu.VMEM((rows, width), bf16),
                        pltpu.VMEM((rows, width), f32), pltpu.VMEM((rows, PAIR), f32),
                        pltpu.VMEM((2, width, width), bf16), pltpu.VMEM((rows, width), bf16),
                        pltpu.VMEM((width, rows), bf16), dma(6), dma(2)],
        compiler_params=params(18),
        cost_estimate=cost(4 * rows * width * width, 4 * width * width + 10 * rows * width),
        name="first_back",
    )(g2, dq, *far(n1, r1), w_query, w_out, gain, sums2)


def summed(first, others):
    total = first.astype(f32)
    for ref in others:
        total = total + ref.astype(f32)
    return total.astype(bf16)


def key_grads_kernel(count, based, sc_ref, *refs):
    parts, refs = refs[:count], refs[count:]
    if based:
        base, refs = refs[0], refs[1:]
    w_key, w_value, own_out, swap_out, part_v, held, out_v = refs[:7]
    sems, out_sems = refs[-2:]
    block = out_v.shape[1]
    order = [(w_key, held.at[0])] + [(ref, part_v.at[n]) for n, ref in enumerate(parts)]
    order.append((w_value, held.at[1]))
    if based:
        order.append((base, refs[7]))
    copies = start_copies(order, sems)
    wait_all(copies[:1 + count])
    total = None
    for n in range(2):
        if n == 1:
            copies[1 + count].wait()
        value = jnp.concatenate(
            [summed(part_v[b, n], [part_v[r, n] for r in range(2 + b, count, 2)]) for b in range(2)], 0)
        total = add(total, dg(value, held[n], NT))
    if based:
        copies[-1].wait()
        total = total + refs[7][...]
    sent = []
    for b, target in ((1, swap_out), (0, own_out.at[sc_ref[SIDE]])):
        out_v[b] = total[b * block:(b + 1) * block].astype(bf16)
        sent.append(send(out_v.at[b], target, out_sems.at[b]))
    wait_all(sent)


def key_grads(scalars, parts, w_key, w_value, base=None):
    _, block, width = parts[0].shape
    count = len(parts)
    based = base is not None
    extra = [base] if based else []
    return pl.pallas_call(
        functools.partial(key_grads_kernel, count, based),
        in_specs=[SMEM] + [HBM] * (count + 2 + len(extra)),
        out_specs=[HBM] * 2,
        out_shape=[far_shape((2, block, width), bf16), shape((block, width), bf16)],
        scratch_shapes=[pltpu.VMEM((count, 2, block, width), bf16), pltpu.VMEM((2, width, width), bf16),
                        pltpu.VMEM((2, block, width), bf16)]
        + [pltpu.VMEM((2 * block, width), f32)] * len(extra) + [dma(2 + count + len(extra)), dma(2)],
        compiler_params=params(20),
        cost_estimate=cost(8 * block * width * width, 4 * width * width),
        name="token_grad" if based else "enc_grad",
    )(scalars, *parts, *extra, w_key, w_value)


def query_grad_kernel(g1, dq, w_query, out, g1_v, dq_v, held, sems, out_sems):
    copies = start_copies([(dq, dq_v), (w_query, held), (g1, g1_v)], sems)
    wait_all(copies)
    g1_v[...] += dg(dq_v[...], held[...], NT)
    send(g1_v, out, out_sems.at[0]).wait()


def query_grad(g1, dq, w_query):
    rows, width = g1.shape
    return pl.pallas_call(
        query_grad_kernel,
        in_specs=[HBM] * 3,
        out_specs=HBM,
        out_shape=shape((rows, width), f32),
        scratch_shapes=[pltpu.VMEM((rows, width), f32), pltpu.VMEM((rows, width), bf16),
                        pltpu.VMEM((width, width), bf16), dma(3), dma(1)],
        compiler_params=params(14),
        cost_estimate=cost(2 * rows * width * width, 2 * width * width + 10 * rows * width),
        name="query_grad",
    )(g1, dq, w_query)


def assemble_kernel(places, sc_ref, *refs):
    count = len(places)
    pieces = refs[:count]
    sums_a, sums_b, up_ref, down_ref, gains_ref, biases_ref = refs[count:]
    part = up_ref.shape[0] // 2
    core, rank = sc_ref[CORE], sc_ref[HALF]
    for (position, first), piece in zip(places, pieces):
        block = (position // 2) ^ core
        size = piece.shape[0]
        at = pl.ds(pl.multiple_of(((position % 2) ^ rank) * part + first, size), size)

        @pl.when(block == 0)
        def _():
            up_ref[at] = piece[...].astype(f32)

        @pl.when(block == 1)
        def _():
            down_ref[:, at] = piece[...].T.astype(f32)
    total = sums_a[...] + sums_b[...]
    for n in range(3):
        gains_ref[n:n + 1] = total[2 * n:2 * n + 1]
        biases_ref[n:n + 1] = total[2 * n + 1:2 * n + 2]


def assemble(scalars, places, pieces, sums_a, sums_b):
    part, width = pieces[0].shape
    return pl.pallas_call(
        functools.partial(assemble_kernel, places),
        in_specs=[SMEM] + [VMEM] * (len(pieces) + 2),
        out_specs=[VMEM] * 4,
        out_shape=[shape((2 * part, width), f32), shape((width, 2 * part), f32), shape((3, width), f32),
                   shape((3, width), f32)],
        compiler_params=params(14),
        cost_estimate=cost(0, 24 * part * width),
        name="assemble",
    )(scalars, *pieces, sums_a, sums_b)


def exchange(x, step):
    axis, bit = step
    return lax.ppermute(x, axis, [(i, i ^ bit) for i in range(lax.axis_size(axis))])


def after(x, *others):
    return lax.optimization_barrier((x,) + others)[0]


def plus(x, *others):
    total = x.astype(f32)
    for y in others:
        total = total + y.astype(f32)
    return total.astype(x.dtype)


def bits(size):
    return [1 << n for n in range(size.bit_length() - 1)]


def position_table(group, block, far_bit, ranks):
    half = group // 2
    table = []
    for rank in range(ranks):
        for member in range(group):
            side = member // half
            low = group - 1 - member if side else member

            def starts(index):
                own = group - 1 - index if side else index
                return [own * block, (group - 1 - own) * block]

            row = [side, member & 1, int(rank & far_bit != 0), low * block, (group - 1 - low) * block]
            row += starts(low)
            tail = []
            for r in range(1, half):
                index = (low + r) % half
                wrap = low + r >= half
                row += starts(index)
                first, second = index * block, (group - 1 - index) * block
                tail += [int(wrap), first, first if wrap else second]
            table.append(row + tail)
    return jnp.asarray(table, jnp.int32)


def per_device(
    tokens, enc_states, dec_lengths, enc_lengths, adapter_step, out_grad,
    self_query, self_key, self_value, self_out, cross_query, cross_key, cross_value, cross_out,
    ffn_in, ffn_out, adapter_down, adapter_up, ln_gain, ln_bias,
):
    group, ranks = lax.axis_size("seq"), lax.axis_size("dp")
    half = group // 2
    member = lax.axis_index("seq")
    side = member // half
    block = tokens.shape[1]
    swap = [(i, group - 1 - i) for i in range(group)]
    seq_bits, dp_bits = bits(group), bits(ranks)
    core_step, far_step, side_step = ("seq", 1), ("dp", dp_bits[1]), ("dp", 1)
    full_steps = [("dp", b) for b in dp_bits[2:]] + [("seq", b) for b in seq_bits[1:]] + [side_step]
    scalars = lax.dynamic_index_in_dim(
        position_table(group, block, far_step[1], ranks), lax.axis_index("dp") * group + member, 0, keepdims=False)

    def place(s, index):
        return group - 1 - index if s == 1 else index

    def from_shift(r):
        return [(place(s, (i + r) % half), place(s, i)) for s in range(2) for i in range(half)]

    def to_shift(r):
        return [(place(s, i), place(s, (i + r) % half)) for s in range(2) for i in range(half)]

    def theirs(x):
        return lax.dynamic_index_in_dim(x, 1 - side, 0, keepdims=False)

    def swapped(x):
        return lax.ppermute(x, "seq", swap)

    def joined(out, back):
        return lax.dynamic_update_index_in_dim(out, back, 1 - side, 0)

    def gathered(own, other):
        every = [own, other]
        for r in range(1, half):
            every += [lax.ppermute(own, "seq", from_shift(r)), lax.ppermute(other, "seq", from_shift(r))]
        return every

    def returned(parts):
        every = list(parts[:2])
        for r in range(1, half):
            every += [lax.ppermute(parts[2 * r], "seq", to_shift(r)),
                      lax.ppermute(parts[2 * r + 1], "seq", to_shift(r))]
        return every

    x_swap = swapped(theirs(tokens))
    q_own, kv_own, ckv_own = project(
        scalars, [tokens, enc_states], [self_key, self_value, self_query, cross_key, cross_value],
        ((0, 1, 0), (0, 1, 1), (0, 0, None), (1, 2, 0), (1, 2, 1)), "project_own", pin=True)
    e_theirs, g_theirs = theirs(enc_states), theirs(out_grad)
    e_swap = swapped(after(e_theirs, x_swap))
    kv_swap, q_swap = project(
        scalars, [x_swap], [self_key, self_value, self_query], ((0, 0, 0), (0, 0, 1), (0, 1, None)),
        "project_swap")
    kvs = gathered(kv_own, kv_swap)
    oT, probs, inverse = self_forward(scalars, dec_lengths, q_own, q_swap, kvs)
    ckv_swap, = project(
        scalars, [after(e_swap, oT)], [cross_key, cross_value], ((0, 0, 0), (0, 0, 1)), "project_enc")
    g_swap = swapped(after(g_theirs, e_swap))
    ckvs = gathered(ckv_own, ckv_swap)
    n1, r1, cq = first_norm(scalars, after(oT, ckv_swap), tokens, x_swap, self_out, cross_query, ln_gain, ln_bias)
    coT, cprobs, cinverse = cross_forward(scalars, enc_lengths, cq, ckvs)
    out_own, out_swap, n2, r2, slope, g3, gai, *wgs, sums3 = feed_forward(
        scalars, adapter_step, coT, n1, out_grad, g_swap, cross_out, ffn_in, ffn_out, adapter_down, adapter_up,
        ln_gain, ln_bias)

    forwarded = plus(wgs[1], exchange(wgs[3], core_step))
    received = exchange(forwarded, far_step)
    kept = exchange(wgs[2], core_step)
    out_back = swapped(out_swap)
    g2, caT, sums2 = feed_back(after(g3, forwarded), slope, gai, n2, r2, ffn_in, ffn_out, adapter_down, cross_out,
                               ln_gain, sums3)
    wg = plus(wgs[0], kept, after(received, g2))
    layer_output = joined(out_own, after(out_back, g2))

    received = exchange(wg, full_steps[0])
    cdq, *cdkvs = cross_backward(cq, cprobs, after(caT, wg, layer_output), coT, cinverse, ckvs)
    enc_parts = returned(cdkvs)
    for step in full_steps[1:-1]:
        wg = plus(wg, after(received, cdq))
        received = exchange(wg, step)
    g1, aT, sums = first_back(after(g2, wg), cdq, n1, r1, cross_query, self_out, ln_gain, sums2)
    y_steps = [("seq", bit) for bit in seq_bits[1:]]
    received_sums = exchange(sums, y_steps[0])
    enc_own, enc_swap = key_grads(scalars, [after(enc_parts[0], aT)] + enc_parts[1:], cross_key, cross_value)
    wg = plus(wg, after(received, enc_swap))
    sums = plus(sums, after(received_sums, enc_swap))
    received = exchange(wg, side_step)
    received_sums = exchange(sums, side_step)
    enc_back = swapped(enc_swap)

    dq, *dkvs = self_backward(scalars, q_own, q_swap, probs, after(aT, wg, sums, enc_swap), oT, inverse, kvs)
    wg = plus(wg, after(received, dq))
    sums = plus(sums, after(received_sums, dq))
    enc_grad = joined(enc_own, after(enc_back, dq))
    parts = returned([after(x, wg, sums, enc_back) for x in dkvs])
    pieces = [wg, exchange(wg, far_step), exchange(wg, core_step)]
    received_sums = exchange(sums, core_step)
    for step in y_steps[1:]:
        sums = plus(sums, received_sums)
        received_sums = exchange(sums, step)
    base = query_grad(g1, after(dq, sums), self_query)
    sums = plus(sums, after(received_sums, base))
    received_sums = exchange(sums, far_step)
    t_own, t_swap = key_grads(scalars, parts, self_key, self_value, after(base, sums))
    t_back = swapped(t_swap)
    sums = plus(sums, after(received_sums, t_swap))
    last_steps = [("dp", b) for b in dp_bits[2:]]
    for step in last_steps[:-1]:
        sums = plus(sums, exchange(sums, step))
    last = after(pieces[1], t_swap)
    size = last.shape[0] // 2
    places = [(0, 0), (1, 0), (2, 0)] + [(3, n * size) for n in range(2)]
    pieces += [exchange(last[n * size:(n + 1) * size], core_step) for n in range(2)]
    up, down, gains, biases = assemble(scalars, places, pieces, sums, exchange(sums, last_steps[-1]))
    return layer_output, joined(t_own, after(t_back, up)), enc_grad, down, up, gains, biases


def solution(mesh):
    rows = P("dp", "seq", None)
    return jax.shard_map(
        per_device,
        mesh=mesh,
        in_specs=(rows, rows, P("dp"), P("dp"), P("dp"), rows) + (P(),) * 14,
        out_specs=(rows, rows, rows, P(), P(), P(), P()),
        check_vma=False,
    )
```

```python
import functools
import math

import jax
import jax.numpy as jnp
from jax import lax
from jax.experimental import pallas as pl
from jax.experimental.pallas import tpu as pltpu
from jax.sharding import PartitionSpec as P

HEAD_DIM = 64
PAIR = 2 * HEAD_DIM
EPS = 1e-05
NEGATIVE = -1e30
SCALE = HEAD_DIM ** (-0.5)
EXP2_SCALE = SCALE * math.log2(math.e)
HALF_LOG2E = 0.5 * math.log2(math.e)

f32 = jnp.float32
bf16 = jnp.bfloat16

NN = (((1,), (0,)), ((), ()))
NT = (((1,), (1,)), ((), ()))
TN = (((0,), (0,)), ((), ()))

HBM = pl.BlockSpec(memory_space=pltpu.HBM)
SMEM = pl.BlockSpec(memory_space=pltpu.SMEM)
VMEM = pl.BlockSpec(memory_space=pltpu.VMEM)
MIB = 2 ** 20

SIDE, CORE, HALF, NEXT, LOW, HIGH, STARTS = range(7)


def dg(left, right, dims):
    return lax.dot_general(left, right, dims, preferred_element_type=f32)


def add(total, term):
    return term if total is None else total + term


def params(limit_mib):
    return pltpu.CompilerParams(vmem_limit_bytes=limit_mib * MIB)


def cost(flops, nbytes, exps=0):
    return pl.CostEstimate(flops=int(flops), bytes_accessed=int(nbytes), transcendentals=int(exps))


def shape(dims, dtype):
    return jax.ShapeDtypeStruct(dims, dtype)


def far(*arrays):
    return [pltpu.with_memory_space_constraint(x, pltpu.HBM) for x in arrays]


def far_shape(dims, dtype):
    return pltpu.HBM(dims, dtype)


def start_copies(pairs, sems):
    copies = [pltpu.make_async_copy(src, dst, sems.at[n]) for n, (src, dst) in enumerate(pairs)]
    for copy in copies:
        copy.start()
    return copies


def project_kernel(plan, n_in, sc_ref, *refs):
    count = len(plan)
    xs = refs[:n_in]
    ws = refs[n_in:n_in + count]
    n_out = 1 + max(o for _, o, _ in plan)
    outs = refs[n_in + count:n_in + count + n_out]
    x_held, held, out_held, sems, out_sems = refs[n_in + count + n_out:]
    side = sc_ref[0]
    first = [(x.at[side] if len(x.shape) == 3 else x, x_held.at[i]) for i, x in enumerate(xs)]
    copies = start_copies(first + [(w, held.at[j]) for j, w in enumerate(ws)], sems)
    for i in range(n_in):
        copies[i].wait()
    sent = []
    for j, (i, o, row) in enumerate(plan):
        copies[n_in + j].wait()
        out_held[j] = dg(x_held[i], held[j], NN).astype(bf16)
        target = outs[o] if row is None else outs[o].at[row]
        sent.append(pltpu.make_async_copy(out_held.at[j], target, out_sems.at[j]))
        sent[-1].start()
    for copy in sent:
        copy.wait()


def project(scalars, xs, ws, plan, name, pin=False):
    rows, width = xs[0].shape[-2:]
    count = len(plan)
    n_out = 1 + max(o for _, o, _ in plan)
    out_shape = []
    for o in range(n_out):
        used = [row for _, oo, row in plan if oo == o]
        out_shape.append(shape((rows, width) if used[0] is None else (len(used), rows, width), bf16))
    return pl.pallas_call(
        functools.partial(project_kernel, plan, len(xs)),
        in_specs=[SMEM] + [HBM] * (len(xs) + count),
        out_specs=[HBM] * n_out,
        out_shape=out_shape,
        scratch_shapes=[pltpu.VMEM((len(xs), rows, width), bf16), pltpu.VMEM((count, width, width), bf16),
                        pltpu.VMEM((count, rows, width), bf16),
                        pltpu.SemaphoreType.DMA((len(xs) + count,)), pltpu.SemaphoreType.DMA((count,))],
        compiler_params=params(28),
        cost_estimate=cost(2 * count * rows * width * width, 2 * count * width * width),
        name=name,
    )(scalars, *(far(*xs, *ws) if pin else (*xs, *ws)))


def pair_masks():
    lane = lax.broadcasted_iota(jnp.int32, (1, PAIR), 1)
    return lane, lane < HEAD_DIM


def key_bias(start, length, rows):
    pos = start + lax.broadcasted_iota(jnp.int32, (rows, PAIR), 0)
    lane = lax.broadcasted_iota(jnp.int32, (rows, PAIR), 1)
    masked = jnp.where(pos < length, 0.0, NEGATIVE)
    return (
        jnp.where(lane == HEAD_DIM, masked, 0.0).astype(bf16),
        jnp.where(lane == 0, masked, 0.0).astype(bf16),
    )


def queries_with_one(q, half):
    one = jnp.ones((), bf16)
    return jnp.where(half, q, one), jnp.where(half, one, q)


def head_only(x, half):
    zero = jnp.zeros((), bf16)
    return jnp.where(half, x, zero), jnp.where(half, zero, x)


def soft(scores, highest):
    if highest is None:
        return jnp.exp2(scores * EXP2_SCALE).astype(bf16)
    return jnp.exp2((scores - highest) * EXP2_SCALE).astype(bf16)


EXPONENTS = 80.0


def scores_are_small(queries, keys):
    width = queries[0].shape[1]
    row = lax.broadcasted_iota(jnp.int32, (16, width), 0)
    lane = lax.broadcasted_iota(jnp.int32, (16, width), 1)
    pick = jnp.where(row == lane // HEAD_DIM, 1.0, 0.0).astype(bf16)

    def largest(blocks):
        total = None
        for x in blocks:
            norms = dg(pick, x * x, NT)
            total = norms if total is None else jnp.maximum(total, norms)
        return total.max(1, keepdims=True)

    limit = EXPONENTS / EXP2_SCALE / 1.02
    return jnp.max(largest(queries) * largest(keys)) <= limit * limit


def heads_with_ones(vT):
    ones = jnp.ones((16, vT.shape[1]), bf16)
    return [jnp.concatenate([vT[h * HEAD_DIM:(h + 1) * HEAD_DIM], ones], 0) for h in range(2)]


def probs_out(p_v, p_out, sems):
    step, last = pl.program_id(0), pl.num_programs(0) - 1
    count = p_v.shape[1]

    def copy(n, at):
        return pltpu.make_async_copy(p_v.at[at % 2, n], p_out.at[at * count + n], sems.at[at % 2, n])

    def before():
        @pl.when(step >= 2)
        def _():
            for n in range(count):
                copy(n, step - 2).wait()

    def end():
        @pl.when(step == last)
        def _():
            for n in range(count):
                copy(n, step - 1).wait()
            for n in range(count):
                copy(n, step).wait()

    return before, lambda n: copy(n, step).start(), end


def top(chunks):
    highest = chunks[0].max(0, keepdims=True)
    for s in chunks[1:]:
        highest = jnp.maximum(highest, s.max(0, keepdims=True))
    return highest


def grad_columns(aT, oT, inverse, half):
    rows = aT.shape[1]
    sub = lax.broadcasted_iota(jnp.int32, (HEAD_DIM, rows), 0)
    full, plain = [], []
    for h in range(2):
        sl = slice(h * HEAD_DIM, (h + 1) * HEAD_DIM)
        a = aT[sl].astype(f32) * inverse[h:h + 1]
        d = -(a * oT[sl].astype(f32)).sum(0, keepdims=True)
        high = d.astype(bf16).astype(f32)
        extra = jnp.where(sub == 0, high, jnp.where(sub == 1, d - high, 0.0)).astype(bf16)
        a = a.astype(bf16)
        full.append(jnp.concatenate([a, extra] if h == 0 else [extra, a], 0))
        plain.append(a)
    return full, head_only(jnp.concatenate(plain, 0).T, half)


def values_with_ones(v, lane, half):
    first = jnp.where((lane == HEAD_DIM) | (lane == HEAD_DIM + 1), 1.0, 0.0).astype(bf16)
    second = jnp.where(lane < 2, 1.0, 0.0).astype(bf16)
    return jnp.where(half, v, first), jnp.where(half, second, v)


def cross_forward_kernel(n, per, sc_ref, len_ref, q_ref, *refs):
    kvs = refs[:n]
    oT_ref, p_out, inv_ref, bias_ref, p_v, p_sems = refs[n:]
    p_before, p_send, p_end = probs_out(p_v, p_out, p_sems)
    p_ref = p_v.at[pl.program_id(0) % 2]
    rows = q_ref.shape[0]
    block = kvs[0].shape[1]
    lane, half = pair_masks()

    @pl.when(pl.program_id(0) == 0)
    def _():
        length = len_ref[sc_ref[SIDE]]
        for j in range(n):
            bias_ref[0, j], bias_ref[1, j] = key_bias(sc_ref[STARTS + j], length, block)

    def prepare(u):
        lanes = slice(u * PAIR, (u + 1) * PAIR)
        keys, values = [[], []], [[], []]
        for j in range(n):
            k = kvs[j][0, :, lanes]
            keys[0].append(jnp.where(half, k, bias_ref[0, j]))
            keys[1].append(jnp.where(half, bias_ref[1, j], k))
            for h, v in enumerate(heads_with_ones(kvs[j][1, :, lanes].T)):
                values[h].append(v)
        return keys, values, queries_with_one(q_ref[:, lanes], half)

    items = [(u, h, b) for u in range(per) for h in range(2) for b in range(rows // block)]

    def attend(small):
        ready = [prepare(u) for u in range(per)]

        def score(item):
            u, h, b = item
            q = ready[u][2][h][b * block:(b + 1) * block]
            return [dg(k, q, NT) for k in ready[u][0][h]]

        later = score(items[0])
        for step, (u, h, b) in enumerate(items):
            chunks = later
            if step + 1 < len(items):
                later = score(items[step + 1])
            highest = None if small else top(chunks)
            cols = pl.ds(b * block, block)
            out = None
            for j in range(n):
                p = soft(chunks[j], highest)
                p_ref[2 * u + h, pl.ds(j * block, block), cols] = p
                out = add(out, dg(ready[u][1][h][j], p, NN))
            inverse = 1.0 / out[HEAD_DIM:HEAD_DIM + 1]
            inv_ref[u, pl.ds(h, 1), cols] = inverse
            oT_ref[pl.ds((2 * u + h) * HEAD_DIM, HEAD_DIM), cols] = (out[:HEAD_DIM] * inverse).astype(bf16)
            if (b + 1) * block == rows:
                p_send(2 * u + h)

    p_before()
    small = scores_are_small([q_ref[:block], q_ref[block:]], [kv[0] for kv in kvs])
    pl.when(small)(lambda: attend(True))
    pl.when(jnp.logical_not(small))(lambda: attend(False))
    p_end()


def feature_rows(rows, per=1):
    return pl.BlockSpec((per * PAIR, rows), lambda i: (i, 0))


def feature_cols(rows, per=1):
    return pl.BlockSpec((rows, per * PAIR), lambda i: (0, i))


def kv_cols(rows, per=1):
    return pl.BlockSpec((2, rows, per * PAIR), lambda i: (0, 0, i))


def pair_block(*dims):
    return pl.BlockSpec(dims, lambda i: (i,) + (0,) * (len(dims) - 1))


CROSS_FORWARD_PAIRS, CROSS_BACKWARD_PAIRS, SELF_FORWARD_PAIRS, SELF_BACKWARD_PAIRS = 4, 2, 4, 2


def cross_forward(scalars, lengths, q, kvs):
    n = len(kvs)
    rows, width = q.shape
    block = kvs[0].shape[1]
    pairs = width // PAIR
    every = n * block
    per = CROSS_FORWARD_PAIRS
    return pl.pallas_call(
        functools.partial(cross_forward_kernel, n, per),
        grid=(pairs // per,),
        in_specs=[SMEM, SMEM, feature_cols(rows, per)] + [kv_cols(block, per)] * n,
        out_specs=[feature_rows(rows, per), HBM, pair_block(per, 2, rows)],
        out_shape=[
            far_shape((width, rows), bf16),
            far_shape((2 * pairs, every, rows), bf16),
            far_shape((pairs, 2, rows), f32),
        ],
        scratch_shapes=[pltpu.VMEM((2, n, block, PAIR), bf16), pltpu.VMEM((2, 2 * per, every, rows), bf16),
                        pltpu.SemaphoreType.DMA((2, 2 * per))],
        compiler_params=params(36),
        cost_estimate=cost(16 * rows * every * width, 4 * pairs * every * rows, 2 * pairs * every * rows),
        name="cross_forward",
    )(scalars, lengths, q, *kvs)


def cross_backward_kernel(n, per, q_ref, p_ref, aT_ref, oT_ref, inv_ref, *refs):
    kvs = refs[:n]
    dq_ref = refs[n]
    dkvs = refs[n + 1:]
    rows = q_ref.shape[0]
    block = kvs[0].shape[1]
    lane, half = pair_masks()

    def prepare(u):
        lanes = slice(u * PAIR, (u + 1) * PAIR)
        values, keysT = [[], []], []
        for j in range(n):
            first, second = values_with_ones(kvs[j][1, :, lanes], lane, half)
            values[0].append(first)
            values[1].append(second)
            keysT.append(kvs[j][0, :, lanes].T)
        full, plain = grad_columns(aT_ref[lanes], oT_ref[lanes], inv_ref[u], half)
        return values, keysT, head_only(q_ref[:, lanes], half), full, plain

    ready = [prepare(u) for u in range(per)]
    items = [(u, b, h) for u in range(per) for b in range(rows // block) for h in range(2)]

    def grad_probs(item):
        u, b, h = item
        a = ready[u][3][h][:, b * block:(b + 1) * block]
        return [dg(v, a, NN) for v in ready[u][0][h]]

    later = grad_probs(items[0])
    for step, (u, b, h) in enumerate(items):
        values, keysT, queries, full, plain = ready[u]
        dps = later
        if step + 1 < len(items):
            later = grad_probs(items[step + 1])
        if (b, h) == (0, 0):
            dk, dv, halves = [None] * n, [None] * n, []
        dq = None
        sl = slice(b * block, (b + 1) * block)
        for j in range(n):
            p = p_ref[2 * u + h, pl.ds(j * block, block), pl.ds(b * block, block)]
            ds = (p * dps[j]).astype(bf16)
            dv[j] = add(dv[j], dg(p, plain[h][sl], NN))
            dk[j] = add(dk[j], dg(ds, queries[h][sl], NN))
            dq = add(dq, dg(keysT[j][h * HEAD_DIM:(h + 1) * HEAD_DIM], ds, NN))
        halves.append((dq * SCALE).astype(bf16))
        lanes = slice(u * PAIR, (u + 1) * PAIR)
        if h == 1:
            dq_ref[sl, lanes] = jnp.concatenate(halves[-2:], 0).T
        if sl.stop == rows and h == 1:
            for j in range(n):
                dkvs[j][0, :, lanes] = (dk[j] * SCALE).astype(bf16)
                dkvs[j][1, :, lanes] = dv[j].astype(bf16)


def cross_backward(q, probs, aT, oT, inverse, kvs):
    n = len(kvs)
    rows, width = q.shape
    block = kvs[0].shape[1]
    pairs = width // PAIR
    every = n * block
    per = CROSS_BACKWARD_PAIRS
    return pl.pallas_call(
        functools.partial(cross_backward_kernel, n, per),
        grid=(pairs // per,),
        in_specs=[feature_cols(rows, per), pair_block(2 * per, every, rows), feature_rows(rows, per),
                  feature_rows(rows, per), pair_block(per, 2, rows)] + [kv_cols(block, per)] * n,
        out_specs=[feature_cols(rows, per)] + [kv_cols(block, per)] * n,
        out_shape=[shape((rows, width), bf16)] + [shape((2, block, width), bf16)] * n,
        compiler_params=params(24),
        cost_estimate=cost(32 * rows * every * width, 4 * pairs * every * rows),
        name="cross_backward",
    )(*far(q, probs), aT, *far(oT, inverse, *kvs))


def self_forward_kernel(others, per, sc_ref, len_ref, q_own, q_swap, *refs):
    kvs = refs[:2 + 2 * others]
    oT_ref, p_out, inv_ref, tri_ref, p_v, p_sems = refs[2 + 2 * others:]
    p_before, p_send, p_end = probs_out(p_v, p_out, p_sems)
    p_ref = p_v.at[pl.program_id(0) % 2]
    block = q_own.shape[0]
    lane, half = pair_masks()
    swapped = sc_ref[SIDE] == 1
    length = len_ref[sc_ref[SIDE]]
    first_wrap = STARTS + 2 + 2 * others
    wraps = [sc_ref[first_wrap + 3 * r] == 1 for r in range(others)]
    key_starts = [sc_ref[LOW], sc_ref[HIGH]]
    for r in range(others):
        key_starts += [sc_ref[first_wrap + 3 * r + 1], sc_ref[first_wrap + 3 * r + 2]]

    @pl.when(pl.program_id(0) == 0)
    def _():
        key = lax.broadcasted_iota(jnp.int32, (block, block), 0)
        query = lax.broadcasted_iota(jnp.int32, (block, block), 1)
        tri_ref[...] = jnp.where(key <= query, 0.0, NEGATIVE)

    biases = [key_bias(start, length, block) for start in key_starts]

    def low_high(first, second):
        return jnp.where(swapped, second, first), jnp.where(swapped, first, second)

    def prepare(u):
        lanes = slice(u * PAIR, (u + 1) * PAIR)
        q_low, q_high = low_high(q_own[:, lanes], q_swap[:, lanes])
        ks = list(low_high(kvs[0][0, :, lanes], kvs[1][0, :, lanes]))
        vs = list(low_high(kvs[0][1, :, lanes], kvs[1][1, :, lanes]))
        for r in range(others):
            first, second = low_high(kvs[2 + 2 * r][0, :, lanes], kvs[3 + 2 * r][0, :, lanes])
            ks += [first, jnp.where(wraps[r], first, second)]
            first, second = low_high(kvs[2 + 2 * r][1, :, lanes], kvs[3 + 2 * r][1, :, lanes])
            vs += [first, jnp.where(wraps[r], first, second)]
        keys = [(jnp.where(half, k, bias[0]), jnp.where(half, bias[1], k)) for k, bias in zip(ks, biases)]
        values = [heads_with_ones(v.T) for v in vs]
        ones = [queries_with_one(q_low, half), queries_with_one(q_high, half)]
        either = [tuple(jnp.where(w, ones[0][h], ones[1][h]) for h in range(2)) for w in wraps]
        return keys, values, ones, either

    def attend(small):
        ready = [prepare(u) for u in range(per)]
        tri = tri_ref[...]
        items = [(u, h) for u in range(per) for h in range(2)]

        def score(item):
            u, h = item
            keys, _, ones, either = ready[u]
            low = dg(keys[0][h], ones[0][h], NT) + tri
            high = [dg(keys[0][h], ones[1][h], NT), dg(keys[1][h], ones[1][h], NT) + tri]
            free = []
            for r in range(others):
                high.append(dg(keys[2 + 2 * r][h], ones[1][h], NT))
                free.append(dg(keys[3 + 2 * r][h], either[r][h], NT))
            return low, high, free

        later = score(items[0])
        for step, (u, h) in enumerate(items):
            values = ready[u][1]
            low, high, free = later
            if step + 1 < len(items):
                later = score(items[step + 1])
            top_low, top_high = None, None
            if not small:
                top_low = low.max(0, keepdims=True)
                top_high = top(high)
                for r in range(others):
                    peak = free[r].max(0, keepdims=True)
                    top_low = jnp.where(wraps[r], jnp.maximum(top_low, peak), top_low)
                    top_high = jnp.where(wraps[r], top_high, jnp.maximum(top_high, peak))

            def weigh(tile, scores, highest, v):
                p = soft(scores, highest)
                p_ref[2 * u + h, tile] = p
                return dg(v[h], p, NN)

            out_low = weigh(0, low, top_low, values[0])
            out_high = weigh(1, high[0], top_high, values[0]) + weigh(2, high[1], top_high, values[1])
            for r in range(others):
                out_high = out_high + weigh(3 + 2 * r, high[2 + r], top_high, values[2 + 2 * r])
                highest = None if small else jnp.where(wraps[r], top_low, top_high)
                out = weigh(4 + 2 * r, free[r], highest, values[3 + 2 * r])
                out_low = jnp.where(wraps[r], out_low + out, out_low)
                out_high = jnp.where(wraps[r], out_high, out_high + out)
            results = []
            for n, out in enumerate((out_low, out_high)):
                inverse = 1.0 / out[HEAD_DIM:HEAD_DIM + 1]
                inv_ref[u, n, pl.ds(h, 1), :] = inverse
                results.append((out[:HEAD_DIM] * inverse).astype(bf16))
            for n, out in enumerate(low_high(*results)):
                oT_ref[pl.ds((2 * u + h) * HEAD_DIM, HEAD_DIM), pl.ds(n * block, block)] = out
            p_send(2 * u + h)

    p_before()
    small = scores_are_small([q_own[...], q_swap[...]], [kv[0] for kv in kvs])
    pl.when(small)(lambda: attend(True))
    pl.when(jnp.logical_not(small))(lambda: attend(False))
    p_end()


def self_forward(scalars, lengths, q_own, q_swap, kvs):
    others = len(kvs) // 2 - 1
    block, width = q_own.shape
    pairs = width // PAIR
    tiles = 3 + 2 * others
    per = SELF_FORWARD_PAIRS
    return pl.pallas_call(
        functools.partial(self_forward_kernel, others, per),
        grid=(pairs // per,),
        in_specs=[SMEM, SMEM] + [feature_cols(block, per)] * 2 + [kv_cols(block, per)] * len(kvs),
        out_specs=[feature_rows(2 * block, per), HBM, pair_block(per, 2, 2, block)],
        out_shape=[
            shape((width, 2 * block), bf16),
            far_shape((2 * pairs, tiles, block, block), bf16),
            far_shape((pairs, 2, 2, block), f32),
        ],
        scratch_shapes=[pltpu.VMEM((block, block), f32), pltpu.VMEM((2, 2 * per, tiles, block, block), bf16),
                        pltpu.SemaphoreType.DMA((2, 2 * per))],
        compiler_params=params(26),
        cost_estimate=cost(16 * tiles * block * block * width, 4 * pairs * tiles * block * block,
                           2 * pairs * tiles * block * block),
        name="self_forward",
    )(scalars, lengths, q_own, q_swap, *kvs)


def self_backward_kernel(others, per, sc_ref, q_own, q_swap, p_ref, aT_ref, oT_ref, inv_ref, *refs):
    kvs = refs[:2 + 2 * others]
    dq_ref = refs[2 + 2 * others]
    dkvs = refs[3 + 2 * others:]
    block = q_own.shape[0]
    lane, half = pair_masks()
    swapped = sc_ref[SIDE] == 1
    first_wrap = STARTS + 2 + 2 * others
    wraps = [sc_ref[first_wrap + 3 * r] == 1 for r in range(others)]

    def low_high(first, second):
        return jnp.where(swapped, second, first), jnp.where(swapped, first, second)

    def prepare(u):
        lanes = slice(u * PAIR, (u + 1) * PAIR)
        ks = list(low_high(kvs[0][0, :, lanes], kvs[1][0, :, lanes]))
        vs = list(low_high(kvs[0][1, :, lanes], kvs[1][1, :, lanes]))
        for r in range(others):
            first, second = low_high(kvs[2 + 2 * r][0, :, lanes], kvs[3 + 2 * r][0, :, lanes])
            ks += [first, jnp.where(wraps[r], first, second)]
            first, second = low_high(kvs[2 + 2 * r][1, :, lanes], kvs[3 + 2 * r][1, :, lanes])
            vs += [first, jnp.where(wraps[r], first, second)]
        keysT = [k.T for k in ks]
        values = [values_with_ones(v, lane, half) for v in vs]
        sides = []
        a_blocks = low_high(aT_ref[lanes, 0:block], aT_ref[lanes, block:2 * block])
        o_blocks = low_high(oT_ref[lanes, 0:block], oT_ref[lanes, block:2 * block])
        q_blocks = low_high(q_own[:, lanes], q_swap[:, lanes])
        for n in range(2):
            full, plain = grad_columns(a_blocks[n], o_blocks[n], inv_ref[u, n], half)
            sides.append((full, plain, head_only(q_blocks[n], half)))
        for w in wraps:
            sides.append(tuple([jnp.where(w, x, y) for x, y in zip(first, second)]
                               for first, second in zip(sides[0], sides[1])))
        return keysT, values, sides

    ready = [prepare(u) for u in range(per)]
    tiles = [(0, 0, 0), (1, 0, 1), (2, 1, 1)]
    for r in range(others):
        tiles += [(3 + 2 * r, 2 + 2 * r, 1), (4 + 2 * r, 3 + 2 * r, 2 + r)]
    items = [(u, h) for u in range(per) for h in range(2)]

    def grad_probs(item):
        u, h = item
        _, values, sides = ready[u]
        return [dg(values[key][h], sides[side][0][h], NN) for _, key, side in tiles]

    later = grad_probs(items[0])
    for step, (u, h) in enumerate(items):
        keysT, _, sides = ready[u]
        dps = later
        if step + 1 < len(items):
            later = grad_probs(items[step + 1])
        if h == 0:
            dk, dv, both = [None] * len(keysT), [None] * len(keysT), []
        dq = [None] * len(sides)
        for (index, key, side), dp in zip(tiles, dps):
            p = p_ref[2 * u + h, index]
            ds = (p * dp).astype(bf16)
            dv[key] = add(dv[key], dg(p, sides[side][1][h], NN))
            dk[key] = add(dk[key], dg(ds, sides[side][2][h], NN))
            dq[side] = add(dq[side], dg(keysT[key][h * HEAD_DIM:(h + 1) * HEAD_DIM], ds, NN))
        for wrap, term in zip(wraps, dq[2:]):
            dq[0] = jnp.where(wrap, dq[0] + term, dq[0])
            dq[1] = jnp.where(wrap, dq[1], dq[1] + term)
        both.append([(x * SCALE).astype(bf16) for x in low_high(dq[0], dq[1])])
        if h == 0:
            continue
        lanes = slice(u * PAIR, (u + 1) * PAIR)
        for n in range(2):
            dq_ref[pl.ds(n * block, block), lanes] = jnp.concatenate([both[0][n], both[1][n]], 0).T

        for row, terms, factor in ((0, dk, SCALE), (1, dv, 1.0)):
            pairs = [(terms[0], terms[1])]
            for r, wrap in enumerate(wraps):
                always, either = terms[2 + 2 * r], terms[3 + 2 * r]
                pairs.append((jnp.where(wrap, always + either, always), jnp.where(wrap, 0.0, either)))
            for n, pair in enumerate(pairs):
                first, second = low_high(*pair)
                dkvs[2 * n][row, :, lanes] = (first * factor).astype(bf16)
                dkvs[2 * n + 1][row, :, lanes] = (second * factor).astype(bf16)


def self_backward(scalars, q_own, q_swap, probs, aT, oT, inverse, kvs):
    others = len(kvs) // 2 - 1
    block, width = q_own.shape
    pairs = width // PAIR
    tiles = 3 + 2 * others
    per = SELF_BACKWARD_PAIRS
    return pl.pallas_call(
        functools.partial(self_backward_kernel, others, per),
        grid=(pairs // per,),
        in_specs=[SMEM] + [feature_cols(block, per)] * 2
        + [pair_block(2 * per, tiles, block, block), feature_rows(2 * block, per), feature_rows(2 * block, per),
           pair_block(per, 2, 2, block)] + [kv_cols(block, per)] * len(kvs),
        out_specs=[feature_cols(2 * block, per)] + [kv_cols(block, per)] * len(kvs),
        out_shape=[shape((2 * block, width), bf16)] + [shape((2, block, width), bf16)] * len(kvs),
        compiler_params=params(24),
        cost_estimate=cost(32 * tiles * block * block * width, 4 * pairs * tiles * block * block),
        name="self_backward",
    )(scalars, *far(q_own, q_swap, probs), aT, *far(oT, inverse, *kvs))


ROWS = 256


def normalized(z):
    center = z - jnp.mean(z, axis=-1, keepdims=True)
    spread = jnp.mean(center * center, axis=-1, keepdims=True)
    r = lax.rsqrt(spread + EPS)
    return center * r, r


def norm_back(G, n, r, gain):
    scaled = G * gain
    return r * (scaled - jnp.mean(scaled, -1, keepdims=True) - n * jnp.mean(scaled * n, -1, keepdims=True))


def spread_lanes(r):
    return jnp.broadcast_to(r, (r.shape[0], PAIR))


def for_rows(total, body, init=0):
    count = min(ROWS, total)

    def step(i, carry):
        return body(lambda base: pl.ds(pl.multiple_of(i * count + base, count), count), carry)

    return lax.fori_loop(0, total // count, step, init)


def fold(x):
    return x.reshape(x.shape[0] // 8, 8, x.shape[1]).sum(0)


def zero_sums(count, width):
    return tuple(jnp.zeros((8, width), f32) for _ in range(count))


def store_sums(ref, sums):
    for n, total in enumerate(sums):
        ref[n:n + 1] = total.sum(0, keepdims=True)


def wait_all(copies):
    for copy in copies:
        copy.wait()


def send(src, dst, sem):
    copy = pltpu.make_async_copy(src, dst, sem)
    copy.start()
    return copy


def dma(count):
    return pltpu.SemaphoreType.DMA((count,))


def first_norm_kernel(sc_ref, oT, tokens, x_swap, w_out, w_query, gain_ref, bias_ref, n_out, r_out, cq_out,
                      oT_v, x_v, held, n_v, r_v, low_v, cq_v, sems, out_sems):
    copies = start_copies([(oT, oT_v), (w_out, held.at[0]), (tokens.at[sc_ref[SIDE]], x_v.at[0]),
                           (x_swap, x_v.at[1]), (w_query, held.at[1])], sems)
    block = x_v.shape[1]
    wait_all(copies[:2])
    n_v[...] = dg(oT_v[...], held[0], TN)
    gain, bias = gain_ref[0:1], bias_ref[0:1]
    wait_all(copies[2:4])
    for half in range(2):
        def body(at, carry, half=half):
            here = at(half * block)
            n, r = normalized(n_v[here] + x_v[half, at(0)].astype(f32))
            n_v[here] = n
            r_v[here] = spread_lanes(r)
            low_v[here] = (n * gain + bias).astype(bf16)
            return carry
        for_rows(block, body)
    sent = [send(n_v, n_out, out_sems.at[0]), send(r_v, r_out, out_sems.at[1])]
    copies[4].wait()
    cq_v[...] = dg(low_v[...], held[1], NN).astype(bf16)
    sent.append(send(cq_v, cq_out, out_sems.at[2]))
    wait_all(sent)


def first_norm(scalars, oT, tokens, x_swap, w_out, w_query, gain, bias):
    width, rows = oT.shape
    block = x_swap.shape[0]
    return pl.pallas_call(
        first_norm_kernel,
        in_specs=[SMEM] + [HBM] * 5 + [VMEM] * 2,
        out_specs=[HBM] * 3,
        out_shape=[far_shape((rows, width), f32), far_shape((rows, PAIR), f32), shape((rows, width), bf16)],
        scratch_shapes=[pltpu.VMEM((width, rows), bf16), pltpu.VMEM((2, block, width), bf16),
                        pltpu.VMEM((2, width, width), bf16), pltpu.VMEM((rows, width), f32),
                        pltpu.VMEM((rows, PAIR), f32), pltpu.VMEM((rows, width), bf16),
                        pltpu.VMEM((rows, width), bf16), dma(5), dma(3)],
        compiler_params=params(16),
        cost_estimate=cost(4 * rows * width * width, 4 * width * width + 10 * rows * width),
        name="first_norm",
    )(scalars, oT, tokens, x_swap, w_out, w_query, gain, bias)


def gelu_parts(x):
    phi = 0.5 + 0.5 * lax.erf(x * math.sqrt(0.5))
    gauss = jnp.exp2(x * x * (-HALF_LOG2E))
    return x * phi, phi + x * gauss * (1.0 / math.sqrt(2.0 * math.pi))


def feed_forward_kernel(chunk, sc_ref, step_ref, oT, n1, grads, g_swap, w_out, w_in, w_back, w_down, w_up,
                        gain_ref, bias_ref,
                        out_own, out_swap, n2_out, r2_out, slope_out, g3_out, gai_out, wg_out0, wg_out1, wg_out2, wg_out3, sums_ref,
                        oT_v, g_v, out_w, in_w, back_w, down_w, up_w, n2_v, r2_v, low_v, upd_v, slope_v,
                        y_v, gai_v, wg_v, sems, in_sems, back_sems, out_sems, slope_sems):
    block = g_v.shape[1]
    rows, width = upd_v.shape
    chunks = in_w.shape[0]
    adapter = down_w.shape[1]
    side = sc_ref[SIDE]
    wg_outs = (wg_out0, wg_out1, wg_out2, wg_out3)

    def in_copy(c):
        return pltpu.make_async_copy(
            w_in.at[:, pl.ds(pl.multiple_of(c * chunk, chunk), chunk)], in_w.at[c], in_sems.at[c])

    def back_copy(c):
        return pltpu.make_async_copy(
            w_back.at[pl.ds(pl.multiple_of(c * chunk, chunk), chunk)], back_w.at[c], back_sems.at[c])

    def slope_copy(c):
        cols = pl.ds(pl.multiple_of(c * chunk, chunk), chunk)
        return pltpu.make_async_copy(slope_v.at[c], slope_out.at[:, cols], slope_sems.at[c])

    copies = [pltpu.make_async_copy(src, dst, sems.at[n]) for n, (src, dst) in enumerate(
        ((oT, oT_v), (w_out, out_w), (n1, upd_v), (w_down, down_w), (w_up, up_w),
         (grads.at[side], g_v.at[0]), (g_swap, g_v.at[1])))]
    for copy in copies[:3]:
        copy.start()

    gain1, bias1 = gain_ref[0:1], bias_ref[0:1]
    gain2, bias2 = gain_ref[1:2], bias_ref[1:2]
    gain3, bias3 = gain_ref[2:3], bias_ref[2:3]
    wait_all(copies[:2])
    for copy in copies[3:5]:
        copy.start()
    in_copy(0).start()
    back_copy(0).start()
    n2_v[...] = dg(oT_v[...], out_w[...], TN)
    copies[2].wait()
    for copy in copies[5:]:
        copy.start()

    def second(at, carry):
        sl = at(0)
        n, r = normalized(n2_v[sl] + upd_v[sl] * gain1 + bias1)
        n2_v[sl] = n
        r2_v[sl] = spread_lanes(r)
        low_v[sl] = (n * gain2 + bias2).astype(bf16)
        return carry

    for_rows(rows, second)
    sent = [send(n2_v, n2_out, out_sems.at[0]), send(r2_v, r2_out, out_sems.at[1])]

    wait_all(copies[3:5])
    factor = (1.0 + step_ref[side].astype(f32)) * 0.25
    adapter_in = dg(low_v[...], down_w[...], NN)
    sig = 1.0 / (1.0 + jnp.exp(-adapter_in))
    adapter_hidden = (factor * (adapter_in * sig)).astype(bf16)
    adapter_slope = factor * (sig * (1.0 + adapter_in * (1.0 - sig)))
    upd_v[...] = dg(adapter_hidden, up_w[...], NN)

    def step(c, carry):
        @pl.when(c + 1 < chunks)
        def _():
            in_copy(c + 1).start()
            back_copy(c + 1).start()

        in_copy(c).wait()
        weight = in_w[c]
        parts = [dg(low_v[pl.ds(b * block, block)], weight, NN) for b in range(2)]
        back_copy(c).wait()
        weight = back_w[c]
        for b in range(2):
            here = pl.ds(b * block, block)
            value, slope = gelu_parts(parts[b])
            slope_v[c, here] = slope.astype(bf16)
            upd_v[here] += dg(value.astype(bf16), weight, NN)
        slope_copy(c).start()
        return carry

    lax.fori_loop(0, chunks, step, 0)

    sums = zero_sums(2, width)
    wait_all(copies[5:])
    for half, target in enumerate((out_own.at[side], out_swap)):
        def third(at, carry, half=half):
            sl = at(0)
            here = at(half * block)
            n, r = normalized(n2_v[here] * gain2 + bias2 + upd_v[here])
            y_v[half, sl] = (n * gain3 + bias3).astype(bf16)
            G = g_v[half, sl].astype(f32)
            upd_v[here] = norm_back(G, n, r, gain3)
            return carry[0] + fold(G * n), carry[1] + fold(G)
        sums = for_rows(block, third, sums)
        sent.append(send(y_v.at[half], target, out_sems.at[2 + half]))
    sent.append(send(upd_v, g3_out, out_sems.at[4]))
    store_sums(sums_ref, sums)

    core, rank, beside = sc_ref[CORE], sc_ref[HALF], sc_ref[NEXT]

    def put(which, value):
        part = adapter // 4
        for n in range(4):
            rows_here = pl.ds(pl.multiple_of(((n % 2) ^ beside) * part, part), part)
            wg_v[2 * (which ^ core) + ((n // 2) ^ rank), rows_here] = value[n * part:(n + 1) * part]

    grad_update = upd_v[...].astype(bf16)
    put(0, dg(adapter_hidden, grad_update, TN).astype(bf16))
    gai = (adapter_slope * dg(grad_update, up_w[...], NT)).astype(bf16)
    gai_v[...] = gai
    sent.append(send(gai_v, gai_out, out_sems.at[5]))
    put(1, dg(gai, low_v[...], TN).astype(bf16))
    for n in (3, 1, 2, 0):
        sent.append(send(wg_v.at[n], wg_outs[n], out_sems.at[6 + n]))

    def drain(c, carry):
        slope_copy(c).wait()
        return carry

    lax.fori_loop(0, chunks, drain, 0)
    wait_all(sent)


def feed_forward(scalars, steps, oT, n1, grads, g_swap, w_out, w_in, w_back, w_down, w_up, gain, bias):
    rows, width = n1.shape
    block = g_swap.shape[0]
    units = w_in.shape[1]
    adapter = w_down.shape[1]
    chunk = 1024
    chunks = units // chunk
    return pl.pallas_call(
        functools.partial(feed_forward_kernel, chunk),
        in_specs=[SMEM, SMEM] + [HBM] * 9 + [VMEM] * 2,
        out_specs=[HBM] * 11 + [VMEM],
        out_shape=[
            far_shape((2, block, width), bf16), far_shape((block, width), bf16), far_shape((rows, width), f32),
            far_shape((rows, PAIR), f32), far_shape((rows, units), bf16), far_shape((rows, width), f32),
            far_shape((rows, adapter), bf16)]
        + [far_shape((adapter // 2, width), bf16)] * 4 + [
            shape((2, width), f32),
        ],
        scratch_shapes=[
            pltpu.VMEM((width, rows), bf16), pltpu.VMEM((2, block, width), bf16),
            pltpu.VMEM((width, width), bf16), pltpu.VMEM((chunks, width, chunk), bf16),
            pltpu.VMEM((chunks, chunk, width), bf16), pltpu.VMEM((width, adapter), bf16),
            pltpu.VMEM((adapter, width), bf16), pltpu.VMEM((rows, width), f32), pltpu.VMEM((rows, PAIR), f32),
            pltpu.VMEM((rows, width), bf16), pltpu.VMEM((rows, width), f32),
            pltpu.VMEM((chunks, rows, chunk), bf16),
            pltpu.VMEM((2, block, width), bf16), pltpu.VMEM((rows, adapter), bf16),
            pltpu.VMEM((4, adapter // 2, width), bf16),
            dma(7), dma(chunks), dma(chunks), dma(10), dma(chunks),
        ],
        compiler_params=params(52),
        cost_estimate=cost(4 * rows * width * units + 12 * rows * width * adapter + 2 * rows * width * width,
                           4 * width * units, 2 * rows * units),
        name="feed_forward",
    )(scalars, steps, *far(oT, n1, grads, g_swap, w_out, w_in, w_back, w_down, w_up), gain, bias)


def feed_back_kernel(chunk, g3, slope, gai, n2, r2, w_in, w_back, w_down, w_out, gain_ref, sums3_ref,
                     g2_out, aT_out, sums_ref,
                     g2_v, slope_v, gai_v, n2_v, r2_v, out_w, in_w, back_w, down_w, low_v, aT_v,
                     sems, in_sems, back_sems, slope_sems, out_sems):
    rows, width = g2_v.shape
    chunks = in_w.shape[0]
    block = rows // 2

    def in_copy(c):
        return pltpu.make_async_copy(
            w_in.at[:, pl.ds(pl.multiple_of(c * chunk, chunk), chunk)], in_w.at[c], in_sems.at[c])

    def back_copy(c):
        return pltpu.make_async_copy(
            w_back.at[pl.ds(pl.multiple_of(c * chunk, chunk), chunk)], back_w.at[c], back_sems.at[c])

    def slope_copy(c):
        cols = pl.ds(pl.multiple_of(c * chunk, chunk), chunk)
        return pltpu.make_async_copy(slope.at[:, cols], slope_v.at[c], slope_sems.at[c])

    copies = start_copies([(g3, g2_v), (w_down, down_w), (gai, gai_v)], sems)
    for c in range(chunks):
        back_copy(c).start()
        slope_copy(c).start()
        in_copy(c).start()
    copies += [send(n2, n2_v, sems.at[3]), send(r2, r2_v, sems.at[4]), send(w_out, out_w, sems.at[5])]
    copies[0].wait()
    low_v[...] = g2_v[...].astype(bf16)
    wait_all(copies[1:3])
    g2_v[...] += dg(gai_v[...], down_w[...], NT)

    def step(c, carry):
        back_copy(c).wait()
        weight = back_w[c]
        parts = [dg(low_v[pl.ds(b * block, block)], weight, NT) for b in range(2)]
        in_copy(c).wait()
        slope_copy(c).wait()
        weight = in_w[c]
        for b in range(2):
            here = pl.ds(b * block, block)
            inner = (parts[b] * slope_v[c, here].astype(f32)).astype(bf16)
            g2_v[here] += dg(inner, weight, NT)
        return carry

    lax.fori_loop(0, chunks, step, 0)
    gain2 = gain_ref[1:2]
    wait_all(copies[3:])

    def second(at, carry):
        sl = at(0)
        G = g2_v[sl]
        n = n2_v[sl]
        grad = norm_back(G, n, r2_v[sl][:, 0:1], gain2)
        g2_v[sl] = grad
        low_v[sl] = grad.astype(bf16)
        return carry[0] + fold(G * n), carry[1] + fold(G)

    sums = for_rows(rows, second, zero_sums(2, width))
    sent = [send(g2_v, g2_out, out_sems.at[0])]
    store_sums(sums_ref, sums)
    sums_ref[2:4] = sums3_ref[...]
    aT_v[...] = dg(out_w[...], low_v[...], NT).astype(bf16)
    sent.append(send(aT_v, aT_out, out_sems.at[1]))
    wait_all(sent)


def feed_back(g3, slope, gai, n2, r2, w_in, w_back, w_down, w_out, gain, sums3):
    rows, width = g3.shape
    units = w_in.shape[1]
    adapter = w_down.shape[1]
    chunk = 1024
    chunks = units // chunk
    return pl.pallas_call(
        functools.partial(feed_back_kernel, chunk),
        in_specs=[HBM] * 9 + [VMEM] * 2,
        out_specs=[HBM] * 2 + [VMEM],
        out_shape=[shape((rows, width), f32), shape((width, rows), bf16), shape((4, width), f32)],
        scratch_shapes=[
            pltpu.VMEM((rows, width), f32), pltpu.VMEM((chunks, rows, chunk), bf16),
            pltpu.VMEM((rows, adapter), bf16), pltpu.VMEM((rows, width), f32), pltpu.VMEM((rows, PAIR), f32),
            pltpu.VMEM((width, width), bf16), pltpu.VMEM((chunks, width, chunk), bf16),
            pltpu.VMEM((chunks, chunk, width), bf16), pltpu.VMEM((width, adapter), bf16),
            pltpu.VMEM((rows, width), bf16), pltpu.VMEM((width, rows), bf16),
            dma(6), dma(chunks), dma(chunks), dma(chunks), dma(2),
        ],
        compiler_params=params(38),
        cost_estimate=cost(4 * rows * width * units + 2 * rows * width * adapter + 2 * rows * width * width,
                           4 * width * units),
        name="feed_back",
    )(*far(g3, slope, gai, n2, r2, w_in, w_back, w_down, w_out), gain, sums3)


def first_back_kernel(g2, dq, n1, r1, w_query, w_out, gain_ref, sums2_ref, g1_out, aT_out, sums_ref,
                      g1_v, dq_v, n_v, r_v, held, low_v, aT_v, sems, out_sems):
    copies = start_copies([(dq, dq_v), (w_query, held.at[0]), (g2, g1_v), (n1, n_v), (r1, r_v),
                           (w_out, held.at[1])], sems)
    rows, width = g1_v.shape
    wait_all(copies[:3])
    g1_v[...] += dg(dq_v[...], held[0], NT)
    gain = gain_ref[0:1]
    wait_all(copies[3:5])

    def body(at, carry):
        sl = at(0)
        G = g1_v[sl]
        n = n_v[sl]
        grad = norm_back(G, n, r_v[sl][:, 0:1], gain)
        g1_v[sl] = grad
        low_v[sl] = grad.astype(bf16)
        return carry[0] + fold(G * n), carry[1] + fold(G)

    sums = for_rows(rows, body, zero_sums(2, width))
    sent = [send(g1_v, g1_out, out_sems.at[0])]
    store_sums(sums_ref, sums)
    sums_ref[2:6] = sums2_ref[...]
    copies[5].wait()
    aT_v[...] = dg(held[1], low_v[...], NT).astype(bf16)
    sent.append(send(aT_v, aT_out, out_sems.at[1]))
    wait_all(sent)


def first_back(g2, dq, n1, r1, w_query, w_out, gain, sums2):
    rows, width = g2.shape
    return pl.pallas_call(
        first_back_kernel,
        in_specs=[HBM] * 6 + [VMEM] * 2,
        out_specs=[HBM] * 2 + [VMEM],
        out_shape=[shape((rows, width), f32), shape((width, rows), bf16), shape((6, width), f32)],
        scratch_shapes=[pltpu.VMEM((rows, width), f32), pltpu.VMEM((rows, width), bf16),
                        pltpu.VMEM((rows, width), f32), pltpu.VMEM((rows, PAIR), f32),
                        pltpu.VMEM((2, width, width), bf16), pltpu.VMEM((rows, width), bf16),
                        pltpu.VMEM((width, rows), bf16), dma(6), dma(2)],
        compiler_params=params(18),
        cost_estimate=cost(4 * rows * width * width, 4 * width * width + 10 * rows * width),
        name="first_back",
    )(g2, dq, *far(n1, r1), w_query, w_out, gain, sums2)


def summed(first, others):
    total = first.astype(f32)
    for ref in others:
        total = total + ref.astype(f32)
    return total.astype(bf16)


def key_grads_kernel(count, blocks, based, sc_ref, *refs):
    parts, refs = refs[:count], refs[count:]
    if based:
        base, dq, w_query, refs = refs[0], refs[1], refs[2], refs[3:]
    w_key, w_value, refs = refs[0], refs[1], refs[2:]
    outs, refs = refs[:len(blocks)], refs[len(blocks):]
    part_v, held, out_v = refs[:3]
    sems, out_sems = refs[-2:]
    size = out_v.shape[1]
    rows = size * len(blocks)
    order = [(w_key, held.at[0])] + [(ref, part_v.at[n]) for n, ref in enumerate(parts)]
    order.append((w_value, held.at[1]))
    total = None
    if based:
        here = pl.ds(blocks[0] * size, rows)
        first = start_copies([(dq.at[here], refs[4]), (w_query, held.at[2]), (base.at[here], refs[3])],
                             sems.at[pl.ds(2 + count, 3)])
    copies = start_copies(order, sems)
    if based:
        wait_all(first)
        total = refs[3][...] + dg(refs[4][...], held[2], NT)
    wait_all(copies[:1 + count])
    step = len(blocks)
    for n in range(2):
        if n == 1:
            copies[1 + count].wait()
        value = [summed(part_v[b, n], [part_v[r, n] for r in range(step + b, count, step)]) for b in range(step)]
        value = value[0] if step == 1 else jnp.concatenate(value, 0)
        total = add(total, dg(value, held[n], NT))
    sent = []
    for b in reversed(range(step)):
        out_v[b] = total[b * size:(b + 1) * size].astype(bf16)
        target = outs[b].at[sc_ref[SIDE]] if blocks[b] == 0 else outs[b]
        sent.append(send(out_v.at[b], target, out_sems.at[b]))
    wait_all(sent)


def key_grads(scalars, parts, w_key, w_value, base=None, blocks=(0, 1)):
    _, block, width = parts[0].shape
    count = len(parts)
    based = base is not None
    extra = list(base) if based else []
    return pl.pallas_call(
        functools.partial(key_grads_kernel, count, blocks, based),
        in_specs=[SMEM] + [HBM] * (count + 2 + len(extra)),
        out_specs=[HBM] * len(blocks),
        out_shape=[far_shape((2, block, width), bf16) if b == 0 else shape((block, width), bf16) for b in blocks],
        scratch_shapes=[pltpu.VMEM((count, 2, block, width), bf16),
                        pltpu.VMEM((3 if based else 2, width, width), bf16),
                        pltpu.VMEM((len(blocks), block, width), bf16)]
        + ([pltpu.VMEM((len(blocks) * block, width), f32), pltpu.VMEM((len(blocks) * block, width), bf16)]
           if based else [])
        + [dma(2 + count + len(extra)), dma(len(blocks))],
        compiler_params=params(20),
        cost_estimate=cost(8 * block * width * width, 4 * width * width),
        name="token_grad" if based else "enc_grad",
    )(scalars, *parts, *extra, w_key, w_value)


def place_kernel(sc_ref, held, back, out, sem):
    send(back, out.at[1 - sc_ref[SIDE]], sem.at[0]).wait()


def put_back(scalars, out, back):
    return pl.pallas_call(
        place_kernel,
        in_specs=[SMEM, HBM, HBM],
        out_specs=HBM,
        out_shape=far_shape(out.shape, out.dtype),
        scratch_shapes=[dma(1)],
        input_output_aliases={1: 0},
        compiler_params=params(4),
        cost_estimate=cost(0, back.size * 4),
        name="place",
    )(scalars, *far(out), back)


def assemble_kernel(places, sc_ref, *refs):
    count = len(places)
    pieces = refs[:count]
    sums_a, sums_b, up_ref, down_ref, gains_ref, biases_ref = refs[count:]
    core, rank, beside = sc_ref[CORE], sc_ref[HALF], sc_ref[NEXT]
    for (first, second, third), piece in zip(places, pieces):
        block = first ^ core
        size = piece.shape[0]
        at = pl.ds(pl.multiple_of((2 * (second ^ rank) + (third ^ beside)) * size, size), size)

        @pl.when(block == 0)
        def _():
            up_ref[at] = piece[...].astype(f32)

        @pl.when(block == 1)
        def _():
            down_ref[:, at] = piece[...].T.astype(f32)
    total = sums_a[...] + sums_b[...]
    for n in range(3):
        gains_ref[n:n + 1] = total[2 * n:2 * n + 1]
        biases_ref[n:n + 1] = total[2 * n + 1:2 * n + 2]


def assemble(scalars, places, pieces, sums_a, sums_b):
    part, width = pieces[0].shape
    return pl.pallas_call(
        functools.partial(assemble_kernel, places),
        in_specs=[SMEM] + [VMEM] * (len(pieces) + 2),
        out_specs=[VMEM] * 4,
        out_shape=[shape((4 * part, width), f32), shape((width, 4 * part), f32), shape((3, width), f32),
                   shape((3, width), f32)],
        compiler_params=params(14),
        cost_estimate=cost(0, 24 * part * width),
        name="assemble",
    )(scalars, *pieces, sums_a, sums_b)


def exchange(x, step):
    axis, bit = step
    return lax.ppermute(x, axis, [(i, i ^ bit) for i in range(lax.axis_size(axis))])


def after(x, *others):
    return lax.optimization_barrier((x,) + others)[0]


def plus(x, *others):
    total = x.astype(f32)
    for y in others:
        total = total + y.astype(f32)
    return total.astype(x.dtype)


def bits(size):
    return [1 << n for n in range(size.bit_length() - 1)]


def position_table(group, block, far_bit, ranks):
    half = group // 2
    table = []
    for rank in range(ranks):
        for member in range(group):
            side = member // half
            low = group - 1 - member if side else member

            def starts(index):
                own = group - 1 - index if side else index
                return [own * block, (group - 1 - own) * block]

            row = [side, member & 1, int(rank & far_bit != 0), rank & 1, low * block, (group - 1 - low) * block]
            row += starts(low)
            tail = []
            for r in range(1, half):
                index = (low + r) % half
                wrap = low + r >= half
                row += starts(index)
                first, second = index * block, (group - 1 - index) * block
                tail += [int(wrap), first, first if wrap else second]
            table.append(row + tail)
    return jnp.asarray(table, jnp.int32)


def per_device(
    tokens, enc_states, dec_lengths, enc_lengths, adapter_step, out_grad,
    self_query, self_key, self_value, self_out, cross_query, cross_key, cross_value, cross_out,
    ffn_in, ffn_out, adapter_down, adapter_up, ln_gain, ln_bias,
):
    group, ranks = lax.axis_size("seq"), lax.axis_size("dp")
    half = group // 2
    member = lax.axis_index("seq")
    side = member // half
    block = tokens.shape[1]
    swap = [(i, group - 1 - i) for i in range(group)]
    seq_bits, dp_bits = bits(group), bits(ranks)
    core_step, far_step, side_step = ("seq", 1), ("dp", dp_bits[1]), ("dp", 1)
    full_steps = [("seq", b) for b in seq_bits[1:]] + [("dp", b) for b in dp_bits[2:]]
    scalars = lax.dynamic_index_in_dim(
        position_table(group, block, far_step[1], ranks), lax.axis_index("dp") * group + member, 0, keepdims=False)

    def place(s, index):
        return group - 1 - index if s == 1 else index

    def from_shift(r):
        return [(place(s, (i + r) % half), place(s, i)) for s in range(2) for i in range(half)]

    def to_shift(r):
        return [(place(s, i), place(s, (i + r) % half)) for s in range(2) for i in range(half)]

    def theirs(x):
        return lax.dynamic_index_in_dim(x, 1 - side, 0, keepdims=False)

    def swapped(x):
        return lax.ppermute(x, "seq", swap)

    def joined(out, back):
        return lax.dynamic_update_index_in_dim(out, back, 1 - side, 0)

    def gathered(own, other):
        every = [own, other]
        for r in range(1, half):
            every += [lax.ppermute(own, "seq", from_shift(r)), lax.ppermute(other, "seq", from_shift(r))]
        return every

    def returned(parts):
        return parts[:1] + [lax.ppermute(parts[r], "seq", to_shift(r)) for r in range(1, half)]

    x_swap = swapped(theirs(tokens))
    q_own, kv_own, ckv_own = project(
        scalars, [tokens, enc_states], [self_key, self_value, self_query, cross_key, cross_value],
        ((0, 1, 0), (0, 1, 1), (0, 0, None), (1, 2, 0), (1, 2, 1)), "project_own", pin=True)
    e_theirs, g_theirs = theirs(enc_states), theirs(out_grad)
    e_swap = swapped(after(e_theirs, x_swap))
    kv_swap, q_swap = project(
        scalars, [x_swap], [self_key, self_value, self_query], ((0, 0, 0), (0, 0, 1), (0, 1, None)),
        "project_swap")
    kvs = gathered(kv_own, kv_swap)
    oT, probs, inverse = self_forward(scalars, dec_lengths, q_own, q_swap, kvs)
    ckv_swap, = project(
        scalars, [after(e_swap, oT)], [cross_key, cross_value], ((0, 0, 0), (0, 0, 1)), "project_enc")
    g_swap = swapped(after(g_theirs, e_swap))
    ckvs = gathered(ckv_own, ckv_swap)
    n1, r1, cq = first_norm(scalars, after(oT, ckv_swap), tokens, x_swap, self_out, cross_query, ln_gain, ln_bias)
    coT, cprobs, cinverse = cross_forward(scalars, enc_lengths, cq, ckvs)
    out_own, out_swap, n2, r2, slope, g3, gai, *wgs, sums3 = feed_forward(
        scalars, adapter_step, coT, n1, out_grad, g_swap, cross_out, ffn_in, ffn_out, adapter_down, adapter_up,
        ln_gain, ln_bias)

    forwarded = plus(wgs[1], exchange(wgs[3], core_step))
    received = exchange(forwarded, far_step)
    kept = exchange(wgs[2], core_step)
    out_back = swapped(out_swap)
    g2, caT, sums2 = feed_back(after(g3, forwarded), slope, gai, n2, r2, ffn_in, ffn_out, adapter_down, cross_out,
                               ln_gain, sums3)
    size = kept.shape[0] // 2
    received = after(received, g2)
    wg, forwarded = [plus(x, y, z) for x, y, z in zip(*(
        (part[:size], part[size:]) for part in (wgs[0], kept, received)))]
    layer_output = joined(out_own, after(out_back, g2))

    received = exchange(forwarded, side_step)
    cdq, *cdkvs = cross_backward(cq, cprobs, after(caT, forwarded, layer_output), coT, cinverse, ckvs)
    wg = plus(wg, after(received, cdq))
    cdkvs = [after(x, wg) for x in cdkvs]
    enc_parts = [x for pair in zip(returned(cdkvs[0::2]), returned(cdkvs[1::2])) for x in pair]
    received = exchange(wg, full_steps[0])
    g1, aT, sums = first_back(after(g2, wg), cdq, n1, r1, cross_query, self_out, ln_gain, sums2)
    y_steps = [("seq", bit) for bit in seq_bits[1:]]
    z_steps = [("dp", b) for b in dp_bits[2:]]
    received_sums = exchange(sums, z_steps[0])
    enc_own, enc_swap = key_grads(scalars, [after(enc_parts[0], aT)] + enc_parts[1:], cross_key, cross_value)
    wg = plus(wg, after(received, enc_swap))
    sums = plus(sums, after(received_sums, enc_swap))
    for step in full_steps[1:-1]:
        wg = plus(wg, exchange(wg, step))
    received = exchange(wg, full_steps[-1])
    received_sums = exchange(sums, far_step)
    enc_back = swapped(enc_swap)

    dq, *dkvs = self_backward(scalars, q_own, q_swap, probs, after(aT, wg, sums, enc_swap), oT, inverse, kvs)
    wg = plus(wg, after(received, dq))
    sums = plus(sums, after(received_sums, dq))
    enc_grad = joined(enc_own, after(enc_back, dq))
    dkvs = [after(x, wg, sums, enc_back) for x in dkvs]
    swap_parts = returned(dkvs[1::2])
    both_step = ("dp", side_step[1] | far_step[1])
    beside, beyond, across, sibling = (exchange(wg, step) for step in (side_step, far_step, both_step, core_step))
    for step in y_steps[1:] + z_steps[1:]:
        sums = plus(sums, exchange(sums, step))
    received_sums = exchange(sums, y_steps[0])
    base = (g1, dq, self_query)
    own_parts = returned(dkvs[0::2])
    t_swap, = key_grads(scalars, swap_parts, self_key, self_value, base, (1,))
    t_back = swapped(t_swap)
    sums = plus(sums, after(received_sums, t_swap))
    received_sums = exchange(sums, side_step)
    across = after(across, t_swap)
    t_own, = key_grads(scalars, own_parts, self_key, self_value, (after(g1, t_swap, across), dq, self_query), (0,))
    beside, beyond = (after(x, t_own) for x in (beside, beyond))
    sums = plus(sums, after(received_sums, t_own))
    received_sums = exchange(sums, core_step)
    places = [(0, 0, 0), (0, 0, 1), (0, 1, 0), (0, 1, 1), (1, 0, 0), (1, 0, 1), (1, 1, 0), (1, 1, 1)]
    pieces = [wg, beside, beyond, across, sibling] + [exchange(x, core_step) for x in (beside, beyond, across)]
    up, down, gains, biases = assemble(scalars, places, pieces, sums, received_sums)
    return layer_output, put_back(scalars, t_own, after(t_back, up)), enc_grad, down, up, gains, biases


def solution(mesh):
    rows = P("dp", "seq", None)
    return jax.shard_map(
        per_device,
        mesh=mesh,
        in_specs=(rows, rows, P("dp"), P("dp"), P("dp"), rows) + (P(),) * 14,
        out_specs=(rows, rows, rows, P(), P(), P(), P()),
        check_vma=False,
    )
```

```python
import functools
import math

import jax
import jax.numpy as jnp
from jax import lax
from jax.experimental import pallas as pl
from jax.experimental.pallas import tpu as pltpu
from jax.sharding import PartitionSpec as P

HEAD_DIM = 64
PAIR = 2 * HEAD_DIM
EPS = 1e-05
NEGATIVE = -1e30
SCALE = HEAD_DIM ** (-0.5)
EXP2_SCALE = SCALE * math.log2(math.e)
HALF_LOG2E = 0.5 * math.log2(math.e)

f32 = jnp.float32
bf16 = jnp.bfloat16

NN = (((1,), (0,)), ((), ()))
NT = (((1,), (1,)), ((), ()))
TN = (((0,), (0,)), ((), ()))

HBM = pl.BlockSpec(memory_space=pltpu.HBM)
SMEM = pl.BlockSpec(memory_space=pltpu.SMEM)
VMEM = pl.BlockSpec(memory_space=pltpu.VMEM)
MIB = 2 ** 20

SIDE, CORE, HALF, NEXT, LOW, HIGH, STARTS = range(7)


def dg(left, right, dims):
    return lax.dot_general(left, right, dims, preferred_element_type=f32)


def add(total, term):
    return term if total is None else total + term


def params(limit_mib):
    return pltpu.CompilerParams(vmem_limit_bytes=limit_mib * MIB)


def cost(flops, nbytes, exps=0):
    return pl.CostEstimate(flops=int(flops), bytes_accessed=int(nbytes), transcendentals=int(exps))


def shape(dims, dtype):
    return jax.ShapeDtypeStruct(dims, dtype)


def far(*arrays):
    return [pltpu.with_memory_space_constraint(x, pltpu.HBM) for x in arrays]


def far_shape(dims, dtype):
    return pltpu.HBM(dims, dtype)


def start_copies(pairs, sems):
    copies = [pltpu.make_async_copy(src, dst, sems.at[n]) for n, (src, dst) in enumerate(pairs)]
    for copy in copies:
        copy.start()
    return copies


def project_kernel(plan, n_in, sc_ref, *refs):
    count = len(plan)
    xs = refs[:n_in]
    ws = refs[n_in:n_in + count]
    n_out = 1 + max(o for _, o, _ in plan)
    outs = refs[n_in + count:n_in + count + n_out]
    x_held, held, out_held, sems, out_sems = refs[n_in + count + n_out:]
    side = sc_ref[0]
    first = [(x.at[side] if len(x.shape) == 3 else x, x_held.at[i]) for i, x in enumerate(xs)]
    copies = start_copies(first + [(w, held.at[j]) for j, w in enumerate(ws)], sems)
    for i in range(n_in):
        copies[i].wait()
    sent = []
    for j, (i, o, row) in enumerate(plan):
        copies[n_in + j].wait()
        out_held[j] = dg(x_held[i], held[j], NN).astype(bf16)
        target = outs[o] if row is None else outs[o].at[row]
        sent.append(pltpu.make_async_copy(out_held.at[j], target, out_sems.at[j]))
        sent[-1].start()
    for copy in sent:
        copy.wait()


def project(scalars, xs, ws, plan, name, pin=False):
    rows, width = xs[0].shape[-2:]
    count = len(plan)
    n_out = 1 + max(o for _, o, _ in plan)
    out_shape = []
    for o in range(n_out):
        used = [row for _, oo, row in plan if oo == o]
        out_shape.append(shape((rows, width) if used[0] is None else (len(used), rows, width), bf16))
    return pl.pallas_call(
        functools.partial(project_kernel, plan, len(xs)),
        in_specs=[SMEM] + [HBM] * (len(xs) + count),
        out_specs=[HBM] * n_out,
        out_shape=out_shape,
        scratch_shapes=[pltpu.VMEM((len(xs), rows, width), bf16), pltpu.VMEM((count, width, width), bf16),
                        pltpu.VMEM((count, rows, width), bf16),
                        pltpu.SemaphoreType.DMA((len(xs) + count,)), pltpu.SemaphoreType.DMA((count,))],
        compiler_params=params(28),
        cost_estimate=cost(2 * count * rows * width * width, 2 * count * width * width),
        name=name,
    )(scalars, *(far(*xs, *ws) if pin else (*xs, *ws)))


def pair_masks():
    lane = lax.broadcasted_iota(jnp.int32, (1, PAIR), 1)
    return lane, lane < HEAD_DIM


def key_bias(start, length, rows):
    pos = start + lax.broadcasted_iota(jnp.int32, (rows, PAIR), 0)
    lane = lax.broadcasted_iota(jnp.int32, (rows, PAIR), 1)
    masked = jnp.where(pos < length, 0.0, NEGATIVE)
    return (
        jnp.where(lane == HEAD_DIM, masked, 0.0).astype(bf16),
        jnp.where(lane == 0, masked, 0.0).astype(bf16),
    )


def queries_with_one(q, half):
    one = jnp.ones((), bf16)
    return jnp.where(half, q, one), jnp.where(half, one, q)


def head_only(x, half):
    zero = jnp.zeros((), bf16)
    return jnp.where(half, x, zero), jnp.where(half, zero, x)


def soft(scores, highest):
    if highest is None:
        return jnp.exp2(scores * EXP2_SCALE).astype(bf16)
    return jnp.exp2((scores - highest) * EXP2_SCALE).astype(bf16)


EXPONENTS = 80.0


def scores_are_small(queries, keys):
    width = queries[0].shape[1]
    row = lax.broadcasted_iota(jnp.int32, (16, width), 0)
    lane = lax.broadcasted_iota(jnp.int32, (16, width), 1)
    pick = jnp.where(row == lane // HEAD_DIM, 1.0, 0.0).astype(bf16)

    def largest(blocks):
        total = None
        for x in blocks:
            norms = dg(pick, x * x, NT)
            total = norms if total is None else jnp.maximum(total, norms)
        return total.max(1, keepdims=True)

    limit = EXPONENTS / EXP2_SCALE / 1.02
    return jnp.max(largest(queries) * largest(keys)) <= limit * limit


def heads_with_ones(vT):
    ones = jnp.ones((16, vT.shape[1]), bf16)
    return [jnp.concatenate([vT[h * HEAD_DIM:(h + 1) * HEAD_DIM], ones], 0) for h in range(2)]


def probs_out(p_v, p_out, sems):
    step, last = pl.program_id(0), pl.num_programs(0) - 1
    count = p_v.shape[1]

    def copy(n, at):
        return pltpu.make_async_copy(p_v.at[at % 2, n], p_out.at[at * count + n], sems.at[at % 2, n])

    def before():
        @pl.when(step >= 2)
        def _():
            for n in range(count):
                copy(n, step - 2).wait()

    def end():
        @pl.when(step == last)
        def _():
            for n in range(count):
                copy(n, step - 1).wait()
            for n in range(count):
                copy(n, step).wait()

    return before, lambda n: copy(n, step).start(), end


def top(chunks):
    highest = chunks[0].max(0, keepdims=True)
    for s in chunks[1:]:
        highest = jnp.maximum(highest, s.max(0, keepdims=True))
    return highest


def grad_columns(aT, oT, inverse, half):
    rows = aT.shape[1]
    sub = lax.broadcasted_iota(jnp.int32, (HEAD_DIM, rows), 0)
    full, plain = [], []
    for h in range(2):
        sl = slice(h * HEAD_DIM, (h + 1) * HEAD_DIM)
        a = aT[sl].astype(f32) * inverse[h:h + 1]
        d = -(a * oT[sl].astype(f32)).sum(0, keepdims=True)
        high = d.astype(bf16).astype(f32)
        extra = jnp.where(sub == 0, high, jnp.where(sub == 1, d - high, 0.0)).astype(bf16)
        a = a.astype(bf16)
        full.append(jnp.concatenate([a, extra] if h == 0 else [extra, a], 0))
        plain.append(a)
    return full, head_only(jnp.concatenate(plain, 0).T, half)


def values_with_ones(v, lane, half):
    first = jnp.where((lane == HEAD_DIM) | (lane == HEAD_DIM + 1), 1.0, 0.0).astype(bf16)
    second = jnp.where(lane < 2, 1.0, 0.0).astype(bf16)
    return jnp.where(half, v, first), jnp.where(half, second, v)


def cross_forward_kernel(n, per, sc_ref, len_ref, q_ref, *refs):
    kvs = refs[:n]
    oT_ref, p_out, inv_ref, bias_ref, p_v, p_sems = refs[n:]
    p_before, p_send, p_end = probs_out(p_v, p_out, p_sems)
    p_ref = p_v.at[pl.program_id(0) % 2]
    rows = q_ref.shape[0]
    block = kvs[0].shape[1]
    lane, half = pair_masks()

    @pl.when(pl.program_id(0) == 0)
    def _():
        length = len_ref[sc_ref[SIDE]]
        for j in range(n):
            bias_ref[0, j], bias_ref[1, j] = key_bias(sc_ref[STARTS + j], length, block)

    def prepare(u):
        lanes = slice(u * PAIR, (u + 1) * PAIR)
        keys, values = [[], []], [[], []]
        for j in range(n):
            k = kvs[j][0, :, lanes]
            keys[0].append(jnp.where(half, k, bias_ref[0, j]))
            keys[1].append(jnp.where(half, bias_ref[1, j], k))
            for h, v in enumerate(heads_with_ones(kvs[j][1, :, lanes].T)):
                values[h].append(v)
        return keys, values, queries_with_one(q_ref[:, lanes], half)

    items = [(u, h, b) for u in range(per) for h in range(2) for b in range(rows // block)]

    def attend(small):
        ready = [prepare(u) for u in range(per)]

        def score(item):
            u, h, b = item
            q = ready[u][2][h][b * block:(b + 1) * block]
            return [dg(k, q, NT) for k in ready[u][0][h]]

        later = score(items[0])
        for step, (u, h, b) in enumerate(items):
            chunks = later
            if step + 1 < len(items):
                later = score(items[step + 1])
            highest = None if small else top(chunks)
            cols = pl.ds(b * block, block)
            out = None
            for j in range(n):
                p = soft(chunks[j], highest)
                p_ref[2 * u + h, pl.ds(j * block, block), cols] = p
                out = add(out, dg(ready[u][1][h][j], p, NN))
            inverse = 1.0 / out[HEAD_DIM:HEAD_DIM + 1]
            inv_ref[u, pl.ds(h, 1), cols] = inverse
            oT_ref[pl.ds((2 * u + h) * HEAD_DIM, HEAD_DIM), cols] = (out[:HEAD_DIM] * inverse).astype(bf16)
            if (b + 1) * block == rows:
                p_send(2 * u + h)

    p_before()
    small = scores_are_small([q_ref[:block], q_ref[block:]], [kv[0] for kv in kvs])
    pl.when(small)(lambda: attend(True))
    pl.when(jnp.logical_not(small))(lambda: attend(False))
    p_end()


def feature_rows(rows, per=1):
    return pl.BlockSpec((per * PAIR, rows), lambda i: (i, 0))


def feature_cols(rows, per=1):
    return pl.BlockSpec((rows, per * PAIR), lambda i: (0, i))


def kv_cols(rows, per=1):
    return pl.BlockSpec((2, rows, per * PAIR), lambda i: (0, 0, i))


def pair_block(*dims):
    return pl.BlockSpec(dims, lambda i: (i,) + (0,) * (len(dims) - 1))


CROSS_FORWARD_PAIRS, CROSS_BACKWARD_PAIRS, SELF_FORWARD_PAIRS, SELF_BACKWARD_PAIRS = 4, 2, 4, 2


def cross_forward(scalars, lengths, q, kvs):
    n = len(kvs)
    rows, width = q.shape
    block = kvs[0].shape[1]
    pairs = width // PAIR
    every = n * block
    per = CROSS_FORWARD_PAIRS
    return pl.pallas_call(
        functools.partial(cross_forward_kernel, n, per),
        grid=(pairs // per,),
        in_specs=[SMEM, SMEM, feature_cols(rows, per)] + [kv_cols(block, per)] * n,
        out_specs=[feature_rows(rows, per), HBM, pair_block(per, 2, rows)],
        out_shape=[
            far_shape((width, rows), bf16),
            far_shape((2 * pairs, every, rows), bf16),
            far_shape((pairs, 2, rows), f32),
        ],
        scratch_shapes=[pltpu.VMEM((2, n, block, PAIR), bf16), pltpu.VMEM((2, 2 * per, every, rows), bf16),
                        pltpu.SemaphoreType.DMA((2, 2 * per))],
        compiler_params=params(36),
        cost_estimate=cost(16 * rows * every * width, 4 * pairs * every * rows, 2 * pairs * every * rows),
        name="cross_forward",
    )(scalars, lengths, q, *kvs)


def cross_backward_kernel(n, per, q_ref, p_ref, aT_ref, oT_ref, inv_ref, *refs):
    kvs = refs[:n]
    dq_ref = refs[n]
    dkvs = refs[n + 1:]
    rows = q_ref.shape[0]
    block = kvs[0].shape[1]
    lane, half = pair_masks()

    def prepare(u):
        lanes = slice(u * PAIR, (u + 1) * PAIR)
        values, keysT = [[], []], []
        for j in range(n):
            first, second = values_with_ones(kvs[j][1, :, lanes], lane, half)
            values[0].append(first)
            values[1].append(second)
            keysT.append(kvs[j][0, :, lanes].T)
        full, plain = grad_columns(aT_ref[lanes], oT_ref[lanes], inv_ref[u], half)
        return values, keysT, head_only(q_ref[:, lanes], half), full, plain

    ready = [prepare(u) for u in range(per)]
    items = [(u, b, h) for u in range(per) for b in range(rows // block) for h in range(2)]

    def grad_probs(item):
        u, b, h = item
        a = ready[u][3][h][:, b * block:(b + 1) * block]
        return [dg(v, a, NN) for v in ready[u][0][h]]

    later = grad_probs(items[0])
    for step, (u, b, h) in enumerate(items):
        values, keysT, queries, full, plain = ready[u]
        dps = later
        if step + 1 < len(items):
            later = grad_probs(items[step + 1])
        if (b, h) == (0, 0):
            dk, dv, halves = [None] * n, [None] * n, []
        dq = None
        sl = slice(b * block, (b + 1) * block)
        for j in range(n):
            p = p_ref[2 * u + h, pl.ds(j * block, block), pl.ds(b * block, block)]
            ds = (p * dps[j]).astype(bf16)
            dv[j] = add(dv[j], dg(p, plain[h][sl], NN))
            dk[j] = add(dk[j], dg(ds, queries[h][sl], NN))
            dq = add(dq, dg(keysT[j][h * HEAD_DIM:(h + 1) * HEAD_DIM], ds, NN))
        halves.append((dq * SCALE).astype(bf16))
        lanes = slice(u * PAIR, (u + 1) * PAIR)
        if h == 1:
            dq_ref[sl, lanes] = jnp.concatenate(halves[-2:], 0).T
        if sl.stop == rows and h == 1:
            for j in range(n):
                dkvs[j][0, :, lanes] = (dk[j] * SCALE).astype(bf16)
                dkvs[j][1, :, lanes] = dv[j].astype(bf16)


def cross_backward(q, probs, aT, oT, inverse, kvs):
    n = len(kvs)
    rows, width = q.shape
    block = kvs[0].shape[1]
    pairs = width // PAIR
    every = n * block
    per = CROSS_BACKWARD_PAIRS
    return pl.pallas_call(
        functools.partial(cross_backward_kernel, n, per),
        grid=(pairs // per,),
        in_specs=[feature_cols(rows, per), pair_block(2 * per, every, rows), feature_rows(rows, per),
                  feature_rows(rows, per), pair_block(per, 2, rows)] + [kv_cols(block, per)] * n,
        out_specs=[feature_cols(rows, per)] + [kv_cols(block, per)] * n,
        out_shape=[shape((rows, width), bf16)] + [shape((2, block, width), bf16)] * n,
        compiler_params=params(24),
        cost_estimate=cost(32 * rows * every * width, 4 * pairs * every * rows),
        name="cross_backward",
    )(*far(q, probs), aT, *far(oT, inverse, *kvs))


def self_forward_kernel(others, per, sc_ref, len_ref, q_own, q_swap, *refs):
    kvs = refs[:2 + 2 * others]
    oT_ref, p_out, inv_ref, tri_ref, p_v, p_sems = refs[2 + 2 * others:]
    p_before, p_send, p_end = probs_out(p_v, p_out, p_sems)
    p_ref = p_v.at[pl.program_id(0) % 2]
    block = q_own.shape[0]
    lane, half = pair_masks()
    swapped = sc_ref[SIDE] == 1
    length = len_ref[sc_ref[SIDE]]
    first_wrap = STARTS + 2 + 2 * others
    wraps = [sc_ref[first_wrap + 3 * r] == 1 for r in range(others)]
    key_starts = [sc_ref[LOW], sc_ref[HIGH]]
    for r in range(others):
        key_starts += [sc_ref[first_wrap + 3 * r + 1], sc_ref[first_wrap + 3 * r + 2]]

    @pl.when(pl.program_id(0) == 0)
    def _():
        key = lax.broadcasted_iota(jnp.int32, (block, block), 0)
        query = lax.broadcasted_iota(jnp.int32, (block, block), 1)
        tri_ref[...] = jnp.where(key <= query, 0.0, NEGATIVE)

    biases = [key_bias(start, length, block) for start in key_starts]

    def low_high(first, second):
        return jnp.where(swapped, second, first), jnp.where(swapped, first, second)

    def prepare(u):
        lanes = slice(u * PAIR, (u + 1) * PAIR)
        q_low, q_high = low_high(q_own[:, lanes], q_swap[:, lanes])
        ks = list(low_high(kvs[0][0, :, lanes], kvs[1][0, :, lanes]))
        vs = list(low_high(kvs[0][1, :, lanes], kvs[1][1, :, lanes]))
        for r in range(others):
            first, second = low_high(kvs[2 + 2 * r][0, :, lanes], kvs[3 + 2 * r][0, :, lanes])
            ks += [first, jnp.where(wraps[r], first, second)]
            first, second = low_high(kvs[2 + 2 * r][1, :, lanes], kvs[3 + 2 * r][1, :, lanes])
            vs += [first, jnp.where(wraps[r], first, second)]
        keys = [(jnp.where(half, k, bias[0]), jnp.where(half, bias[1], k)) for k, bias in zip(ks, biases)]
        values = [heads_with_ones(v.T) for v in vs]
        ones = [queries_with_one(q_low, half), queries_with_one(q_high, half)]
        either = [tuple(jnp.where(w, ones[0][h], ones[1][h]) for h in range(2)) for w in wraps]
        return keys, values, ones, either

    def attend(small):
        ready = [prepare(u) for u in range(per)]
        tri = tri_ref[...]
        items = [(u, h) for u in range(per) for h in range(2)]

        def score(item):
            u, h = item
            keys, _, ones, either = ready[u]
            low = dg(keys[0][h], ones[0][h], NT) + tri
            high = [dg(keys[0][h], ones[1][h], NT), dg(keys[1][h], ones[1][h], NT) + tri]
            free = []
            for r in range(others):
                high.append(dg(keys[2 + 2 * r][h], ones[1][h], NT))
                free.append(dg(keys[3 + 2 * r][h], either[r][h], NT))
            return low, high, free

        later = score(items[0])
        for step, (u, h) in enumerate(items):
            values = ready[u][1]
            low, high, free = later
            if step + 1 < len(items):
                later = score(items[step + 1])
            top_low, top_high = None, None
            if not small:
                top_low = low.max(0, keepdims=True)
                top_high = top(high)
                for r in range(others):
                    peak = free[r].max(0, keepdims=True)
                    top_low = jnp.where(wraps[r], jnp.maximum(top_low, peak), top_low)
                    top_high = jnp.where(wraps[r], top_high, jnp.maximum(top_high, peak))

            def weigh(tile, scores, highest, v):
                p = soft(scores, highest)
                p_ref[2 * u + h, tile] = p
                return dg(v[h], p, NN)

            out_low = weigh(0, low, top_low, values[0])
            out_high = weigh(1, high[0], top_high, values[0]) + weigh(2, high[1], top_high, values[1])
            for r in range(others):
                out_high = out_high + weigh(3 + 2 * r, high[2 + r], top_high, values[2 + 2 * r])
                highest = None if small else jnp.where(wraps[r], top_low, top_high)
                out = weigh(4 + 2 * r, free[r], highest, values[3 + 2 * r])
                out_low = jnp.where(wraps[r], out_low + out, out_low)
                out_high = jnp.where(wraps[r], out_high, out_high + out)
            results = []
            for n, out in enumerate((out_low, out_high)):
                inverse = 1.0 / out[HEAD_DIM:HEAD_DIM + 1]
                inv_ref[u, n, pl.ds(h, 1), :] = inverse
                results.append((out[:HEAD_DIM] * inverse).astype(bf16))
            for n, out in enumerate(low_high(*results)):
                oT_ref[pl.ds((2 * u + h) * HEAD_DIM, HEAD_DIM), pl.ds(n * block, block)] = out
            p_send(2 * u + h)

    p_before()
    small = scores_are_small([q_own[...], q_swap[...]], [kv[0] for kv in kvs])
    pl.when(small)(lambda: attend(True))
    pl.when(jnp.logical_not(small))(lambda: attend(False))
    p_end()


def self_forward(scalars, lengths, q_own, q_swap, kvs):
    others = len(kvs) // 2 - 1
    block, width = q_own.shape
    pairs = width // PAIR
    tiles = 3 + 2 * others
    per = SELF_FORWARD_PAIRS
    return pl.pallas_call(
        functools.partial(self_forward_kernel, others, per),
        grid=(pairs // per,),
        in_specs=[SMEM, SMEM] + [feature_cols(block, per)] * 2 + [kv_cols(block, per)] * len(kvs),
        out_specs=[feature_rows(2 * block, per), HBM, pair_block(per, 2, 2, block)],
        out_shape=[
            shape((width, 2 * block), bf16),
            far_shape((2 * pairs, tiles, block, block), bf16),
            far_shape((pairs, 2, 2, block), f32),
        ],
        scratch_shapes=[pltpu.VMEM((block, block), f32), pltpu.VMEM((2, 2 * per, tiles, block, block), bf16),
                        pltpu.SemaphoreType.DMA((2, 2 * per))],
        compiler_params=params(26),
        cost_estimate=cost(16 * tiles * block * block * width, 4 * pairs * tiles * block * block,
                           2 * pairs * tiles * block * block),
        name="self_forward",
    )(scalars, lengths, q_own, q_swap, *kvs)


def self_backward_kernel(others, per, sc_ref, q_own, q_swap, p_ref, aT_ref, oT_ref, inv_ref, *refs):
    kvs = refs[:2 + 2 * others]
    dq_ref = refs[2 + 2 * others]
    dkvs = refs[3 + 2 * others:]
    block = q_own.shape[0]
    lane, half = pair_masks()
    swapped = sc_ref[SIDE] == 1
    first_wrap = STARTS + 2 + 2 * others
    wraps = [sc_ref[first_wrap + 3 * r] == 1 for r in range(others)]

    def low_high(first, second):
        return jnp.where(swapped, second, first), jnp.where(swapped, first, second)

    def prepare(u):
        lanes = slice(u * PAIR, (u + 1) * PAIR)
        ks = list(low_high(kvs[0][0, :, lanes], kvs[1][0, :, lanes]))
        vs = list(low_high(kvs[0][1, :, lanes], kvs[1][1, :, lanes]))
        for r in range(others):
            first, second = low_high(kvs[2 + 2 * r][0, :, lanes], kvs[3 + 2 * r][0, :, lanes])
            ks += [first, jnp.where(wraps[r], first, second)]
            first, second = low_high(kvs[2 + 2 * r][1, :, lanes], kvs[3 + 2 * r][1, :, lanes])
            vs += [first, jnp.where(wraps[r], first, second)]
        keysT = [k.T for k in ks]
        values = [values_with_ones(v, lane, half) for v in vs]
        sides = []
        a_blocks = low_high(aT_ref[lanes, 0:block], aT_ref[lanes, block:2 * block])
        o_blocks = low_high(oT_ref[lanes, 0:block], oT_ref[lanes, block:2 * block])
        q_blocks = low_high(q_own[:, lanes], q_swap[:, lanes])
        for n in range(2):
            full, plain = grad_columns(a_blocks[n], o_blocks[n], inv_ref[u, n], half)
            sides.append((full, plain, head_only(q_blocks[n], half)))
        for w in wraps:
            sides.append(tuple([jnp.where(w, x, y) for x, y in zip(first, second)]
                               for first, second in zip(sides[0], sides[1])))
        return keysT, values, sides

    ready = [prepare(u) for u in range(per)]
    tiles = [(0, 0, 0), (1, 0, 1), (2, 1, 1)]
    for r in range(others):
        tiles += [(3 + 2 * r, 2 + 2 * r, 1), (4 + 2 * r, 3 + 2 * r, 2 + r)]
    items = [(u, h) for u in range(per) for h in range(2)]

    def grad_probs(item):
        u, h = item
        _, values, sides = ready[u]
        return [dg(values[key][h], sides[side][0][h], NN) for _, key, side in tiles]

    later = grad_probs(items[0])
    for step, (u, h) in enumerate(items):
        keysT, _, sides = ready[u]
        dps = later
        if step + 1 < len(items):
            later = grad_probs(items[step + 1])
        if h == 0:
            dk, dv, both = [None] * len(keysT), [None] * len(keysT), []
        dq = [None] * len(sides)
        for (index, key, side), dp in zip(tiles, dps):
            p = p_ref[2 * u + h, index]
            ds = (p * dp).astype(bf16)
            dv[key] = add(dv[key], dg(p, sides[side][1][h], NN))
            dk[key] = add(dk[key], dg(ds, sides[side][2][h], NN))
            dq[side] = add(dq[side], dg(keysT[key][h * HEAD_DIM:(h + 1) * HEAD_DIM], ds, NN))
        for wrap, term in zip(wraps, dq[2:]):
            dq[0] = jnp.where(wrap, dq[0] + term, dq[0])
            dq[1] = jnp.where(wrap, dq[1], dq[1] + term)
        both.append([(x * SCALE).astype(bf16) for x in low_high(dq[0], dq[1])])
        if h == 0:
            continue
        lanes = slice(u * PAIR, (u + 1) * PAIR)
        for n in range(2):
            dq_ref[pl.ds(n * block, block), lanes] = jnp.concatenate([both[0][n], both[1][n]], 0).T

        for row, terms, factor in ((0, dk, SCALE), (1, dv, 1.0)):
            pairs = [(terms[0], terms[1])]
            for r, wrap in enumerate(wraps):
                always, either = terms[2 + 2 * r], terms[3 + 2 * r]
                pairs.append((jnp.where(wrap, always + either, always), jnp.where(wrap, 0.0, either)))
            for n, pair in enumerate(pairs):
                first, second = low_high(*pair)
                dkvs[2 * n][row, :, lanes] = (first * factor).astype(bf16)
                dkvs[2 * n + 1][row, :, lanes] = (second * factor).astype(bf16)


def self_backward(scalars, q_own, q_swap, probs, aT, oT, inverse, kvs):
    others = len(kvs) // 2 - 1
    block, width = q_own.shape
    pairs = width // PAIR
    tiles = 3 + 2 * others
    per = SELF_BACKWARD_PAIRS
    return pl.pallas_call(
        functools.partial(self_backward_kernel, others, per),
        grid=(pairs // per,),
        in_specs=[SMEM] + [feature_cols(block, per)] * 2
        + [pair_block(2 * per, tiles, block, block), feature_rows(2 * block, per), feature_rows(2 * block, per),
           pair_block(per, 2, 2, block)] + [kv_cols(block, per)] * len(kvs),
        out_specs=[feature_cols(2 * block, per)] + [kv_cols(block, per)] * len(kvs),
        out_shape=[shape((2 * block, width), bf16)] + [shape((2, block, width), bf16)] * len(kvs),
        compiler_params=params(24),
        cost_estimate=cost(32 * tiles * block * block * width, 4 * pairs * tiles * block * block),
        name="self_backward",
    )(scalars, *far(q_own, q_swap, probs), aT, *far(oT, inverse, *kvs))


ROWS = 256


def normalized(z):
    center = z - jnp.mean(z, axis=-1, keepdims=True)
    spread = jnp.mean(center * center, axis=-1, keepdims=True)
    r = lax.rsqrt(spread + EPS)
    return center * r, r


def norm_back(G, n, r, gain):
    scaled = G * gain
    return r * (scaled - jnp.mean(scaled, -1, keepdims=True) - n * jnp.mean(scaled * n, -1, keepdims=True))


def spread_lanes(r):
    return jnp.broadcast_to(r, (r.shape[0], PAIR))


def for_rows(total, body, init=0):
    count = min(ROWS, total)
    for i in range(total // count):
        init = body(lambda base, i=i: pl.ds(i * count + base, count), init)
    return init


def fold(x):
    return x.reshape(x.shape[0] // 8, 8, x.shape[1]).sum(0)


def zero_sums(count, width):
    return tuple(jnp.zeros((8, width), f32) for _ in range(count))


def store_sums(ref, sums):
    for n, total in enumerate(sums):
        ref[n:n + 1] = total.sum(0, keepdims=True)


def wait_all(copies):
    for copy in copies:
        copy.wait()


def send(src, dst, sem):
    copy = pltpu.make_async_copy(src, dst, sem)
    copy.start()
    return copy


def dma(count):
    return pltpu.SemaphoreType.DMA((count,))


def first_norm_kernel(sc_ref, oT, tokens, x_swap, w_out, w_query, gain_ref, bias_ref, n_out, r_out, cq_out,
                      oT_v, x_v, held, n_v, r_v, low_v, cq_v, sems, out_sems):
    copies = start_copies([(oT, oT_v), (w_out, held.at[0]), (tokens.at[sc_ref[SIDE]], x_v.at[0]),
                           (x_swap, x_v.at[1]), (w_query, held.at[1])], sems)
    block = x_v.shape[1]
    wait_all(copies[:2])
    n_v[...] = dg(oT_v[...], held[0], TN)
    gain, bias = gain_ref[0:1], bias_ref[0:1]
    wait_all(copies[2:4])
    for half in range(2):
        def body(at, carry, half=half):
            here = at(half * block)
            n, r = normalized(n_v[here] + x_v[half, at(0)].astype(f32))
            n_v[here] = n
            r_v[here] = spread_lanes(r)
            low_v[here] = (n * gain + bias).astype(bf16)
            return carry
        for_rows(block, body)
    sent = [send(n_v, n_out, out_sems.at[0]), send(r_v, r_out, out_sems.at[1])]
    copies[4].wait()
    cq_v[...] = dg(low_v[...], held[1], NN).astype(bf16)
    sent.append(send(cq_v, cq_out, out_sems.at[2]))
    wait_all(sent)


def first_norm(scalars, oT, tokens, x_swap, w_out, w_query, gain, bias):
    width, rows = oT.shape
    block = x_swap.shape[0]
    return pl.pallas_call(
        first_norm_kernel,
        in_specs=[SMEM] + [HBM] * 5 + [VMEM] * 2,
        out_specs=[HBM] * 3,
        out_shape=[far_shape((rows, width), f32), far_shape((rows, PAIR), f32), shape((rows, width), bf16)],
        scratch_shapes=[pltpu.VMEM((width, rows), bf16), pltpu.VMEM((2, block, width), bf16),
                        pltpu.VMEM((2, width, width), bf16), pltpu.VMEM((rows, width), f32),
                        pltpu.VMEM((rows, PAIR), f32), pltpu.VMEM((rows, width), bf16),
                        pltpu.VMEM((rows, width), bf16), dma(5), dma(3)],
        compiler_params=params(16),
        cost_estimate=cost(4 * rows * width * width, 4 * width * width + 10 * rows * width),
        name="first_norm",
    )(scalars, oT, tokens, x_swap, w_out, w_query, gain, bias)


def gelu_parts(x):
    phi = 0.5 + 0.5 * lax.erf(x * math.sqrt(0.5))
    gauss = jnp.exp2(x * x * (-HALF_LOG2E))
    return x * phi, phi + x * gauss * (1.0 / math.sqrt(2.0 * math.pi))


def feed_forward_kernel(chunk, sc_ref, step_ref, oT, n1, grads, g_swap, w_out, w_in, w_back, w_down, w_up,
                        gain_ref, bias_ref,
                        out_own, out_swap, n2_out, r2_out, slope_out, g3_out, gai_out, wg_out0, wg_out1, wg_out2, wg_out3, sums_ref,
                        oT_v, g_v, out_w, in_w, back_w, down_w, up_w, n2_v, r2_v, low_v, upd_v, slope_v,
                        y_v, gai_v, wg_v, sems, in_sems, back_sems, out_sems, slope_sems):
    block = g_v.shape[1]
    rows, width = upd_v.shape
    chunks = in_w.shape[0]
    adapter = down_w.shape[1]
    side = sc_ref[SIDE]
    wg_outs = (wg_out0, wg_out1, wg_out2, wg_out3)

    def in_copy(c):
        return pltpu.make_async_copy(
            w_in.at[:, pl.ds(pl.multiple_of(c * chunk, chunk), chunk)], in_w.at[c], in_sems.at[c])

    def back_copy(c):
        return pltpu.make_async_copy(
            w_back.at[pl.ds(pl.multiple_of(c * chunk, chunk), chunk)], back_w.at[c], back_sems.at[c])

    def slope_copy(c):
        cols = pl.ds(pl.multiple_of(c * chunk, chunk), chunk)
        return pltpu.make_async_copy(slope_v.at[c], slope_out.at[:, cols], slope_sems.at[c])

    copies = [pltpu.make_async_copy(src, dst, sems.at[n]) for n, (src, dst) in enumerate(
        ((oT, oT_v), (w_out, out_w), (n1, upd_v), (w_down, down_w), (w_up, up_w),
         (grads.at[side], g_v.at[0]), (g_swap, g_v.at[1])))]
    for copy in copies[:3]:
        copy.start()

    gain1, bias1 = gain_ref[0:1], bias_ref[0:1]
    gain2, bias2 = gain_ref[1:2], bias_ref[1:2]
    gain3, bias3 = gain_ref[2:3], bias_ref[2:3]
    wait_all(copies[:2])
    for copy in copies[3:5]:
        copy.start()
    in_copy(0).start()
    back_copy(0).start()
    n2_v[...] = dg(oT_v[...], out_w[...], TN)
    copies[2].wait()
    for copy in copies[5:]:
        copy.start()

    def second(at, carry):
        sl = at(0)
        n, r = normalized(n2_v[sl] + upd_v[sl] * gain1 + bias1)
        n2_v[sl] = n
        r2_v[sl] = spread_lanes(r)
        low_v[sl] = (n * gain2 + bias2).astype(bf16)
        return carry

    for_rows(rows, second)
    sent = [send(n2_v, n2_out, out_sems.at[0]), send(r2_v, r2_out, out_sems.at[1])]

    wait_all(copies[3:5])
    factor = (1.0 + step_ref[side].astype(f32)) * 0.25
    adapter_in = dg(low_v[...], down_w[...], NN)
    sig = 1.0 / (1.0 + jnp.exp(-adapter_in))
    adapter_hidden = (factor * (adapter_in * sig)).astype(bf16)
    adapter_slope = factor * (sig * (1.0 + adapter_in * (1.0 - sig)))
    upd_v[...] = dg(adapter_hidden, up_w[...], NN)

    def step(c, carry):
        @pl.when(c + 1 < chunks)
        def _():
            in_copy(c + 1).start()
            back_copy(c + 1).start()

        in_copy(c).wait()
        weight = in_w[c]
        parts = [dg(low_v[pl.ds(b * block, block)], weight, NN) for b in range(2)]
        back_copy(c).wait()
        weight = back_w[c]
        for b in range(2):
            here = pl.ds(b * block, block)
            value, slope = gelu_parts(parts[b])
            slope_v[c, here] = slope.astype(bf16)
            upd_v[here] += dg(value.astype(bf16), weight, NN)
        slope_copy(c).start()
        return carry

    lax.fori_loop(0, chunks, step, 0)

    sums = zero_sums(2, width)
    wait_all(copies[5:])
    for half, target in enumerate((out_own.at[side], out_swap)):
        def third(at, carry, half=half):
            sl = at(0)
            here = at(half * block)
            n, r = normalized(n2_v[here] * gain2 + bias2 + upd_v[here])
            y_v[half, sl] = (n * gain3 + bias3).astype(bf16)
            G = g_v[half, sl].astype(f32)
            upd_v[here] = norm_back(G, n, r, gain3)
            return carry[0] + fold(G * n), carry[1] + fold(G)
        sums = for_rows(block, third, sums)
        sent.append(send(y_v.at[half], target, out_sems.at[2 + half]))
    sent.append(send(upd_v, g3_out, out_sems.at[4]))
    store_sums(sums_ref, sums)

    core, rank, beside = sc_ref[CORE], sc_ref[HALF], sc_ref[NEXT]

    def put(which, value):
        part = adapter // 4
        for n in range(4):
            rows_here = pl.ds(pl.multiple_of(((n % 2) ^ beside) * part, part), part)
            wg_v[2 * (which ^ core) + ((n // 2) ^ rank), rows_here] = value[n * part:(n + 1) * part]

    grad_update = upd_v[...].astype(bf16)
    put(0, dg(adapter_hidden, grad_update, TN).astype(bf16))
    gai = (adapter_slope * dg(grad_update, up_w[...], NT)).astype(bf16)
    gai_v[...] = gai
    sent.append(send(gai_v, gai_out, out_sems.at[5]))
    put(1, dg(gai, low_v[...], TN).astype(bf16))
    for n in (3, 1, 2, 0):
        sent.append(send(wg_v.at[n], wg_outs[n], out_sems.at[6 + n]))

    def drain(c, carry):
        slope_copy(c).wait()
        return carry

    lax.fori_loop(0, chunks, drain, 0)
    wait_all(sent)


def feed_forward(scalars, steps, oT, n1, grads, g_swap, w_out, w_in, w_back, w_down, w_up, gain, bias):
    rows, width = n1.shape
    block = g_swap.shape[0]
    units = w_in.shape[1]
    adapter = w_down.shape[1]
    chunk = 1024
    chunks = units // chunk
    return pl.pallas_call(
        functools.partial(feed_forward_kernel, chunk),
        in_specs=[SMEM, SMEM] + [HBM] * 9 + [VMEM] * 2,
        out_specs=[HBM] * 11 + [VMEM],
        out_shape=[
            far_shape((2, block, width), bf16), far_shape((block, width), bf16), far_shape((rows, width), f32),
            far_shape((rows, PAIR), f32), far_shape((rows, units), bf16), far_shape((rows, width), f32),
            far_shape((rows, adapter), bf16)]
        + [far_shape((adapter // 2, width), bf16)] * 4 + [
            shape((2, width), f32),
        ],
        scratch_shapes=[
            pltpu.VMEM((width, rows), bf16), pltpu.VMEM((2, block, width), bf16),
            pltpu.VMEM((width, width), bf16), pltpu.VMEM((chunks, width, chunk), bf16),
            pltpu.VMEM((chunks, chunk, width), bf16), pltpu.VMEM((width, adapter), bf16),
            pltpu.VMEM((adapter, width), bf16), pltpu.VMEM((rows, width), f32), pltpu.VMEM((rows, PAIR), f32),
            pltpu.VMEM((rows, width), bf16), pltpu.VMEM((rows, width), f32),
            pltpu.VMEM((chunks, rows, chunk), bf16),
            pltpu.VMEM((2, block, width), bf16), pltpu.VMEM((rows, adapter), bf16),
            pltpu.VMEM((4, adapter // 2, width), bf16),
            dma(7), dma(chunks), dma(chunks), dma(10), dma(chunks),
        ],
        compiler_params=params(52),
        cost_estimate=cost(4 * rows * width * units + 12 * rows * width * adapter + 2 * rows * width * width,
                           4 * width * units, 2 * rows * units),
        name="feed_forward",
    )(scalars, steps, *far(oT, n1, grads, g_swap, w_out, w_in, w_back, w_down, w_up), gain, bias)


def feed_back_kernel(chunk, g3, slope, gai, n2, r2, w_in, w_back, w_down, w_out, gain_ref, sums3_ref,
                     g2_out, aT_out, sums_ref,
                     g2_v, slope_v, gai_v, n2_v, r2_v, out_w, in_w, back_w, down_w, low_v, aT_v,
                     sems, in_sems, back_sems, slope_sems, out_sems):
    rows, width = g2_v.shape
    chunks = in_w.shape[0]
    block = rows // 2

    def in_copy(c):
        return pltpu.make_async_copy(
            w_in.at[:, pl.ds(pl.multiple_of(c * chunk, chunk), chunk)], in_w.at[c], in_sems.at[c])

    def back_copy(c):
        return pltpu.make_async_copy(
            w_back.at[pl.ds(pl.multiple_of(c * chunk, chunk), chunk)], back_w.at[c], back_sems.at[c])

    def slope_copy(c):
        cols = pl.ds(pl.multiple_of(c * chunk, chunk), chunk)
        return pltpu.make_async_copy(slope.at[:, cols], slope_v.at[c], slope_sems.at[c])

    copies = start_copies([(g3, g2_v), (w_down, down_w), (gai, gai_v)], sems)
    for c in range(chunks):
        back_copy(c).start()
        slope_copy(c).start()
        in_copy(c).start()
    copies += [send(n2, n2_v, sems.at[3]), send(r2, r2_v, sems.at[4]), send(w_out, out_w, sems.at[5])]
    copies[0].wait()
    low_v[...] = g2_v[...].astype(bf16)
    wait_all(copies[1:3])
    g2_v[...] += dg(gai_v[...], down_w[...], NT)

    def step(c, carry):
        back_copy(c).wait()
        weight = back_w[c]
        parts = [dg(low_v[pl.ds(b * block, block)], weight, NT) for b in range(2)]
        in_copy(c).wait()
        slope_copy(c).wait()
        weight = in_w[c]
        for b in range(2):
            here = pl.ds(b * block, block)
            inner = (parts[b] * slope_v[c, here].astype(f32)).astype(bf16)
            g2_v[here] += dg(inner, weight, NT)
        return carry

    lax.fori_loop(0, chunks, step, 0)
    gain2 = gain_ref[1:2]
    wait_all(copies[3:])

    def second(at, carry):
        sl = at(0)
        G = g2_v[sl]
        n = n2_v[sl]
        grad = norm_back(G, n, r2_v[sl][:, 0:1], gain2)
        g2_v[sl] = grad
        low_v[sl] = grad.astype(bf16)
        return carry[0] + fold(G * n), carry[1] + fold(G)

    sums = for_rows(rows, second, zero_sums(2, width))
    sent = [send(g2_v, g2_out, out_sems.at[0])]
    store_sums(sums_ref, sums)
    sums_ref[2:4] = sums3_ref[...]
    aT_v[...] = dg(out_w[...], low_v[...], NT).astype(bf16)
    sent.append(send(aT_v, aT_out, out_sems.at[1]))
    wait_all(sent)


def feed_back(g3, slope, gai, n2, r2, w_in, w_back, w_down, w_out, gain, sums3):
    rows, width = g3.shape
    units = w_in.shape[1]
    adapter = w_down.shape[1]
    chunk = 1024
    chunks = units // chunk
    return pl.pallas_call(
        functools.partial(feed_back_kernel, chunk),
        in_specs=[HBM] * 9 + [VMEM] * 2,
        out_specs=[HBM] * 2 + [VMEM],
        out_shape=[shape((rows, width), f32), shape((width, rows), bf16), shape((4, width), f32)],
        scratch_shapes=[
            pltpu.VMEM((rows, width), f32), pltpu.VMEM((chunks, rows, chunk), bf16),
            pltpu.VMEM((rows, adapter), bf16), pltpu.VMEM((rows, width), f32), pltpu.VMEM((rows, PAIR), f32),
            pltpu.VMEM((width, width), bf16), pltpu.VMEM((chunks, width, chunk), bf16),
            pltpu.VMEM((chunks, chunk, width), bf16), pltpu.VMEM((width, adapter), bf16),
            pltpu.VMEM((rows, width), bf16), pltpu.VMEM((width, rows), bf16),
            dma(6), dma(chunks), dma(chunks), dma(chunks), dma(2),
        ],
        compiler_params=params(38),
        cost_estimate=cost(4 * rows * width * units + 2 * rows * width * adapter + 2 * rows * width * width,
                           4 * width * units),
        name="feed_back",
    )(*far(g3, slope, gai, n2, r2, w_in, w_back, w_down, w_out), gain, sums3)


def first_back_kernel(g2, dq, n1, r1, w_query, w_out, gain_ref, sums2_ref, g1_out, aT_out, sums_ref,
                      g1_v, dq_v, n_v, r_v, held, low_v, aT_v, sems, out_sems):
    copies = start_copies([(dq, dq_v), (w_query, held.at[0]), (g2, g1_v), (n1, n_v), (r1, r_v),
                           (w_out, held.at[1])], sems)
    rows, width = g1_v.shape
    wait_all(copies[:3])
    g1_v[...] += dg(dq_v[...], held[0], NT)
    gain = gain_ref[0:1]
    wait_all(copies[3:5])

    def body(at, carry):
        sl = at(0)
        G = g1_v[sl]
        n = n_v[sl]
        grad = norm_back(G, n, r_v[sl][:, 0:1], gain)
        g1_v[sl] = grad
        low_v[sl] = grad.astype(bf16)
        return carry[0] + fold(G * n), carry[1] + fold(G)

    sums = for_rows(rows, body, zero_sums(2, width))
    sent = [send(g1_v, g1_out, out_sems.at[0])]
    store_sums(sums_ref, sums)
    sums_ref[2:6] = sums2_ref[...]
    copies[5].wait()
    aT_v[...] = dg(held[1], low_v[...], NT).astype(bf16)
    sent.append(send(aT_v, aT_out, out_sems.at[1]))
    wait_all(sent)


def first_back(g2, dq, n1, r1, w_query, w_out, gain, sums2):
    rows, width = g2.shape
    return pl.pallas_call(
        first_back_kernel,
        in_specs=[HBM] * 6 + [VMEM] * 2,
        out_specs=[HBM] * 2 + [VMEM],
        out_shape=[shape((rows, width), f32), shape((width, rows), bf16), shape((6, width), f32)],
        scratch_shapes=[pltpu.VMEM((rows, width), f32), pltpu.VMEM((rows, width), bf16),
                        pltpu.VMEM((rows, width), f32), pltpu.VMEM((rows, PAIR), f32),
                        pltpu.VMEM((2, width, width), bf16), pltpu.VMEM((rows, width), bf16),
                        pltpu.VMEM((width, rows), bf16), dma(6), dma(2)],
        compiler_params=params(18),
        cost_estimate=cost(4 * rows * width * width, 4 * width * width + 10 * rows * width),
        name="first_back",
    )(g2, dq, *far(n1, r1), w_query, w_out, gain, sums2)


def summed(first, others):
    total = first.astype(f32)
    for ref in others:
        total = total + ref.astype(f32)
    return total.astype(bf16)


def key_grads_kernel(count, blocks, based, sc_ref, *refs):
    parts, refs = refs[:count], refs[count:]
    if based:
        base, dq, w_query, refs = refs[0], refs[1], refs[2], refs[3:]
    w_key, w_value, refs = refs[0], refs[1], refs[2:]
    outs, refs = refs[:len(blocks)], refs[len(blocks):]
    part_v, held, out_v = refs[:3]
    sems, out_sems = refs[-2:]
    size = out_v.shape[1]
    rows = size * len(blocks)
    order = [(w_key, held.at[0])] + [(ref, part_v.at[n]) for n, ref in enumerate(parts)]
    order.append((w_value, held.at[1]))
    total = None
    if based:
        here = pl.ds(blocks[0] * size, rows)
        first = start_copies([(dq.at[here], refs[4]), (w_query, held.at[2]), (base.at[here], refs[3])],
                             sems.at[pl.ds(2 + count, 3)])
    copies = start_copies(order, sems)
    if based:
        wait_all(first)
        total = refs[3][...] + dg(refs[4][...], held[2], NT)
    wait_all(copies[:1 + count])
    step = len(blocks)
    for n in range(2):
        if n == 1:
            copies[1 + count].wait()
        value = [summed(part_v[b, n], [part_v[r, n] for r in range(step + b, count, step)]) for b in range(step)]
        value = value[0] if step == 1 else jnp.concatenate(value, 0)
        total = add(total, dg(value, held[n], NT))
    sent = []
    for b in reversed(range(step)):
        out_v[b] = total[b * size:(b + 1) * size].astype(bf16)
        target = outs[b].at[sc_ref[SIDE]] if blocks[b] == 0 else outs[b]
        sent.append(send(out_v.at[b], target, out_sems.at[b]))
    wait_all(sent)


def key_grads(scalars, parts, w_key, w_value, base=None, blocks=(0, 1)):
    _, block, width = parts[0].shape
    count = len(parts)
    based = base is not None
    extra = list(base) if based else []
    return pl.pallas_call(
        functools.partial(key_grads_kernel, count, blocks, based),
        in_specs=[SMEM] + [HBM] * (count + 2 + len(extra)),
        out_specs=[HBM] * len(blocks),
        out_shape=[far_shape((2, block, width), bf16) if b == 0 else shape((block, width), bf16) for b in blocks],
        scratch_shapes=[pltpu.VMEM((count, 2, block, width), bf16),
                        pltpu.VMEM((3 if based else 2, width, width), bf16),
                        pltpu.VMEM((len(blocks), block, width), bf16)]
        + ([pltpu.VMEM((len(blocks) * block, width), f32), pltpu.VMEM((len(blocks) * block, width), bf16)]
           if based else [])
        + [dma(2 + count + len(extra)), dma(len(blocks))],
        compiler_params=params(20),
        cost_estimate=cost(8 * block * width * width, 4 * width * width),
        name="token_grad" if based else "enc_grad",
    )(scalars, *parts, *extra, w_key, w_value)


def place_kernel(sc_ref, held, back, out, sem):
    send(back, out.at[1 - sc_ref[SIDE]], sem.at[0]).wait()


def put_back(scalars, out, back):
    return pl.pallas_call(
        place_kernel,
        in_specs=[SMEM, HBM, HBM],
        out_specs=HBM,
        out_shape=far_shape(out.shape, out.dtype),
        scratch_shapes=[dma(1)],
        input_output_aliases={1: 0},
        compiler_params=params(4),
        cost_estimate=cost(0, back.size * 4),
        name="place",
    )(scalars, *far(out), back)


def assemble_kernel(places, sc_ref, *refs):
    count = len(places)
    pieces = refs[:count]
    sums_a, sums_b, up_ref, down_ref, gains_ref, biases_ref = refs[count:]
    core, rank, beside = sc_ref[CORE], sc_ref[HALF], sc_ref[NEXT]
    for (first, second, third), piece in zip(places, pieces):
        block = first ^ core
        size = piece.shape[0]
        at = pl.ds(pl.multiple_of((2 * (second ^ rank) + (third ^ beside)) * size, size), size)

        @pl.when(block == 0)
        def _():
            up_ref[at] = piece[...].astype(f32)

        @pl.when(block == 1)
        def _():
            down_ref[:, at] = piece[...].T.astype(f32)
    total = sums_a[...] + sums_b[...]
    for n in range(3):
        gains_ref[n:n + 1] = total[2 * n:2 * n + 1]
        biases_ref[n:n + 1] = total[2 * n + 1:2 * n + 2]


def assemble(scalars, places, pieces, sums_a, sums_b):
    part, width = pieces[0].shape
    return pl.pallas_call(
        functools.partial(assemble_kernel, places),
        in_specs=[SMEM] + [VMEM] * (len(pieces) + 2),
        out_specs=[VMEM] * 4,
        out_shape=[shape((4 * part, width), f32), shape((width, 4 * part), f32), shape((3, width), f32),
                   shape((3, width), f32)],
        compiler_params=params(14),
        cost_estimate=cost(0, 24 * part * width),
        name="assemble",
    )(scalars, *pieces, sums_a, sums_b)


def exchange(x, step):
    axis, bit = step
    return lax.ppermute(x, axis, [(i, i ^ bit) for i in range(lax.axis_size(axis))])


def after(x, *others):
    return lax.optimization_barrier((x,) + others)[0]


def plus(x, *others):
    total = x.astype(f32)
    for y in others:
        total = total + y.astype(f32)
    return total.astype(x.dtype)


def bits(size):
    return [1 << n for n in range(size.bit_length() - 1)]


def position_table(group, block, far_bit, ranks):
    half = group // 2
    table = []
    for rank in range(ranks):
        for member in range(group):
            side = member // half
            low = group - 1 - member if side else member

            def starts(index):
                own = group - 1 - index if side else index
                return [own * block, (group - 1 - own) * block]

            row = [side, member & 1, int(rank & far_bit != 0), rank & 1, low * block, (group - 1 - low) * block]
            row += starts(low)
            tail = []
            for r in range(1, half):
                index = (low + r) % half
                wrap = low + r >= half
                row += starts(index)
                first, second = index * block, (group - 1 - index) * block
                tail += [int(wrap), first, first if wrap else second]
            table.append(row + tail)
    return jnp.asarray(table, jnp.int32)


def per_device(
    tokens, enc_states, dec_lengths, enc_lengths, adapter_step, out_grad,
    self_query, self_key, self_value, self_out, cross_query, cross_key, cross_value, cross_out,
    ffn_in, ffn_out, adapter_down, adapter_up, ln_gain, ln_bias,
):
    group, ranks = lax.axis_size("seq"), lax.axis_size("dp")
    half = group // 2
    member = lax.axis_index("seq")
    side = member // half
    block = tokens.shape[1]
    swap = [(i, group - 1 - i) for i in range(group)]
    seq_bits, dp_bits = bits(group), bits(ranks)
    core_step, far_step, side_step = ("seq", 1), ("dp", dp_bits[1]), ("dp", 1)
    full_steps = [("seq", b) for b in seq_bits[1:]] + [("dp", b) for b in dp_bits[2:]]
    scalars = lax.dynamic_index_in_dim(
        position_table(group, block, far_step[1], ranks), lax.axis_index("dp") * group + member, 0, keepdims=False)

    def place(s, index):
        return group - 1 - index if s == 1 else index

    def from_shift(r):
        return [(place(s, (i + r) % half), place(s, i)) for s in range(2) for i in range(half)]

    def to_shift(r):
        return [(place(s, i), place(s, (i + r) % half)) for s in range(2) for i in range(half)]

    def theirs(x):
        return lax.dynamic_index_in_dim(x, 1 - side, 0, keepdims=False)

    def swapped(x):
        return lax.ppermute(x, "seq", swap)

    def joined(out, back):
        return lax.dynamic_update_index_in_dim(out, back, 1 - side, 0)

    def gathered(own, other):
        every = [own, other]
        for r in range(1, half):
            every += [lax.ppermute(own, "seq", from_shift(r)), lax.ppermute(other, "seq", from_shift(r))]
        return every

    def returned(parts):
        return parts[:1] + [lax.ppermute(parts[r], "seq", to_shift(r)) for r in range(1, half)]

    x_swap = swapped(theirs(tokens))
    q_own, kv_own, ckv_own = project(
        scalars, [tokens, enc_states], [self_key, self_value, self_query, cross_key, cross_value],
        ((0, 1, 0), (0, 1, 1), (0, 0, None), (1, 2, 0), (1, 2, 1)), "project_own", pin=True)
    e_theirs, g_theirs = theirs(enc_states), theirs(out_grad)
    e_swap = swapped(after(e_theirs, x_swap))
    kv_swap, q_swap = project(
        scalars, [x_swap], [self_key, self_value, self_query], ((0, 0, 0), (0, 0, 1), (0, 1, None)),
        "project_swap")
    kvs = gathered(kv_own, kv_swap)
    oT, probs, inverse = self_forward(scalars, dec_lengths, q_own, q_swap, kvs)
    ckv_swap, = project(
        scalars, [after(e_swap, oT)], [cross_key, cross_value], ((0, 0, 0), (0, 0, 1)), "project_enc")
    g_swap = swapped(after(g_theirs, e_swap))
    ckvs = gathered(ckv_own, ckv_swap)
    n1, r1, cq = first_norm(scalars, after(oT, ckv_swap), tokens, x_swap, self_out, cross_query, ln_gain, ln_bias)
    coT, cprobs, cinverse = cross_forward(scalars, enc_lengths, cq, ckvs)
    out_own, out_swap, n2, r2, slope, g3, gai, *wgs, sums3 = feed_forward(
        scalars, adapter_step, coT, n1, out_grad, g_swap, cross_out, ffn_in, ffn_out, adapter_down, adapter_up,
        ln_gain, ln_bias)

    forwarded = plus(wgs[1], exchange(wgs[3], core_step))
    received = exchange(forwarded, far_step)
    kept = exchange(wgs[2], core_step)
    out_back = swapped(out_swap)
    g2, caT, sums2 = feed_back(after(g3, forwarded), slope, gai, n2, r2, ffn_in, ffn_out, adapter_down, cross_out,
                               ln_gain, sums3)
    size = kept.shape[0] // 2
    received = after(received, g2)
    wg, forwarded = [plus(x, y, z) for x, y, z in zip(*(
        (part[:size], part[size:]) for part in (wgs[0], kept, received)))]
    layer_output = joined(out_own, after(out_back, g2))

    received = exchange(forwarded, side_step)
    cdq, *cdkvs = cross_backward(cq, cprobs, after(caT, forwarded, layer_output), coT, cinverse, ckvs)
    wg = plus(wg, after(received, cdq))
    cdkvs = [after(x, wg) for x in cdkvs]
    enc_parts = [x for pair in zip(returned(cdkvs[0::2]), returned(cdkvs[1::2])) for x in pair]
    received = exchange(wg, full_steps[0])
    g1, aT, sums = first_back(after(g2, wg), cdq, n1, r1, cross_query, self_out, ln_gain, sums2)
    y_steps = [("seq", bit) for bit in seq_bits[1:]]
    z_steps = [("dp", b) for b in dp_bits[2:]]
    received_sums = exchange(sums, z_steps[0])
    enc_own, enc_swap = key_grads(scalars, [after(enc_parts[0], aT)] + enc_parts[1:], cross_key, cross_value)
    wg = plus(wg, after(received, enc_swap))
    sums = plus(sums, after(received_sums, enc_swap))
    for step in full_steps[1:-1]:
        wg = plus(wg, exchange(wg, step))
    received = exchange(wg, full_steps[-1])
    received_sums = exchange(sums, far_step)
    enc_back = swapped(enc_swap)

    dq, *dkvs = self_backward(scalars, q_own, q_swap, probs, after(aT, wg, sums, enc_swap), oT, inverse, kvs)
    wg = plus(wg, after(received, dq))
    sums = plus(sums, after(received_sums, dq))
    enc_grad = joined(enc_own, after(enc_back, dq))
    dkvs = [after(x, wg, sums, enc_back) for x in dkvs]
    swap_parts = returned(dkvs[1::2])
    both_step = ("dp", side_step[1] | far_step[1])
    beside, beyond, across, sibling = (exchange(wg, step) for step in (side_step, far_step, both_step, core_step))
    for step in y_steps[1:] + z_steps[1:]:
        sums = plus(sums, exchange(sums, step))
    received_sums = exchange(sums, y_steps[0])
    base = (g1, dq, self_query)
    own_parts = returned(dkvs[0::2])
    t_swap, = key_grads(scalars, swap_parts, self_key, self_value, base, (1,))
    t_back = swapped(t_swap)
    sums = plus(sums, after(received_sums, t_swap))
    received_sums = exchange(sums, side_step)
    across = after(across, t_swap)
    t_own, = key_grads(scalars, own_parts, self_key, self_value, (after(g1, t_swap, across), dq, self_query), (0,))
    beside, beyond = (after(x, t_own) for x in (beside, beyond))
    sums = plus(sums, after(received_sums, t_own))
    received_sums = exchange(sums, core_step)
    places = [(0, 0, 0), (0, 0, 1), (0, 1, 0), (0, 1, 1), (1, 0, 0), (1, 0, 1), (1, 1, 0), (1, 1, 1)]
    pieces = [wg, beside, beyond, across, sibling] + [exchange(x, core_step) for x in (beside, beyond, across)]
    up, down, gains, biases = assemble(scalars, places, pieces, sums, received_sums)
    return layer_output, put_back(scalars, t_own, after(t_back, up)), enc_grad, down, up, gains, biases


def solution(mesh):
    rows = P("dp", "seq", None)
    return jax.shard_map(
        per_device,
        mesh=mesh,
        in_specs=(rows, rows, P("dp"), P("dp"), P("dp"), rows) + (P(),) * 14,
        out_specs=(rows, rows, rows, P(), P(), P(), P()),
        check_vma=False,
    )
```
